32 devices in a mesh: ctx: 16 (over z, y, core), kvh: 2 (over x).
Axes of the slice: x: 2, y: 2, z: 4, core: 2. Of those that a mesh axis runs over, the one named last changes fastest.
Arguments:
- queries: bfloat16 [256, 128, 128], P(('ctx', 'kvh')), may hold values from -6 to 6
- new_keys: bfloat16 [256, 8, 128], P('ctx', 'kvh'), may hold values from -6 to 6
- new_values: bfloat16 [256, 8, 128], P('ctx', 'kvh'), may hold values from -6 to 6
- new_positions: int32 [256], P('ctx'), may hold values from 0 to 255, each once
- hist_keys: bfloat16 [48, 128, 8, 128], P('ctx', None, 'kvh'), may hold values from -6 to 6
- hist_values: bfloat16 [48, 128, 8, 128], P('ctx', None, 'kvh'), may hold values from -6 to 6
- page_slots: int32 [32], replicated, may hold values from 0 to 47, as said below
Outputs:
- attention: bfloat16 [256, 128, 128], P(('ctx', 'kvh'))
The draws below stay inside these ranges and needn't reach their ends.
Inputs may be any that keep to these rules, and one draw needn't show every extreme that they name: `page_slots`: entry p equals 3 * d + s: history page p is held in slot s of index d of ctx. Page p belongs to index p // 2, and d is that index or the one 16 // 2 away; an index holds at most one page that belongs to that other index and at most 3 pages in all; no slot holds two pages; slots that hold no page carry data that is not part of the history.
All inputs are finite; a program needn't handle non-finite values.
Results may differ from the reference program's by a relative error of at most 0.01.
Values may be sent and summed in bfloat16 or wider, within the bound.
A program may use at most 64 MiB of HBM per device.

```python
import math
import jax
import jax.numpy as jnp
from jax import lax

QH = 128
KVH = 8
HD = 128
PAGE = 128
PAGES_DEV = 2
SLOTS_DEV = 3
NEW = 256
PAGES = 32
N_CTX = 16


def draw_queries(key, part):
    key = jax.random.fold_in(key, 1)
    sample = jnp.clip(jax.random.normal(key, (NEW, QH, HD), jnp.float32), -6.0, 6.0)
    return sample.astype(jnp.bfloat16)


def draw_hist_keys(key, part):
    key = jax.random.fold_in(key, 2)
    sample = jnp.clip(jax.random.normal(key, (N_CTX * SLOTS_DEV, PAGE, KVH, HD), jnp.float32), -6.0, 6.0)
    return sample.astype(jnp.bfloat16)


def draw_page_slots(key, part):
    key = jax.random.fold_in(key, 3)
    subkeys = jax.random.split(key, 2)
    half_cycle = N_CTX // 2
    pair_index = jnp.arange(half_cycle)
    upper_hot = jax.random.randint(subkeys[0], (half_cycle,), 0, 2)
    upper_hot = upper_hot.at[0].set(0).at[half_cycle - 1].set(1)
    hot_dev = pair_index + half_cycle * upper_hot
    cold_dev = pair_index + half_cycle * (1 - upper_hot)
    rotation = jax.random.randint(subkeys[1], (N_CTX,), 0, SLOTS_DEV)
    page_index = jnp.arange(PAGES_DEV)

    def slot_of(device, base):
        return device * SLOTS_DEV + (base + rotation[device]) % SLOTS_DEV
    hot_pages = hot_dev[:, None] * PAGES_DEV + page_index[None, :]
    hot_slots = slot_of(hot_dev[:, None], page_index[None, :])
    cold_pages = cold_dev[:, None] * PAGES_DEV + page_index[None, :]
    moved_slot = slot_of(hot_dev[:, None], PAGES_DEV + 0 * page_index[None, :])
    kept_slot = slot_of(cold_dev[:, None], page_index[None, :])
    cold_slots = jnp.where(page_index[None, :] == PAGES_DEV - 1, moved_slot, kept_slot)
    result = jnp.zeros((PAGES,), jnp.int32)
    result = result.at[hot_pages.reshape(-1)].set(hot_slots.reshape(-1).astype(jnp.int32))
    result = result.at[cold_pages.reshape(-1)].set(cold_slots.reshape(-1).astype(jnp.int32))
    return result


def block_scale(own_key, extent, cuts, smallest, high):
    def one(dim, parts):
        heights = jax.random.uniform(jax.random.fold_in(jax.random.fold_in(own_key, 6), dim), (parts,), jnp.float32, smallest / len(cuts), high / len(cuts))
        return jnp.repeat(jnp.exp(heights), extent[dim] // parts).reshape((-1,) + (1,) * (len(extent) - dim - 1))

    loudness = one(*cuts[0])
    for cut in cuts[1:]:
        loudness = loudness * one(*cut)
    return loudness


def gaussian(key, shape, scale, reach, shards=(), kind=jnp.bfloat16):
    values = jax.random.normal(key, shape, jnp.float32) * scale
    if len(shards) > 0:
        values = block_scale(key, shape, shards, -0.22, 0.18) * values
    return jnp.clip(values, min=-reach, max=reach).astype(kind)


def setup_inputs(seed: int = 0) -> dict:
    streams_of = jax.random.split(jax.random.key(seed), 8)
    return {
        "queries": draw_queries(jax.random.fold_in(streams_of[7], 71), 0),
        "new_keys": gaussian(streams_of[1], (NEW, KVH, HD), 1.0, 6.0, ((0, 16), (1, 2))),
        "new_values": gaussian(streams_of[2], (NEW, KVH, HD), 1.0, 6.0, ((0, 16), (1, 2))),
        "new_positions": jax.random.permutation(streams_of[3], NEW).astype(jnp.int32),
        "hist_keys": draw_hist_keys(jax.random.fold_in(streams_of[7], 71), 0),
        "hist_values": gaussian(streams_of[5], (N_CTX * SLOTS_DEV, PAGE, KVH, HD), 1.0, 6.0, ((0, 16), (2, 2))),
        "page_slots": draw_page_slots(jax.random.fold_in(streams_of[7], 71), 0),
    }


def attend_rows(query_rows, key_rows, value_rows, visible):
    tokens_here, per_group, width = query_rows.shape
    flat = query_rows.reshape(tokens_here * per_group, width)
    scores = jnp.dot(flat, key_rows.T, preferred_element_type=jnp.float32)
    scores = scores.reshape(tokens_here, per_group, -1) * (1.0 / math.sqrt(width))
    masked_in = visible[:, None, :]
    scores = jnp.where(masked_in, scores, -1e+30)
    row_max = lax.optimization_barrier(jnp.max(scores, axis=-1, keepdims=True))
    weights = jnp.where(masked_in, jnp.exp(scores - row_max), 0.0)
    totals = lax.optimization_barrier(jnp.sum(weights, axis=-1))
    rounded = weights.astype(jnp.bfloat16).reshape(tokens_here * per_group, -1)
    summed = jnp.dot(rounded, value_rows, preferred_element_type=jnp.float32)
    summed = summed.reshape(tokens_here, per_group, width) / totals[..., None]
    return summed.astype(jnp.bfloat16)

def reference(queries, new_keys, new_values, new_positions, hist_keys, hist_values, page_slots):
    history_keys = hist_keys[page_slots].reshape(-1, KVH, HD)
    history_values = hist_values[page_slots].reshape(-1, KVH, HD)
    all_keys = jnp.concatenate([history_keys, new_keys], axis=0)
    all_values = jnp.concatenate([history_values, new_values], axis=0)
    hist_len = history_keys.shape[0]
    group_size = QH // KVH
    block_len = math.gcd(NEW, 128)
    block_count = NEW // block_len
    grouped = queries.reshape(NEW, KVH, group_size, HD).transpose(1, 0, 2, 3)
    keys_by_head = all_keys.transpose(1, 0, 2)
    values_by_head = all_values.transpose(1, 0, 2)
    position_blocks = new_positions.reshape(block_count, block_len)
    history_seen = jnp.ones((block_len, hist_len), dtype=bool)

    def per_head(operands):
        head_queries, head_keys, head_values = operands

        def per_block(pieces):
            query_block, position_block = pieces
            fresh_seen = new_positions[None, :] <= position_block[:, None]
            visible = jnp.concatenate([history_seen, fresh_seen], axis=1)
            return attend_rows(query_block, head_keys, head_values, visible)
        blocks = head_queries.reshape(block_count, block_len, group_size, HD)
        result = lax.map(per_block, (blocks, position_blocks))
        return result.reshape(NEW, group_size, HD)
    outputs = lax.map(per_head, (grouped, keys_by_head, values_by_head))
    return outputs.transpose(1, 0, 2, 3).reshape(NEW, QH, HD)
```

```python
import math

import jax
import jax.numpy as jnp
from jax import lax
from jax.experimental import pallas as pl
from jax.experimental.pallas import tpu as pltpu
from jax.sharding import PartitionSpec as P

MESH = pl.DeviceIdType.MESH
NEG = -1e30
DELAY = 2


def split_ctx(n):
    rows = max(a for a in range(1, n + 1) if n % a == 0 and a * a <= n)
    group = n // rows
    pair = 2 if group > 2 and group % 2 == 0 else 1
    return rows, group, pair


def kernel(dims, q_in, hist, new, posk, posq, bias, out,
           qbuf, kvbuf, nbuf, pkbuf, pqbuf, sbuf, pbuf, lbuf, obuf, stbuf,
           in_l, st_l, in_r, st_r, fin,
           loc_q, loc_kv, loc_n, qx_s, qx_r, qr_s, ql_s, qz_r, kv_s, kv_r, fw_s,
           n_s, n_r, pk_s, pk_r, pq_s, pq_r, or_s, ol_s, sr_s, sl_s,
           ol_r, or_r, tl_r, tr_r, ox_s, ox_r):
    A, B, B2, K, H, T, T_loc, G, HPD, SL = dims
    B1 = B // B2
    R = T * G
    c = lax.axis_index("ctx")
    k = lax.axis_index("kvh")
    z, g = c // B, c % B
    b1, b2 = g // B2, g % B2
    cc = math.log2(math.e) / math.sqrt(128)

    def remote(src, dst, ss, rs, dev):
        return pltpu.make_async_remote_copy(
            src_ref=src, dst_ref=dst, send_sem=ss, recv_sem=rs,
            device_id=dev, device_id_type=MESH)

    def heads(kk, h):
        return pl.ds(pl.multiple_of(kk * HPD + h * G, G), G)

    def toks(kk):
        return pl.ds(kk * T_loc, T_loc)

    def grp(d):
        return (g + d) % B

    def q_x(h, d):
        kk = (k + d) % K
        return remote(q_in.at[:, heads(kk, h), :], qbuf.at[h, z, toks(k)],
                      qx_s.at[h, d - 1], qx_r.at[h, d - 1], (c, kk))

    def q_x_in(h, d):
        kk = (k + K - d) % K
        dst = qbuf.at[h, z, toks(kk)]
        return remote(dst, dst, qx_s.at[h, d - 1], qx_r.at[h, d - 1], (c, kk))

    def q_loc(h):
        return pltpu.make_async_copy(q_in.at[:, heads(k, h), :], qbuf.at[h, z, toks(k)], loc_q.at[h])

    def kv_loc(h):
        return pltpu.make_async_copy(hist.at[h], kvbuf.at[h, g], loc_kv.at[h])

    def q_right(h, o):
        return remote(qbuf.at[h, o], qbuf.at[h, o], qr_s.at[h, o], qz_r.at[h, o], (c + B, k))

    def q_left(h, o):
        return remote(qbuf.at[h, o], qbuf.at[h, o], ql_s.at[h, o], qz_r.at[h, o], (c - B, k))

    def kv_far(h, d1):
        to = z * B + ((b1 + d1) % B1) * B2 + b2
        return remote(hist.at[h], kvbuf.at[h, g], kv_s.at[h, d1 - 1], kv_r.at[h, g], (to, k))

    def kv_near(h, d2):
        to = z * B + b1 * B2 + (b2 + d2) % B2
        return remote(hist.at[h], kvbuf.at[h, g], kv_s.at[h, B1 - 1 + d2 - 1], kv_r.at[h, g], (to, k))

    def kv_in(h, src):
        dst = kvbuf.at[h, src]
        return remote(dst, dst, kv_s.at[h, 0], kv_r.at[h, src], (c, k))

    def kv_pass(h, d1, d2):
        src = ((b1 + B1 - d1) % B1) * B2 + b2
        to = z * B + b1 * B2 + (b2 + d2) % B2
        return remote(kvbuf.at[h, src], kvbuf.at[h, src], fw_s.at[h, d1 - 1, d2 - 1], kv_r.at[h, src], (to, k))

    def n_out(d):
        return remote(new, nbuf.at[g], n_s.at[d - 1], n_r.at[d - 1], (z * B + grp(d), k))

    def pk_out(d):
        return remote(posk, pkbuf.at[g], pk_s.at[d - 1], pk_r.at[d - 1], (z * B + grp(d), k))

    def pq_out(d):
        return remote(posq, pqbuf.at[z], pq_s.at[d - 1], pq_r.at[d - 1], (((z + d) % A) * B + g, k))

    def n_in(d):
        src = nbuf.at[(g + B - d) % B]
        return remote(src, src, n_s.at[d - 1], n_r.at[d - 1], (c, k))

    def pk_in(d):
        src = pkbuf.at[(g + B - d) % B]
        return remote(src, src, pk_s.at[d - 1], pk_r.at[d - 1], (c, k))

    def pq_in(d):
        src = pqbuf.at[(z + A - d) % A]
        return remote(src, src, pq_s.at[d - 1], pq_r.at[d - 1], (c, k))

    def o_right(h, o):
        return (remote(obuf.at[h, o], in_l.at[h, o], or_s.at[h, o], ol_r.at[h, o], (c + B, k)),
                remote(stbuf.at[h, o], st_l.at[h, o], sr_s.at[h, o], tl_r.at[h, o], (c + B, k)))

    def o_left(h, o):
        return (remote(obuf.at[h, o], in_r.at[h, o], ol_s.at[h, o], or_r.at[h, o], (c - B, k)),
                remote(stbuf.at[h, o], st_r.at[h, o], sl_s.at[h, o], tr_r.at[h, o], (c - B, k)))

    def out_x(h, d):
        kk = (k + d) % K
        return remote(fin.at[h, toks(kk)], out.at[:, heads(k, h), :],
                      ox_s.at[h, d - 1], ox_r.at[h, d - 1], (c, kk))

    def out_x_in(h, d):
        kk = (k + K - d) % K
        dst = out.at[:, heads(kk, h), :]
        return remote(fin.at[h, toks(kk)], dst, ox_s.at[h, d - 1], ox_r.at[h, d - 1], (c, kk))

    barrier = pltpu.get_barrier_semaphore()
    for d in range(1, K):
        pl.semaphore_signal(barrier, inc=1, device_id=(c, (k + d) % K), device_id_type=MESH)
    for d in range(1, A):
        pl.semaphore_signal(barrier, inc=1, device_id=(((z + d) % A) * B + g, k), device_id_type=MESH)
    for d in range(1, B):
        pl.semaphore_signal(barrier, inc=1, device_id=(z * B + grp(d), k), device_id_type=MESH)
    pl.semaphore_wait(barrier, K - 1 + A - 1 + B - 1)

    for h in range(H):
        for d in range(1, K):
            q_x(h, d).start()
        q_loc(h).start()
        for d1 in range(1, B1):
            kv_far(h, d1).start()
        for d2 in range(1, B2):
            kv_near(h, d2).start()
        kv_loc(h).start()
        if h == 0:
            for d in range(1, B):
                n_out(d).start()
                pk_out(d).start()
            for d in range(1, A):
                pq_out(d).start()
            pltpu.make_async_copy(new, nbuf.at[g], loc_n).start()
            pkbuf[g] = posk[...]
            pqbuf[z] = posq[...]

    for h in range(H):
        q_loc(h).wait()
        for d in range(1, K):
            q_x_in(h, d).wait_recv()

        @pl.when(z < A - 1)
        def _():
            q_right(h, z).start()

        @pl.when(z > 0)
        def _():
            q_left(h, z).start()

    def q_forward(h, d):
        @pl.when(z - d >= 0)
        def _():
            q_right(h, z - d).wait_recv()

            @pl.when(z < A - 1)
            def _():
                q_right(h, z - d).start()

        @pl.when(z + d <= A - 1)
        def _():
            q_left(h, z + d).wait_recv()

            @pl.when(z > 0)
            def _():
                q_left(h, z + d).start()

    def kv_stage1(h):
        for d1 in range(1, B1):
            kv_in(h, ((b1 + B1 - d1) % B1) * B2 + b2).wait_recv()
            for d2 in range(1, B2):
                kv_pass(h, d1, d2).start()

    def kv_stage2(h):
        kv_loc(h).wait()
        for d2 in range(1, B2):
            for d1 in range(B1):
                kv_in(h, ((b1 + B1 - d1) % B1) * B2 + (b2 + B2 - d2) % B2).wait_recv()

    for d in range(1, A - 1):
        q_forward(0, d)
    kv_stage1(0)
    if A > 1:
        q_forward(0, A - 1)
    pltpu.make_async_copy(new, nbuf.at[g], loc_n).wait()
    for d in range(1, B):
        n_in(d).wait_recv()
        pk_in(d).wait_recv()
    for d in range(1, A):
        pq_in(d).wait_recv()

    low = z < A // 2
    zf = jnp.where(low, z, A - 1 - z)

    def order(j):
        far = A - 1 - zf
        f = jnp.where(j < far, A - 1 - j, jnp.where(j < A - 1, j - far, zf))
        return jnp.where(low, f, A - 1 - f)

    def attend(h, o, slot):
        q = qbuf[h, o].reshape(R, 128)
        top = jnp.full((R, 128), NEG, jnp.float32)
        for b in range(B):
            s = lax.dot_general(q, kvbuf[h, b, 0], (((1,), (1,)), ((), ())),
                                preferred_element_type=jnp.float32)
            s = s * cc + bias[8 * b:8 * b + 1, :]
            sbuf[:, b * SL:(b + 1) * SL] = s
            for i in range(SL // 128):
                top = jnp.maximum(top, s[:, i * 128:(i + 1) * 128])
        nk = nbuf[:, h, 0].reshape(B * T, 128)
        sn = lax.dot_general(q, nk, (((1,), (1,)), ((), ())), preferred_element_type=jnp.float32)
        pos_k = pkbuf[0]
        for b in range(1, B):
            pos_k = pos_k + pkbuf[b]
        pos_q = jnp.broadcast_to(pqbuf[o][:, None, :], (T, G, 128)).reshape(R, 128)
        seen = pos_k[0:1, :B * T] <= pos_q[:, :B * T]
        sn = jnp.where(seen, sn * cc, NEG)
        m = jnp.maximum(jnp.max(top, axis=-1, keepdims=True), jnp.max(sn, axis=-1, keepdims=True))
        pn = jnp.exp2(sn - m)
        nv = nbuf[:, h, 1].reshape(B * T, 128)
        acc = jnp.dot(pn.astype(jnp.bfloat16), nv, preferred_element_type=jnp.float32)
        total = jnp.zeros((R, 128), jnp.float32)
        for b in range(B):
            p = jnp.exp2(sbuf[:, b * SL:(b + 1) * SL] - m)
            for i in range(SL // 128):
                total = total + p[:, i * 128:(i + 1) * 128]
            acc = acc + jnp.dot(p.astype(jnp.bfloat16), kvbuf[h, b, 1], preferred_element_type=jnp.float32)
        denom = jnp.sum(total, axis=-1, keepdims=True) + jnp.sum(pn, axis=-1, keepdims=True)
        pbuf[slot] = acc * (1.0 / denom)
        lbuf[slot] = jnp.broadcast_to(m + jnp.log(denom) * math.log2(math.e), (R, 128))

    def merge(h, o, slot, copies, data, stats):
        for cp in copies:
            cp.wait_recv()
        x = data[h, o].astype(jnp.float32)
        for r in range(R // 128):
            rows = slice(r * 128, (r + 1) * 128)
            lx = jnp.transpose(jnp.broadcast_to(stats[h, o, 8 * r:8 * r + 1, :], (128, 128)))
            lo = lbuf[slot, rows, :]
            m = jnp.maximum(lx, lo)
            wx, wo = jnp.exp2(lx - m), jnp.exp2(lo - m)
            den = wx + wo
            pbuf[slot, rows, :] = (wx * x[rows] + wo * pbuf[slot, rows, :]) * (1.0 / den)
            lbuf[slot, rows, :] = m + jnp.log(den) * math.log2(math.e)

    def emit(h, o, slot, copies):
        obuf[h, o] = pbuf[slot].astype(jnp.bfloat16)
        for r in range(R // 128):
            stbuf[h, o, 8 * r:8 * r + 8, :] = jnp.transpose(lbuf[slot, r * 128:(r + 1) * 128, :])[0:8, :]
        for cp in copies:
            cp.start()

    steps = H * A

    def step(s, carry):
        @pl.when(s < steps)
        def _():
            h, j = s // A, s % A

            @pl.when(j == 0)
            def _():
                kv_stage2(h)

            @pl.when(h + 1 < H)
            def _():
                for d in range(1, A):
                    @pl.when(j == d - 1)
                    def _():
                        q_forward(h + 1, d)

                @pl.when(j == A - 1)
                def _():
                    kv_stage1(h + 1)

            attend(h, order(j), s % (DELAY + 1))

        @pl.when(s >= DELAY)
        def _():
            t = s - DELAY
            h, o, slot = t // A, order(t % A), t % (DELAY + 1)

            @pl.when((o >= z) & (z > 0))
            def _():
                merge(h, o, slot, o_right(h, o), in_l, st_l)

            @pl.when((o <= z) & (z < A - 1))
            def _():
                merge(h, o, slot, o_left(h, o), in_r, st_r)

            @pl.when(o > z)
            def _():
                emit(h, o, slot, o_right(h, o))

            @pl.when(o < z)
            def _():
                emit(h, o, slot, o_left(h, o))

            @pl.when(o == z)
            def _():
                fin[h] = pbuf[slot].astype(jnp.bfloat16).reshape(T, G, 128)
                for d in range(1, K):
                    out_x(h, d).start()
                out[:, heads(k, h), :] = fin[h, toks(k)]

        return carry

    lax.fori_loop(0, steps + DELAY, step, 0)

    for d in range(1, B):
        n_out(d).wait_send()
        pk_out(d).wait_send()
    for d in range(1, A):
        pq_out(d).wait_send()

    def drain(h, carry):
        for d in range(1, K):
            q_x(h, d).wait_send()
            out_x(h, d).wait_send()
            out_x_in(h, d).wait_recv()
        for d1 in range(1, B1):
            kv_far(h, d1).wait_send()
            for d2 in range(1, B2):
                kv_pass(h, d1, d2).wait_send()
        for d2 in range(1, B2):
            kv_near(h, d2).wait_send()

        def per_owner(o, inner):
            @pl.when((o <= z) & (z < A - 1))
            def _():
                q_right(h, o).wait_send()

            @pl.when((o >= z) & (z > 0))
            def _():
                q_left(h, o).wait_send()

            @pl.when(o > z)
            def _():
                for cp in o_right(h, o):
                    cp.wait_send()

            @pl.when(o < z)
            def _():
                for cp in o_left(h, o):
                    cp.wait_send()

            return inner

        lax.fori_loop(0, A, per_owner, 0)
        return carry

    lax.fori_loop(0, H, drain, 0)


def solution(mesh):
    n_ctx, K = mesh.shape["ctx"], mesh.shape["kvh"]
    A, B, B2 = split_ctx(n_ctx)
    B1 = B // B2

    def body(queries, new_keys, new_values, new_positions, hist_keys, hist_values, page_slots):
        T_loc, QH, width = queries.shape
        T, H = new_keys.shape[0], new_keys.shape[1]
        HPD = QH // K
        G = HPD // H
        slots, page = hist_keys.shape[:2]
        SL = slots * page
        R = T * G
        c = lax.axis_index("ctx")
        z, g = c // B, c % B
        hist = jnp.stack([hist_keys, hist_values]).transpose(3, 0, 1, 2, 4).reshape(H, 2, SL, width)
        new = jnp.stack([new_keys, new_values]).transpose(2, 0, 1, 3)
        lane = jnp.arange(128)
        row = jnp.where(lane // T == g, jnp.tile(new_positions, 128 // T), 0)
        posk = jnp.broadcast_to(row[None, :], (8, 128))
        posq = jnp.broadcast_to(new_positions[:, None], (T, 128))
        ids = z * B * slots + jnp.arange(B * slots, dtype=jnp.int32)
        live = jnp.any(page_slots[None, :] == ids[:, None], axis=1)
        bias = jnp.where(live, 0.0, NEG).astype(jnp.float32).reshape(B, 1, slots, 1)
        bias = jnp.broadcast_to(bias, (B, 8, slots, page)).reshape(B * 8, SL)

        bf, f32, i32 = jnp.bfloat16, jnp.float32, jnp.int32
        V = pltpu.VMEM
        D = pltpu.SemaphoreType.DMA
        kp, ap, bp = max(K - 1, 1), max(A - 1, 1), max(B - 1, 1)
        dims = (A, B, B2, K, H, T, T_loc, G, HPD, SL)
        scratch = [
            V((H, A, T, G, width), bf), V((H, B, 2, SL, width), bf), V((B, H, 2, T, width), bf),
            V((B, 8, 128), i32), V((A, T, 128), i32), V((R, B * SL), f32),
            V((DELAY + 1, R, 128), f32), V((DELAY + 1, R, 128), f32),
            V((H, A, R, 128), bf), V((H, A, R // 16, 128), f32),
            V((H, A, R, 128), bf), V((H, A, R // 16, 128), f32),
            V((H, A, R, 128), bf), V((H, A, R // 16, 128), f32),
            V((H, T, G, width), bf),
            D((H,)), D((H,)), D, D((H, kp)), D((H, kp)), D((H, A)), D((H, A)), D((H, A)),
            D((H, B)), D((H, B)), D((H, max(B1 - 1, 1), max(B2 - 1, 1))),
            D((bp,)), D((bp,)), D((bp,)), D((bp,)), D((ap,)), D((ap,)),
            D((H, A)), D((H, A)), D((H, A)), D((H, A)),
            D((H, A)), D((H, A)), D((H, A)), D((H, A)), D((H, kp)), D((H, kp)),
        ]
        any_ = pl.BlockSpec(memory_space=pl.ANY)
        vm = pl.BlockSpec(memory_space=pltpu.VMEM)
        work = A * R * (B * SL + B * T) * H
        return pl.pallas_call(
            lambda *refs: kernel(dims, *refs),
            out_shape=jax.ShapeDtypeStruct((T_loc, QH, width), bf),
            in_specs=[any_, any_, any_, vm, vm, vm],
            out_specs=vm,
            scratch_shapes=scratch,
            cost_estimate=pl.CostEstimate(flops=4 * work * width, bytes_accessed=2 * hist.size + 4 * queries.size, transcendentals=work),
            compiler_params=pltpu.CompilerParams(
                collective_id=0, has_side_effects=True, vmem_limit_bytes=40 * 1024 * 1024),
        )(queries, hist, new, posk, posq, bias)

    in_specs = (
        P(("ctx", "kvh"), None, None), P("ctx", "kvh", None), P("ctx", "kvh", None), P("ctx"),
        P("ctx", None, "kvh", None), P("ctx", None, "kvh", None), P(),
    )
    out_specs = P(("ctx", "kvh"), None, None)
    return jax.shard_map(body, mesh=mesh, in_specs=in_specs, out_specs=out_specs, check_vma=False)
```

```python
import math

import jax
import jax.numpy as jnp
from jax import lax
from jax.experimental import pallas as pl
from jax.experimental.pallas import tpu as pltpu
from jax.sharding import PartitionSpec as P

MESH = pl.DeviceIdType.MESH
NEG = -1e30
DELAY = 3
OWN_DELAY = 5
SLOTS = 6


def split_ctx(n):
    rows = max(a for a in range(1, n + 1) if n % a == 0 and a * a <= n)
    group = n // rows
    pair = 2 if group > 2 and group % 2 == 0 else 1
    return rows, group, pair


def kernel(dims, q_in, hist, new, posk, posq, bias, out,
           qbuf, kvbuf, nbuf, pkbuf, pqbuf, sbuf, pbuf, lbuf, obuf, stbuf,
           in_l, st_l, in_r, st_r, fin,
           loc_q, loc_kv, loc_n, qx_s, qx_r, qr_s, ql_s, qz_r, kv_s, kv_r, fw_s,
           n_s, n_r, pk_s, pk_r, pq_s, pq_r, or_s, ol_s, sr_s, sl_s,
           ol_r, or_r, tl_r, tr_r, ox_s, ox_r):
    A, B, B2, K, H, T, T_loc, G, HPD, SL = dims
    B1 = B // B2
    R = T * G
    c = lax.axis_index("ctx")
    k = lax.axis_index("kvh")
    z, g = c // B, c % B
    b1, b2 = g // B2, g % B2
    cc = math.log2(math.e) / math.sqrt(128)

    def remote(src, dst, ss, rs, dev):
        return pltpu.make_async_remote_copy(
            src_ref=src, dst_ref=dst, send_sem=ss, recv_sem=rs,
            device_id=dev, device_id_type=MESH)

    def heads(kk, h):
        return pl.ds(pl.multiple_of(kk * HPD + h * G, G), G)

    def toks(kk):
        return pl.ds(kk * T_loc, T_loc)

    def grp(d):
        return (g + d) % B

    def q_x(h, d):
        kk = (k + d) % K
        return remote(q_in.at[:, heads(kk, h), :], qbuf.at[h, z, toks(k)],
                      qx_s.at[h, d - 1], qx_r.at[h, d - 1], (c, kk))

    def q_x_in(h, d):
        kk = (k + K - d) % K
        dst = qbuf.at[h, z, toks(kk)]
        return remote(dst, dst, qx_s.at[h, d - 1], qx_r.at[h, d - 1], (c, kk))

    def q_loc(h):
        return pltpu.make_async_copy(q_in.at[:, heads(k, h), :], qbuf.at[h, z, toks(k)], loc_q.at[h])

    def kv_loc(h):
        return pltpu.make_async_copy(hist.at[h], kvbuf.at[h, g], loc_kv.at[h])

    def q_right(h, o):
        return remote(qbuf.at[h, o], qbuf.at[h, o], qr_s.at[h, o], qz_r.at[h, o], (c + B, k))

    def q_left(h, o):
        return remote(qbuf.at[h, o], qbuf.at[h, o], ql_s.at[h, o], qz_r.at[h, o], (c - B, k))

    def kv_far(h, d1):
        to = z * B + ((b1 + d1) % B1) * B2 + b2
        return remote(hist.at[h], kvbuf.at[h, g], kv_s.at[h, d1 - 1], kv_r.at[h, g], (to, k))

    def kv_near(h, d2):
        to = z * B + b1 * B2 + (b2 + d2) % B2
        return remote(hist.at[h], kvbuf.at[h, g], kv_s.at[h, B1 - 1 + d2 - 1], kv_r.at[h, g], (to, k))

    def kv_in(h, src):
        dst = kvbuf.at[h, src]
        return remote(dst, dst, kv_s.at[h, 0], kv_r.at[h, src], (c, k))

    def kv_pass(h, d1, d2):
        src = ((b1 + B1 - d1) % B1) * B2 + b2
        to = z * B + b1 * B2 + (b2 + d2) % B2
        return remote(kvbuf.at[h, src], kvbuf.at[h, src], fw_s.at[h, d1 - 1, d2 - 1], kv_r.at[h, src], (to, k))

    def n_out(d):
        return remote(new, nbuf.at[g], n_s.at[d - 1], n_r.at[d - 1], (z * B + grp(d), k))

    def pk_out(d):
        return remote(posk, pkbuf.at[g], pk_s.at[d - 1], pk_r.at[d - 1], (z * B + grp(d), k))

    def pq_out(d):
        return remote(posq, pqbuf.at[z], pq_s.at[d - 1], pq_r.at[d - 1], (((z + d) % A) * B + g, k))

    def n_in(d):
        src = nbuf.at[(g + B - d) % B]
        return remote(src, src, n_s.at[d - 1], n_r.at[d - 1], (c, k))

    def pk_in(d):
        src = pkbuf.at[(g + B - d) % B]
        return remote(src, src, pk_s.at[d - 1], pk_r.at[d - 1], (c, k))

    def pq_in(d):
        src = pqbuf.at[(z + A - d) % A]
        return remote(src, src, pq_s.at[d - 1], pq_r.at[d - 1], (c, k))

    def o_right(h, o):
        return (remote(obuf.at[h, o], in_l.at[h, o], or_s.at[h, o], ol_r.at[h, o], (c + B, k)),
                remote(stbuf.at[h, o], st_l.at[h, o], sr_s.at[h, o], tl_r.at[h, o], (c + B, k)))

    def o_left(h, o):
        return (remote(obuf.at[h, o], in_r.at[h, o], ol_s.at[h, o], or_r.at[h, o], (c - B, k)),
                remote(stbuf.at[h, o], st_r.at[h, o], sl_s.at[h, o], tr_r.at[h, o], (c - B, k)))

    def out_x(h, d):
        kk = (k + d) % K
        return remote(fin.at[h, toks(kk)], out.at[:, heads(k, h), :],
                      ox_s.at[h, d - 1], ox_r.at[h, d - 1], (c, kk))

    def out_x_in(h, d):
        kk = (k + K - d) % K
        dst = out.at[:, heads(kk, h), :]
        return remote(fin.at[h, toks(kk)], dst, ox_s.at[h, d - 1], ox_r.at[h, d - 1], (c, kk))

    barrier = pltpu.get_barrier_semaphore()
    for d in range(1, K):
        pl.semaphore_signal(barrier, inc=1, device_id=(c, (k + d) % K), device_id_type=MESH)
    for d in range(1, A):
        pl.semaphore_signal(barrier, inc=1, device_id=(((z + d) % A) * B + g, k), device_id_type=MESH)
    for d in range(1, B):
        pl.semaphore_signal(barrier, inc=1, device_id=(z * B + grp(d), k), device_id_type=MESH)
    pl.semaphore_wait(barrier, K - 1 + A - 1 + B - 1)

    def kv_send(h):
        for d1 in range(1, B1):
            kv_far(h, d1).start()
        for d2 in range(1, B2):
            kv_near(h, d2).start()
        kv_loc(h).start()

    for h in range(H):
        for d in range(1, K):
            q_x(h, d).start()
        q_loc(h).start()
        if h == 0:
            kv_send(h)
            for d in range(1, B):
                n_out(d).start()
                pk_out(d).start()
            for d in range(1, A):
                pq_out(d).start()
            pltpu.make_async_copy(new, nbuf.at[g], loc_n).start()
            pkbuf[g] = posk[...]
            pqbuf[z] = posq[...]

    def q_own(h):
        q_loc(h).wait()
        for d in range(1, K):
            q_x_in(h, d).wait_recv()

        @pl.when(z < A - 1)
        def _():
            q_right(h, z).start()

        @pl.when(z > 0)
        def _():
            q_left(h, z).start()

    def q_forward(h, d):
        @pl.when(z - d >= 0)
        def _():
            q_right(h, z - d).wait_recv()

            @pl.when(z < A - 1)
            def _():
                q_right(h, z - d).start()

        @pl.when(z + d <= A - 1)
        def _():
            q_left(h, z + d).wait_recv()

            @pl.when(z > 0)
            def _():
                q_left(h, z + d).start()

    def kv_stage1(h):
        for d1 in range(1, B1):
            kv_in(h, ((b1 + B1 - d1) % B1) * B2 + b2).wait_recv()
            if d1 == B1 - 1:
                @pl.when(h + 2 < H)
                def _():
                    kv_send(h + 2)
            for d2 in range(1, B2):
                kv_pass(h, d1, d2).start()

    def kv_stage2(h):
        kv_loc(h).wait()
        for d2 in range(1, B2):
            for d1 in range(B1):
                kv_in(h, ((b1 + B1 - d1) % B1) * B2 + (b2 + B2 - d2) % B2).wait_recv()

    q_own(0)
    if H > 1:
        kv_send(1)
        q_own(1)
    for d in range(1, A - 1):
        q_forward(0, d)
    kv_stage1(0)
    if A > 1:
        q_forward(0, A - 1)
    pltpu.make_async_copy(new, nbuf.at[g], loc_n).wait()
    for d in range(1, B):
        n_in(d).wait_recv()
        pk_in(d).wait_recv()
    for d in range(1, A):
        pq_in(d).wait_recv()

    low = z < A // 2
    zf = jnp.where(low, z, A - 1 - z)

    def order(j):
        far = A - 1 - zf
        f = jnp.where(j < far, A - 1 - j, jnp.where(j < A - 1, j - far, zf))
        return jnp.where(low, f, A - 1 - f)

    def attend(h, o, slot):
        q = qbuf[h, o].reshape(R, 128)
        top = jnp.full((R, 128), NEG, jnp.float32)
        for b in range(B):
            s = lax.dot_general(q, kvbuf[h, b, 0], (((1,), (1,)), ((), ())),
                                preferred_element_type=jnp.float32)
            s = s * cc + bias[8 * b:8 * b + 1, :]
            sbuf[:, b * SL:(b + 1) * SL] = s
            for i in range(SL // 128):
                top = jnp.maximum(top, s[:, i * 128:(i + 1) * 128])
        nk = nbuf[:, h, 0].reshape(B * T, 128)
        sn = lax.dot_general(q, nk, (((1,), (1,)), ((), ())), preferred_element_type=jnp.float32)
        pos_k = pkbuf[0]
        for b in range(1, B):
            pos_k = pos_k + pkbuf[b]
        pos_q = jnp.broadcast_to(pqbuf[o][:, None, :], (T, G, 128)).reshape(R, 128)
        seen = pos_k[0:1, :B * T] <= pos_q[:, :B * T]
        sn = jnp.where(seen, sn * cc, NEG)
        m = jnp.maximum(jnp.max(top, axis=-1, keepdims=True), jnp.max(sn, axis=-1, keepdims=True))
        pn = jnp.exp2(sn - m)
        nv = nbuf[:, h, 1].reshape(B * T, 128)
        acc = jnp.dot(pn.astype(jnp.bfloat16), nv, preferred_element_type=jnp.float32)
        total = jnp.zeros((R, 128), jnp.float32)
        for b in range(B):
            p = jnp.exp2(sbuf[:, b * SL:(b + 1) * SL] - m)
            for i in range(SL // 128):
                total = total + p[:, i * 128:(i + 1) * 128]
            acc = acc + jnp.dot(p.astype(jnp.bfloat16), kvbuf[h, b, 1], preferred_element_type=jnp.float32)
        denom = jnp.sum(total, axis=-1, keepdims=True) + jnp.sum(pn, axis=-1, keepdims=True)
        pbuf[slot] = acc * (1.0 / denom)
        lbuf[slot] = jnp.broadcast_to(m + jnp.log(denom) * math.log2(math.e), (R, 128))

    def merge(h, o, slot, copies, data, stats):
        for cp in copies:
            cp.wait_recv()
        x = data[h, o].astype(jnp.float32)
        for r in range(R // 128):
            rows = slice(r * 128, (r + 1) * 128)
            lx = jnp.transpose(jnp.broadcast_to(stats[h, o, 8 * r:8 * r + 1, :], (128, 128)))
            lo = lbuf[slot, rows, :]
            m = jnp.maximum(lx, lo)
            wx, wo = jnp.exp2(lx - m), jnp.exp2(lo - m)
            den = wx + wo
            pbuf[slot, rows, :] = (wx * x[rows] + wo * pbuf[slot, rows, :]) * (1.0 / den)
            lbuf[slot, rows, :] = m + jnp.log(den) * math.log2(math.e)

    def emit(h, o, slot, copies):
        obuf[h, o] = pbuf[slot].astype(jnp.bfloat16)
        for r in range(R // 128):
            stbuf[h, o, 8 * r:8 * r + 8, :] = jnp.transpose(lbuf[slot, r * 128:(r + 1) * 128, :])[0:8, :]
        for cp in copies:
            cp.start()

    steps = H * A

    def step(s, carry):
        @pl.when(s < steps)
        def _():
            h, j = s // A, s % A

            @pl.when(j == 0)
            def _():
                kv_stage2(h)

                @pl.when(h + 2 < H)
                def _():
                    q_own(h + 2)

            @pl.when(h + 1 < H)
            def _():
                for d in range(1, A):
                    @pl.when(j == d - 1)
                    def _():
                        q_forward(h + 1, d)

                @pl.when(j == A - 1)
                def _():
                    kv_stage1(h + 1)

            o, slot = order(j), s % SLOTS
            attend(h, o, slot)

            @pl.when((o > z) & (z == 0))
            def _():
                emit(h, o, slot, o_right(h, o))

            @pl.when((o < z) & (z == A - 1))
            def _():
                emit(h, o, slot, o_left(h, o))

        @pl.when((s >= DELAY) & (s < steps + DELAY))
        def _():
            t = s - DELAY
            h, o, slot = t // A, order(t % A), t % SLOTS

            @pl.when((o > z) & (z > 0))
            def _():
                merge(h, o, slot, o_right(h, o), in_l, st_l)
                emit(h, o, slot, o_right(h, o))

            @pl.when((o < z) & (z < A - 1))
            def _():
                merge(h, o, slot, o_left(h, o), in_r, st_r)
                emit(h, o, slot, o_left(h, o))

        @pl.when((s >= OWN_DELAY) & ((s - OWN_DELAY) % A == A - 1))
        def _():
            t = s - OWN_DELAY
            h, slot = t // A, t % SLOTS

            @pl.when(z > 0)
            def _():
                merge(h, z, slot, o_right(h, z), in_l, st_l)

            @pl.when(z < A - 1)
            def _():
                merge(h, z, slot, o_left(h, z), in_r, st_r)

            fin[h] = pbuf[slot].astype(jnp.bfloat16).reshape(T, G, 128)
            for d in range(1, K):
                out_x(h, d).start()
            out[:, heads(k, h), :] = fin[h, toks(k)]

        return carry

    lax.fori_loop(0, steps + OWN_DELAY, step, 0)

    for d in range(1, B):
        n_out(d).wait_send()
        pk_out(d).wait_send()
    for d in range(1, A):
        pq_out(d).wait_send()

    def drain(h, carry):
        for d in range(1, K):
            q_x(h, d).wait_send()
            out_x(h, d).wait_send()
            out_x_in(h, d).wait_recv()
        for d1 in range(1, B1):
            kv_far(h, d1).wait_send()
            for d2 in range(1, B2):
                kv_pass(h, d1, d2).wait_send()
        for d2 in range(1, B2):
            kv_near(h, d2).wait_send()

        def per_owner(o, inner):
            @pl.when((o <= z) & (z < A - 1))
            def _():
                q_right(h, o).wait_send()

            @pl.when((o >= z) & (z > 0))
            def _():
                q_left(h, o).wait_send()

            @pl.when(o > z)
            def _():
                for cp in o_right(h, o):
                    cp.wait_send()

            @pl.when(o < z)
            def _():
                for cp in o_left(h, o):
                    cp.wait_send()

            return inner

        lax.fori_loop(0, A, per_owner, 0)
        return carry

    lax.fori_loop(0, H, drain, 0)


def solution(mesh):
    n_ctx, K = mesh.shape["ctx"], mesh.shape["kvh"]
    A, B, B2 = split_ctx(n_ctx)
    B1 = B // B2

    def body(queries, new_keys, new_values, new_positions, hist_keys, hist_values, page_slots):
        T_loc, QH, width = queries.shape
        T, H = new_keys.shape[0], new_keys.shape[1]
        HPD = QH // K
        G = HPD // H
        slots, page = hist_keys.shape[:2]
        SL = slots * page
        R = T * G
        c = lax.axis_index("ctx")
        z, g = c // B, c % B
        hist = jnp.stack([hist_keys, hist_values]).transpose(3, 0, 1, 2, 4).reshape(H, 2, SL, width)
        new = jnp.stack([new_keys, new_values]).transpose(2, 0, 1, 3)
        lane = jnp.arange(128)
        row = jnp.where(lane // T == g, jnp.tile(new_positions, 128 // T), 0)
        posk = jnp.broadcast_to(row[None, :], (8, 128))
        posq = jnp.broadcast_to(new_positions[:, None], (T, 128))
        ids = z * B * slots + jnp.arange(B * slots, dtype=jnp.int32)
        live = jnp.any(page_slots[None, :] == ids[:, None], axis=1)
        bias = jnp.where(live, 0.0, NEG).astype(jnp.float32).reshape(B, 1, slots, 1)
        bias = jnp.broadcast_to(bias, (B, 8, slots, page)).reshape(B * 8, SL)

        bf, f32, i32 = jnp.bfloat16, jnp.float32, jnp.int32
        V = pltpu.VMEM
        D = pltpu.SemaphoreType.DMA
        kp, ap, bp = max(K - 1, 1), max(A - 1, 1), max(B - 1, 1)
        dims = (A, B, B2, K, H, T, T_loc, G, HPD, SL)
        scratch = [
            V((H, A, T, G, width), bf), V((H, B, 2, SL, width), bf), V((B, H, 2, T, width), bf),
            V((B, 8, 128), i32), V((A, T, 128), i32), V((R, B * SL), f32),
            V((SLOTS, R, 128), f32), V((SLOTS, R, 128), f32),
            V((H, A, R, 128), bf), V((H, A, R // 16, 128), f32),
            V((H, A, R, 128), bf), V((H, A, R // 16, 128), f32),
            V((H, A, R, 128), bf), V((H, A, R // 16, 128), f32),
            V((H, T, G, width), bf),
            D((H,)), D((H,)), D, D((H, kp)), D((H, kp)), D((H, A)), D((H, A)), D((H, A)),
            D((H, B)), D((H, B)), D((H, max(B1 - 1, 1), max(B2 - 1, 1))),
            D((bp,)), D((bp,)), D((bp,)), D((bp,)), D((ap,)), D((ap,)),
            D((H, A)), D((H, A)), D((H, A)), D((H, A)),
            D((H, A)), D((H, A)), D((H, A)), D((H, A)), D((H, kp)), D((H, kp)),
        ]
        any_ = pl.BlockSpec(memory_space=pl.ANY)
        vm = pl.BlockSpec(memory_space=pltpu.VMEM)
        work = A * R * (B * SL + B * T) * H
        return pl.pallas_call(
            lambda *refs: kernel(dims, *refs),
            out_shape=jax.ShapeDtypeStruct((T_loc, QH, width), bf),
            in_specs=[any_, any_, any_, vm, vm, vm],
            out_specs=vm,
            scratch_shapes=scratch,
            cost_estimate=pl.CostEstimate(flops=4 * work * width, bytes_accessed=2 * hist.size + 4 * queries.size, transcendentals=work),
            compiler_params=pltpu.CompilerParams(
                collective_id=0, has_side_effects=True, vmem_limit_bytes=40 * 1024 * 1024),
        )(queries, hist, new, posk, posq, bias)

    in_specs = (
        P(("ctx", "kvh"), None, None), P("ctx", "kvh", None), P("ctx", "kvh", None), P("ctx"),
        P("ctx", None, "kvh", None), P("ctx", None, "kvh", None), P(),
    )
    out_specs = P(("ctx", "kvh"), None, None)
    return jax.shard_map(body, mesh=mesh, in_specs=in_specs, out_specs=out_specs, check_vma=False)
```

```python
import math

import jax
import jax.numpy as jnp
from jax import lax
from jax.experimental import pallas as pl
from jax.experimental.pallas import tpu as pltpu
from jax.sharding import PartitionSpec as P

MESH = pl.DeviceIdType.MESH
NEG = -1e30
FIRST_DELAY = 4
HOP_DELAY = 2


def split_ctx(n):
    rows = max(a for a in range(1, n + 1) if n % a == 0 and a * a <= n)
    group = n // rows
    pair = 2 if group > 2 and group % 2 == 0 else 1
    return rows, group, pair


def kernel(dims, q_in, hist, new, posk, posq, bias, out,
           qbuf, kvbuf, nbuf, pkbuf, pqbuf, sbuf, pbuf, lbuf, obuf, stbuf,
           in_l, st_l, in_r, st_r, fin,
           loc_q, loc_kv, loc_n, qx_s, qx_r, qr_s, ql_s, qz_r, kv_s, kv_r, fw_s,
           n_s, n_r, pk_s, pk_r, pq_s, pq_r, or_s, ol_s, sr_s, sl_s,
           ol_r, or_r, tl_r, tr_r, ox_s, ox_r):
    A, B, B2, K, H, T, T_loc, G, HPD, SL = dims
    B1 = B // B2
    R = T * G
    c = lax.axis_index("ctx")
    k = lax.axis_index("kvh")
    z, g = c // B, c % B
    b1, b2 = g // B2, g % B2
    cc = math.log2(math.e) / math.sqrt(128)

    def remote(src, dst, ss, rs, dev):
        return pltpu.make_async_remote_copy(
            src_ref=src, dst_ref=dst, send_sem=ss, recv_sem=rs,
            device_id=dev, device_id_type=MESH)

    def heads(kk, h):
        return pl.ds(pl.multiple_of(kk * HPD + h * G, G), G)

    def toks(kk):
        return pl.ds(kk * T_loc, T_loc)

    def grp(d):
        return (g + d) % B

    def q_x(h, d):
        kk = (k + d) % K
        return remote(q_in.at[:, heads(kk, h), :], qbuf.at[h, z, toks(k)],
                      qx_s.at[h, d - 1], qx_r.at[h, d - 1], (c, kk))

    def q_x_in(h, d):
        kk = (k + K - d) % K
        dst = qbuf.at[h, z, toks(kk)]
        return remote(dst, dst, qx_s.at[h, d - 1], qx_r.at[h, d - 1], (c, kk))

    def q_loc(h):
        return pltpu.make_async_copy(q_in.at[:, heads(k, h), :], qbuf.at[h, z, toks(k)], loc_q.at[h])

    def kv_loc(h):
        return pltpu.make_async_copy(hist.at[h], kvbuf.at[h, g], loc_kv.at[h])

    def q_right(h, o):
        return remote(qbuf.at[h, o], qbuf.at[h, o], qr_s.at[h, o], qz_r.at[h, o], (c + B, k))

    def q_left(h, o):
        return remote(qbuf.at[h, o], qbuf.at[h, o], ql_s.at[h, o], qz_r.at[h, o], (c - B, k))

    def kv_far(h, d1):
        to = z * B + ((b1 + d1) % B1) * B2 + b2
        return remote(hist.at[h], kvbuf.at[h, g], kv_s.at[h, d1 - 1], kv_r.at[h, g], (to, k))

    def kv_near(h, d2):
        to = z * B + b1 * B2 + (b2 + d2) % B2
        return remote(hist.at[h], kvbuf.at[h, g], kv_s.at[h, B1 - 1 + d2 - 1], kv_r.at[h, g], (to, k))

    def kv_in(h, src):
        dst = kvbuf.at[h, src]
        return remote(dst, dst, kv_s.at[h, 0], kv_r.at[h, src], (c, k))

    def kv_pass(h, d1, d2):
        src = ((b1 + B1 - d1) % B1) * B2 + b2
        to = z * B + b1 * B2 + (b2 + d2) % B2
        return remote(kvbuf.at[h, src], kvbuf.at[h, src], fw_s.at[h, d1 - 1, d2 - 1], kv_r.at[h, src], (to, k))

    def n_out(d):
        return remote(new, nbuf.at[g], n_s.at[d - 1], n_r.at[d - 1], (z * B + grp(d), k))

    def pk_out(d):
        return remote(posk, pkbuf.at[g], pk_s.at[d - 1], pk_r.at[d - 1], (z * B + grp(d), k))

    def pq_out(d):
        return remote(posq, pqbuf.at[z], pq_s.at[d - 1], pq_r.at[d - 1], (((z + d) % A) * B + g, k))

    def n_in(d):
        src = nbuf.at[(g + B - d) % B]
        return remote(src, src, n_s.at[d - 1], n_r.at[d - 1], (c, k))

    def pk_in(d):
        src = pkbuf.at[(g + B - d) % B]
        return remote(src, src, pk_s.at[d - 1], pk_r.at[d - 1], (c, k))

    def pq_in(d):
        src = pqbuf.at[(z + A - d) % A]
        return remote(src, src, pq_s.at[d - 1], pq_r.at[d - 1], (c, k))

    def o_right(h, o):
        return (remote(obuf.at[h, o], in_l.at[h, o], or_s.at[h, o], ol_r.at[h, o], (c + B, k)),
                remote(stbuf.at[h, o], st_l.at[h, o], sr_s.at[h, o], tl_r.at[h, o], (c + B, k)))

    def o_left(h, o):
        return (remote(obuf.at[h, o], in_r.at[h, o], ol_s.at[h, o], or_r.at[h, o], (c - B, k)),
                remote(stbuf.at[h, o], st_r.at[h, o], sl_s.at[h, o], tr_r.at[h, o], (c - B, k)))

    def out_x(h, d):
        kk = (k + d) % K
        return remote(fin.at[h, toks(kk)], out.at[:, heads(k, h), :],
                      ox_s.at[h, d - 1], ox_r.at[h, d - 1], (c, kk))

    def out_x_in(h, d):
        kk = (k + K - d) % K
        dst = out.at[:, heads(kk, h), :]
        return remote(fin.at[h, toks(kk)], dst, ox_s.at[h, d - 1], ox_r.at[h, d - 1], (c, kk))

    barrier = pltpu.get_barrier_semaphore()
    for d in range(1, K):
        pl.semaphore_signal(barrier, inc=1, device_id=(c, (k + d) % K), device_id_type=MESH)
    for d in range(1, A):
        pl.semaphore_signal(barrier, inc=1, device_id=(((z + d) % A) * B + g, k), device_id_type=MESH)
    for d in range(1, B):
        pl.semaphore_signal(barrier, inc=1, device_id=(z * B + grp(d), k), device_id_type=MESH)
    pl.semaphore_wait(barrier, K - 1 + A - 1 + B - 1)

    def kv_send(h):
        for d1 in range(1, B1):
            kv_far(h, d1).start()
        for d2 in range(1, B2):
            kv_near(h, d2).start()
        kv_loc(h).start()

    for h in range(H):
        for d in range(1, K):
            q_x(h, d).start()
        q_loc(h).start()
        if h == 0:
            kv_send(h)
            for d in range(1, B):
                n_out(d).start()
                pk_out(d).start()
            for d in range(1, A):
                pq_out(d).start()
            pltpu.make_async_copy(new, nbuf.at[g], loc_n).start()
            pkbuf[g] = posk[...]
            pqbuf[z] = posq[...]

    def q_own(h):
        q_loc(h).wait()
        for d in range(1, K):
            q_x_in(h, d).wait_recv()

        @pl.when(z < A - 1)
        def _():
            q_right(h, z).start()

        @pl.when(z > 0)
        def _():
            q_left(h, z).start()

    def q_forward(h, d):
        @pl.when(z - d >= 0)
        def _():
            q_right(h, z - d).wait_recv()

            @pl.when(z < A - 1)
            def _():
                q_right(h, z - d).start()

        @pl.when(z + d <= A - 1)
        def _():
            q_left(h, z + d).wait_recv()

            @pl.when(z > 0)
            def _():
                q_left(h, z + d).start()

    def kv_stage1(h):
        for d1 in range(1, B1):
            kv_in(h, ((b1 + B1 - d1) % B1) * B2 + b2).wait_recv()
            if d1 == B1 - 1:
                @pl.when(h + 2 < H)
                def _():
                    kv_send(h + 2)
            for d2 in range(1, B2):
                kv_pass(h, d1, d2).start()

    def kv_stage2(h):
        kv_loc(h).wait()
        for d2 in range(1, B2):
            for d1 in range(B1):
                kv_in(h, ((b1 + B1 - d1) % B1) * B2 + (b2 + B2 - d2) % B2).wait_recv()

    q_own(0)
    if H > 1:
        kv_send(1)
        q_own(1)
    if H == 1:
        for d in range(1, A):
            q_forward(0, d)
    kv_stage1(0)
    pltpu.make_async_copy(new, nbuf.at[g], loc_n).wait()
    for d in range(1, B):
        n_in(d).wait_recv()
        pk_in(d).wait_recv()
    for d in range(1, A):
        pq_in(d).wait_recv()

    low = z < A // 2
    zf = jnp.where(low, z, A - 1 - z)

    def order(j):
        far = A - 1 - zf
        f = jnp.where(j < far, A - 1 - j, jnp.where(j < A - 1, j - far, zf))
        return jnp.where(low, f, A - 1 - f)

    def attend(h, o, slot):
        q = qbuf[h, o].reshape(R, 128)
        top = jnp.full((R, 128), NEG, jnp.float32)
        for b in range(B):
            s = lax.dot_general(q, kvbuf[h, b, 0], (((1,), (1,)), ((), ())),
                                preferred_element_type=jnp.float32)
            s = s * cc + bias[8 * b:8 * b + 1, :]
            sbuf[:, b * SL:(b + 1) * SL] = s
            for i in range(SL // 128):
                top = jnp.maximum(top, s[:, i * 128:(i + 1) * 128])
        nk = nbuf[:, h, 0].reshape(B * T, 128)
        sn = lax.dot_general(q, nk, (((1,), (1,)), ((), ())), preferred_element_type=jnp.float32)
        pos_k = pkbuf[0]
        for b in range(1, B):
            pos_k = pos_k + pkbuf[b]
        pos_q = jnp.broadcast_to(pqbuf[o][:, None, :], (T, G, 128)).reshape(R, 128)
        seen = pos_k[0:1, :B * T] <= pos_q[:, :B * T]
        sn = jnp.where(seen, sn * cc, NEG)
        m = jnp.maximum(jnp.max(top, axis=-1, keepdims=True), jnp.max(sn, axis=-1, keepdims=True))
        pn = jnp.exp2(sn - m)
        nv = nbuf[:, h, 1].reshape(B * T, 128)
        acc = jnp.dot(pn.astype(jnp.bfloat16), nv, preferred_element_type=jnp.float32)
        total = jnp.zeros((R, 128), jnp.float32)
        for b in range(B):
            p = jnp.exp2(sbuf[:, b * SL:(b + 1) * SL] - m)
            for i in range(SL // 128):
                total = total + p[:, i * 128:(i + 1) * 128]
            acc = acc + jnp.dot(p.astype(jnp.bfloat16), kvbuf[h, b, 1], preferred_element_type=jnp.float32)
        denom = jnp.sum(total, axis=-1, keepdims=True) + jnp.sum(pn, axis=-1, keepdims=True)
        pbuf[slot] = acc * (1.0 / denom)
        lbuf[slot] = jnp.broadcast_to(m + jnp.log(denom) * math.log2(math.e), (R, 128))

    def merge(h, o, slot, copies, data, stats):
        for cp in copies:
            cp.wait_recv()
        x = data[h, o].astype(jnp.float32)
        for r in range(R // 128):
            rows = slice(r * 128, (r + 1) * 128)
            lx = jnp.transpose(jnp.broadcast_to(stats[h, o, 8 * r:8 * r + 1, :], (128, 128)))
            lo = lbuf[slot, rows, :]
            m = jnp.maximum(lx, lo)
            wx, wo = jnp.exp2(lx - m), jnp.exp2(lo - m)
            den = wx + wo
            pbuf[slot, rows, :] = (wx * x[rows] + wo * pbuf[slot, rows, :]) * (1.0 / den)
            lbuf[slot, rows, :] = m + jnp.log(den) * math.log2(math.e)

    def emit(h, o, slot, copies):
        obuf[h, o] = pbuf[slot].astype(jnp.bfloat16)
        for r in range(R // 128):
            stbuf[h, o, 8 * r:8 * r + 8, :] = jnp.transpose(lbuf[slot, r * 128:(r + 1) * 128, :])[0:8, :]
        for cp in copies:
            cp.start()

    steps = H * A
    from_left = FIRST_DELAY + HOP_DELAY * (z - 1)
    from_right = FIRST_DELAY + HOP_DELAY * (A - 2 - z)
    own_delay = FIRST_DELAY + HOP_DELAY * (A - 2)

    def step(s, carry):
        @pl.when(s < steps)
        def _():
            h, j = s // A, s % A

            @pl.when(j == 0)
            def _():
                kv_stage2(h)

                @pl.when(h + 2 < H)
                def _():
                    q_own(h + 2)

            for d in range(1, A):
                @pl.when((j == d) & (h == 0) & (H > 1))
                def _():
                    q_forward(0, d)

                @pl.when((j == d) & (h + 1 < H))
                def _():
                    q_forward(h + 1, d)

            @pl.when((h + 1 < H) & (j == max(A - 2, 0)))
            def _():
                kv_stage1(h + 1)

            o = order(jnp.where((h == 0) & (H > 1), A - 1 - j, j))
            slot = h * A + o
            attend(h, o, slot)

            @pl.when((o > z) & (z == 0))
            def _():
                emit(h, o, slot, o_right(h, o))

            @pl.when((o < z) & (z == A - 1))
            def _():
                emit(h, o, slot, o_left(h, o))

        tr = s - from_left

        @pl.when((z > 0) & (tr >= 0) & (tr < steps))
        def _():
            h, o = tr // A, order(tr % A)

            @pl.when(o > z)
            def _():
                merge(h, o, h * A + o, o_right(h, o), in_l, st_l)
                emit(h, o, h * A + o, o_right(h, o))

        tl = s - from_right

        @pl.when((z < A - 1) & (tl >= 0) & (tl < steps))
        def _():
            h, o = tl // A, order(tl % A)

            @pl.when(o < z)
            def _():
                merge(h, o, h * A + o, o_left(h, o), in_r, st_r)
                emit(h, o, h * A + o, o_left(h, o))

        to = s - own_delay

        @pl.when((to >= 0) & (to % A == A - 1))
        def _():
            h = to // A
            slot = h * A + z

            @pl.when(z > 0)
            def _():
                merge(h, z, slot, o_right(h, z), in_l, st_l)

            @pl.when(z < A - 1)
            def _():
                merge(h, z, slot, o_left(h, z), in_r, st_r)

            fin[h] = pbuf[slot].astype(jnp.bfloat16).reshape(T, G, 128)
            for d in range(1, K):
                out_x(h, d).start()
            out[:, heads(k, h), :] = fin[h, toks(k)]

        return carry

    lax.fori_loop(0, steps + own_delay, step, 0)

    for d in range(1, B):
        n_out(d).wait_send()
        pk_out(d).wait_send()
    for d in range(1, A):
        pq_out(d).wait_send()

    def drain(h, carry):
        for d in range(1, K):
            q_x(h, d).wait_send()
            out_x(h, d).wait_send()
            out_x_in(h, d).wait_recv()
        for d1 in range(1, B1):
            kv_far(h, d1).wait_send()
            for d2 in range(1, B2):
                kv_pass(h, d1, d2).wait_send()
        for d2 in range(1, B2):
            kv_near(h, d2).wait_send()

        def per_owner(o, inner):
            @pl.when((o <= z) & (z < A - 1))
            def _():
                q_right(h, o).wait_send()

            @pl.when((o >= z) & (z > 0))
            def _():
                q_left(h, o).wait_send()

            @pl.when(o > z)
            def _():
                for cp in o_right(h, o):
                    cp.wait_send()

            @pl.when(o < z)
            def _():
                for cp in o_left(h, o):
                    cp.wait_send()

            return inner

        lax.fori_loop(0, A, per_owner, 0)
        return carry

    lax.fori_loop(0, H, drain, 0)


def solution(mesh):
    n_ctx, K = mesh.shape["ctx"], mesh.shape["kvh"]
    A, B, B2 = split_ctx(n_ctx)
    B1 = B // B2

    def body(queries, new_keys, new_values, new_positions, hist_keys, hist_values, page_slots):
        T_loc, QH, width = queries.shape
        T, H = new_keys.shape[0], new_keys.shape[1]
        HPD = QH // K
        G = HPD // H
        slots, page = hist_keys.shape[:2]
        SL = slots * page
        R = T * G
        c = lax.axis_index("ctx")
        z, g = c // B, c % B
        hist = jnp.stack([hist_keys, hist_values]).transpose(3, 0, 1, 2, 4).reshape(H, 2, SL, width)
        new = jnp.stack([new_keys, new_values]).transpose(2, 0, 1, 3)
        lane = jnp.arange(128)
        row = jnp.where(lane // T == g, jnp.tile(new_positions, 128 // T), 0)
        posk = jnp.broadcast_to(row[None, :], (8, 128))
        posq = jnp.broadcast_to(new_positions[:, None], (T, 128))
        ids = z * B * slots + jnp.arange(B * slots, dtype=jnp.int32)
        live = jnp.any(page_slots[None, :] == ids[:, None], axis=1)
        bias = jnp.where(live, 0.0, NEG).astype(jnp.float32).reshape(B, 1, slots, 1)
        bias = jnp.broadcast_to(bias, (B, 8, slots, page)).reshape(B * 8, SL)

        bf, f32, i32 = jnp.bfloat16, jnp.float32, jnp.int32
        V = pltpu.VMEM
        D = pltpu.SemaphoreType.DMA
        kp, ap, bp = max(K - 1, 1), max(A - 1, 1), max(B - 1, 1)
        dims = (A, B, B2, K, H, T, T_loc, G, HPD, SL)
        scratch = [
            V((H, A, T, G, width), bf), V((H, B, 2, SL, width), bf), V((B, H, 2, T, width), bf),
            V((B, 8, 128), i32), V((A, T, 128), i32), V((R, B * SL), f32),
            V((H * A, R, 128), f32), V((H * A, R, 128), f32),
            V((H, A, R, 128), bf), V((H, A, R // 16, 128), f32),
            V((H, A, R, 128), bf), V((H, A, R // 16, 128), f32),
            V((H, A, R, 128), bf), V((H, A, R // 16, 128), f32),
            V((H, T, G, width), bf),
            D((H,)), D((H,)), D, D((H, kp)), D((H, kp)), D((H, A)), D((H, A)), D((H, A)),
            D((H, B)), D((H, B)), D((H, max(B1 - 1, 1), max(B2 - 1, 1))),
            D((bp,)), D((bp,)), D((bp,)), D((bp,)), D((ap,)), D((ap,)),
            D((H, A)), D((H, A)), D((H, A)), D((H, A)),
            D((H, A)), D((H, A)), D((H, A)), D((H, A)), D((H, kp)), D((H, kp)),
        ]
        any_ = pl.BlockSpec(memory_space=pl.ANY)
        vm = pl.BlockSpec(memory_space=pltpu.VMEM)
        work = A * R * (B * SL + B * T) * H
        return pl.pallas_call(
            lambda *refs: kernel(dims, *refs),
            out_shape=jax.ShapeDtypeStruct((T_loc, QH, width), bf),
            in_specs=[any_, any_, any_, vm, vm, vm],
            out_specs=vm,
            scratch_shapes=scratch,
            cost_estimate=pl.CostEstimate(flops=4 * work * width, bytes_accessed=2 * hist.size + 4 * queries.size, transcendentals=work),
            compiler_params=pltpu.CompilerParams(
                collective_id=0, has_side_effects=True, vmem_limit_bytes=40 * 1024 * 1024),
        )(queries, hist, new, posk, posq, bias)

    in_specs = (
        P(("ctx", "kvh"), None, None), P("ctx", "kvh", None), P("ctx", "kvh", None), P("ctx"),
        P("ctx", None, "kvh", None), P("ctx", None, "kvh", None), P(),
    )
    out_specs = P(("ctx", "kvh"), None, None)
    return jax.shard_map(body, mesh=mesh, in_specs=in_specs, out_specs=out_specs, check_vma=False)
```

```python
import math

import jax
import jax.numpy as jnp
from jax import lax
from jax.experimental import pallas as pl
from jax.experimental.pallas import tpu as pltpu
from jax.sharding import PartitionSpec as P

MESH = pl.DeviceIdType.MESH
NEG = -1e30
FIRST_DELAY = 4
HOP_DELAY = 2


def split_ctx(n):
    rows = max(a for a in range(1, n + 1) if n % a == 0 and a * a <= n)
    group = n // rows
    pair = 2 if group > 2 and group % 2 == 0 else 1
    return rows, group, pair


def kernel(dims, q_in, hist, new, posk, posq, bias, out,
           qbuf, kvbuf, nbuf, pkbuf, pqbuf, nvt, sbuf, pbuf, lbuf, obuf, stbuf,
           in_l, st_l, in_r, st_r, fin,
           loc_q, loc_kv, loc_n, qx_s, qx_r, qr_s, ql_s, qz_r, kv_s, kv_r, fw_s,
           n_s, n_r, pk_s, pk_r, pq_s, pq_r, or_s, ol_s, sr_s, sl_s,
           ol_r, or_r, tl_r, tr_r, ox_s, ox_r):
    A, B, B2, K, H, T, T_loc, G, HPD, SL = dims
    B1 = B // B2
    R = T * G
    c = lax.axis_index("ctx")
    k = lax.axis_index("kvh")
    z, g = c // B, c % B
    b1, b2 = g // B2, g % B2
    cc = math.log2(math.e) / math.sqrt(128)

    def remote(src, dst, ss, rs, dev):
        return pltpu.make_async_remote_copy(
            src_ref=src, dst_ref=dst, send_sem=ss, recv_sem=rs,
            device_id=dev, device_id_type=MESH)

    def heads(kk, h):
        return pl.ds(pl.multiple_of(kk * HPD + h * G, G), G)

    def toks(kk):
        return pl.ds(kk * T_loc, T_loc)

    def grp(d):
        return (g + d) % B

    def q_x(h, d):
        kk = (k + d) % K
        return remote(q_in.at[:, heads(kk, h), :], qbuf.at[h, z, toks(k)],
                      qx_s.at[h, d - 1], qx_r.at[h, d - 1], (c, kk))

    def q_x_in(h, d):
        kk = (k + K - d) % K
        dst = qbuf.at[h, z, toks(kk)]
        return remote(dst, dst, qx_s.at[h, d - 1], qx_r.at[h, d - 1], (c, kk))

    def q_loc(h):
        return pltpu.make_async_copy(q_in.at[:, heads(k, h), :], qbuf.at[h, z, toks(k)], loc_q.at[h])

    def kv_loc(h):
        return pltpu.make_async_copy(hist.at[h], kvbuf.at[h, g], loc_kv.at[h])

    def q_right(h, o):
        return remote(qbuf.at[h, o], qbuf.at[h, o], qr_s.at[h, o], qz_r.at[h, o], (c + B, k))

    def q_left(h, o):
        return remote(qbuf.at[h, o], qbuf.at[h, o], ql_s.at[h, o], qz_r.at[h, o], (c - B, k))

    def kv_far(h, d1):
        to = z * B + ((b1 + d1) % B1) * B2 + b2
        return remote(hist.at[h], kvbuf.at[h, g], kv_s.at[h, d1 - 1], kv_r.at[h, g], (to, k))

    def kv_near(h, d2):
        to = z * B + b1 * B2 + (b2 + d2) % B2
        return remote(hist.at[h], kvbuf.at[h, g], kv_s.at[h, B1 - 1 + d2 - 1], kv_r.at[h, g], (to, k))

    def kv_in(h, src):
        dst = kvbuf.at[h, src]
        return remote(dst, dst, kv_s.at[h, 0], kv_r.at[h, src], (c, k))

    def kv_pass(h, d1, d2):
        src = ((b1 + B1 - d1) % B1) * B2 + b2
        to = z * B + b1 * B2 + (b2 + d2) % B2
        return remote(kvbuf.at[h, src], kvbuf.at[h, src], fw_s.at[h, d1 - 1, d2 - 1], kv_r.at[h, src], (to, k))

    def n_out(d):
        return remote(new, nbuf.at[g], n_s.at[d - 1], n_r.at[d - 1], (z * B + grp(d), k))

    def pk_out(d):
        return remote(posk, pkbuf.at[g], pk_s.at[d - 1], pk_r.at[d - 1], (z * B + grp(d), k))

    def pq_out(d):
        return remote(posq, pqbuf.at[z], pq_s.at[d - 1], pq_r.at[d - 1], (((z + d) % A) * B + g, k))

    def n_in(d):
        src = nbuf.at[(g + B - d) % B]
        return remote(src, src, n_s.at[d - 1], n_r.at[d - 1], (c, k))

    def pk_in(d):
        src = pkbuf.at[(g + B - d) % B]
        return remote(src, src, pk_s.at[d - 1], pk_r.at[d - 1], (c, k))

    def pq_in(d):
        src = pqbuf.at[(z + A - d) % A]
        return remote(src, src, pq_s.at[d - 1], pq_r.at[d - 1], (c, k))

    def o_right(h, o):
        return (remote(obuf.at[h, o], in_l.at[h, o], or_s.at[h, o], ol_r.at[h, o], (c + B, k)),
                remote(stbuf.at[h, o], st_l.at[h, o], sr_s.at[h, o], tl_r.at[h, o], (c + B, k)))

    def o_left(h, o):
        return (remote(obuf.at[h, o], in_r.at[h, o], ol_s.at[h, o], or_r.at[h, o], (c - B, k)),
                remote(stbuf.at[h, o], st_r.at[h, o], sl_s.at[h, o], tr_r.at[h, o], (c - B, k)))

    def out_x(h, d):
        kk = (k + d) % K
        return remote(fin.at[h, toks(kk)], out.at[:, heads(k, h), :],
                      ox_s.at[h, d - 1], ox_r.at[h, d - 1], (c, kk))

    def out_x_in(h, d):
        kk = (k + K - d) % K
        dst = out.at[:, heads(kk, h), :]
        return remote(fin.at[h, toks(kk)], dst, ox_s.at[h, d - 1], ox_r.at[h, d - 1], (c, kk))

    barrier = pltpu.get_barrier_semaphore()
    for d in range(1, K):
        pl.semaphore_signal(barrier, inc=1, device_id=(c, (k + d) % K), device_id_type=MESH)
    for d in range(1, A):
        pl.semaphore_signal(barrier, inc=1, device_id=(((z + d) % A) * B + g, k), device_id_type=MESH)
    for d in range(1, B):
        pl.semaphore_signal(barrier, inc=1, device_id=(z * B + grp(d), k), device_id_type=MESH)
    pl.semaphore_wait(barrier, K - 1 + A - 1 + B - 1)

    def kv_send(h):
        for d1 in range(1, B1):
            kv_far(h, d1).start()
        for d2 in range(1, B2):
            kv_near(h, d2).start()
        kv_loc(h).start()

    for h in range(H):
        for d in range(1, K):
            q_x(h, d).start()
        q_loc(h).start()
        if h == 0:
            kv_send(h)
            for d in range(1, B):
                n_out(d).start()
                pk_out(d).start()
            for d in range(1, A):
                pq_out(d).start()
            pltpu.make_async_copy(new, nbuf.at[g], loc_n).start()
            pkbuf[g] = posk[...]
            pqbuf[z] = posq[...]

    def q_own(h):
        q_loc(h).wait()
        for d in range(1, K):
            q_x_in(h, d).wait_recv()

        @pl.when(z < A - 1)
        def _():
            q_right(h, z).start()

        @pl.when(z > 0)
        def _():
            q_left(h, z).start()

    def q_forward(h, d):
        @pl.when(z - d >= 0)
        def _():
            q_right(h, z - d).wait_recv()

            @pl.when(z < A - 1)
            def _():
                q_right(h, z - d).start()

        @pl.when(z + d <= A - 1)
        def _():
            q_left(h, z + d).wait_recv()

            @pl.when(z > 0)
            def _():
                q_left(h, z + d).start()

    def kv_stage1(h):
        for d1 in range(1, B1):
            kv_in(h, ((b1 + B1 - d1) % B1) * B2 + b2).wait_recv()
            if d1 == B1 - 1:
                @pl.when(h + 2 < H)
                def _():
                    kv_send(h + 2)
            for d2 in range(1, B2):
                kv_pass(h, d1, d2).start()

    def kv_stage2(h):
        kv_loc(h).wait()
        for d2 in range(1, B2):
            for d1 in range(B1):
                kv_in(h, ((b1 + B1 - d1) % B1) * B2 + (b2 + B2 - d2) % B2).wait_recv()

    q_own(0)
    if H > 1:
        kv_send(1)
        q_own(1)
    if H == 1:
        for d in range(1, A):
            q_forward(0, d)
    kv_stage1(0)
    pltpu.make_async_copy(new, nbuf.at[g], loc_n).wait()
    for d in range(1, B):
        n_in(d).wait_recv()
        pk_in(d).wait_recv()
    for d in range(1, A):
        pq_in(d).wait_recv()

    low = z < A // 2
    zf = jnp.where(low, z, A - 1 - z)

    def order(j):
        far = A - 1 - zf
        f = jnp.where(j < far, A - 1 - j, jnp.where(j < A - 1, j - far, zf))
        return jnp.where(low, f, A - 1 - f)

    def attend(h, o, slot):
        q = qbuf[h, o].reshape(R, 128)
        fold = (-1, 8, R)
        top = jnp.full((8, R), NEG, jnp.float32)
        for b in range(B):
            s = lax.dot_general(kvbuf[h, b, 0], q, (((1,), (1,)), ((), ())),
                                preferred_element_type=jnp.float32)
            sbuf[b * SL:(b + 1) * SL, :] = s
            for i in range(SL // 128):
                part = jnp.max(s[i * 128:(i + 1) * 128].reshape(fold), axis=0)
                top = jnp.maximum(top, part + bias[b * (SL // 128) + i])
        nk = nbuf[:, h, 0].reshape(B * T, 128)
        sn = lax.dot_general(nk, q, (((1,), (1,)), ((), ())), preferred_element_type=jnp.float32)
        pos_k = pkbuf[...].reshape(B * T, 128)
        pos_k = jnp.concatenate([pos_k] * (R // 128), axis=1)
        sn = jnp.where(pos_k <= pqbuf[o][0:1, :], sn, NEG)
        top = jnp.maximum(top, jnp.max(sn.reshape(fold), axis=0))
        m = jnp.max(top, axis=0, keepdims=True) * cc
        pn = jnp.exp2(sn * cc - m)
        total = jnp.sum(pn.reshape(fold), axis=0)
        acc = jnp.dot(nvt[...], pn.astype(jnp.bfloat16), preferred_element_type=jnp.float32)
        for b0 in range(0, B, 2):
            ps, vs = [], []
            for b in range(b0, min(b0 + 2, B)):
                for i in range(SL // 128):
                    row = b * SL + i * 128
                    p = jnp.exp2(sbuf[row:row + 128, :] * cc - (m - bias[b * (SL // 128) + i]))
                    total = total + jnp.sum(p.reshape(fold), axis=0)
                    ps.append(p.astype(jnp.bfloat16))
                    vs.append(kvbuf[h, b, 1, i * 128:(i + 1) * 128, :])
            acc = acc + jnp.dot(jnp.concatenate(vs, axis=1), jnp.concatenate(ps, axis=0),
                                preferred_element_type=jnp.float32)
        denom = jnp.sum(total, axis=0, keepdims=True)
        pbuf[slot] = acc * (1.0 / denom)
        lbuf[slot] = jnp.broadcast_to(m + jnp.log(denom) * math.log2(math.e), (8, R))

    def merge(h, o, slot, copies, data, stats):
        for cp in copies:
            cp.wait_recv()
        x = data[h, o].astype(jnp.float32)
        lx, lo = stats[h, o], lbuf[slot]
        m = jnp.maximum(lx, lo)
        wx, wo = jnp.exp2(lx - m), jnp.exp2(lo - m)
        den = wx + wo
        inv = 1.0 / den
        pbuf[slot] = (wx * inv)[0:1] * x + (wo * inv)[0:1] * pbuf[slot]
        lbuf[slot] = m + jnp.log(den) * math.log2(math.e)

    def emit(h, o, slot, copies):
        obuf[h, o] = pbuf[slot].astype(jnp.bfloat16)
        stbuf[h, o] = lbuf[slot]
        for cp in copies:
            cp.start()

    steps = H * A
    from_left = FIRST_DELAY + HOP_DELAY * (z - 1)
    from_right = FIRST_DELAY + HOP_DELAY * (A - 2 - z)
    own_delay = FIRST_DELAY + HOP_DELAY * (A - 2)

    def step(s, carry):
        @pl.when(s < steps)
        def _():
            h, j = s // A, s % A

            @pl.when(j == 0)
            def _():
                kv_stage2(h)
                nv = nbuf[:, h, 1].reshape(B * T, 128).astype(jnp.float32)
                nvt[...] = jnp.transpose(nv).astype(jnp.bfloat16)

                @pl.when(h + 2 < H)
                def _():
                    q_own(h + 2)

            for d in range(1, A):
                @pl.when((j == d) & (h == 0) & (H > 1))
                def _():
                    q_forward(0, d)

                @pl.when((j == d) & (h + 1 < H))
                def _():
                    q_forward(h + 1, d)

            @pl.when((h + 1 < H) & (j == max(A - 2, 0)))
            def _():
                kv_stage1(h + 1)

            o = order(jnp.where((h == 0) & (H > 1), A - 1 - j, j))
            slot = h * A + o
            attend(h, o, slot)

            @pl.when((o > z) & (z == 0))
            def _():
                emit(h, o, slot, o_right(h, o))

            @pl.when((o < z) & (z == A - 1))
            def _():
                emit(h, o, slot, o_left(h, o))

        tr = s - from_left

        @pl.when((z > 0) & (tr >= 0) & (tr < steps))
        def _():
            h, o = tr // A, order(tr % A)

            @pl.when(o > z)
            def _():
                merge(h, o, h * A + o, o_right(h, o), in_l, st_l)
                emit(h, o, h * A + o, o_right(h, o))

        tl = s - from_right

        @pl.when((z < A - 1) & (tl >= 0) & (tl < steps))
        def _():
            h, o = tl // A, order(tl % A)

            @pl.when(o < z)
            def _():
                merge(h, o, h * A + o, o_left(h, o), in_r, st_r)
                emit(h, o, h * A + o, o_left(h, o))

        to = s - own_delay

        @pl.when((to >= 0) & (to % A == A - 1))
        def _():
            h = to // A
            slot = h * A + z

            @pl.when(z > 0)
            def _():
                merge(h, z, slot, o_right(h, z), in_l, st_l)

            @pl.when(z < A - 1)
            def _():
                merge(h, z, slot, o_left(h, z), in_r, st_r)

            fin[h] = jnp.transpose(pbuf[slot]).astype(jnp.bfloat16).reshape(T, G, 128)
            for d in range(1, K):
                out_x(h, d).start()
            out[:, heads(k, h), :] = fin[h, toks(k)]

        return carry

    lax.fori_loop(0, steps + own_delay, step, 0)

    for d in range(1, B):
        n_out(d).wait_send()
        pk_out(d).wait_send()
    for d in range(1, A):
        pq_out(d).wait_send()

    def drain(h, carry):
        for d in range(1, K):
            q_x(h, d).wait_send()
            out_x(h, d).wait_send()
            out_x_in(h, d).wait_recv()
        for d1 in range(1, B1):
            kv_far(h, d1).wait_send()
            for d2 in range(1, B2):
                kv_pass(h, d1, d2).wait_send()
        for d2 in range(1, B2):
            kv_near(h, d2).wait_send()

        def per_owner(o, inner):
            @pl.when((o <= z) & (z < A - 1))
            def _():
                q_right(h, o).wait_send()

            @pl.when((o >= z) & (z > 0))
            def _():
                q_left(h, o).wait_send()

            @pl.when(o > z)
            def _():
                for cp in o_right(h, o):
                    cp.wait_send()

            @pl.when(o < z)
            def _():
                for cp in o_left(h, o):
                    cp.wait_send()

            return inner

        lax.fori_loop(0, A, per_owner, 0)
        return carry

    lax.fori_loop(0, H, drain, 0)


def solution(mesh):
    n_ctx, K = mesh.shape["ctx"], mesh.shape["kvh"]
    A, B, B2 = split_ctx(n_ctx)
    B1 = B // B2

    def body(queries, new_keys, new_values, new_positions, hist_keys, hist_values, page_slots):
        T_loc, QH, width = queries.shape
        T, H = new_keys.shape[0], new_keys.shape[1]
        HPD = QH // K
        G = HPD // H
        slots, page = hist_keys.shape[:2]
        SL = slots * page
        R = T * G
        c = lax.axis_index("ctx")
        z = c // B
        keys = hist_keys.transpose(2, 0, 1, 3)
        values = hist_values.transpose(2, 0, 3, 1)
        hist = jnp.stack([keys, values], axis=1).reshape(H, 2, SL, width)
        new = jnp.stack([new_keys, new_values]).transpose(2, 0, 1, 3)
        posk = jnp.broadcast_to(new_positions[:, None], (T, 128))
        posq = jnp.broadcast_to(jnp.repeat(new_positions, G)[None, :], (8, R))
        ids = z * B * slots + jnp.arange(B * slots, dtype=jnp.int32)
        live = jnp.any(page_slots[None, :] == ids[:, None], axis=1)
        bias = jnp.where(live, 0.0, NEG).astype(jnp.float32)

        bf, f32, i32 = jnp.bfloat16, jnp.float32, jnp.int32
        V = pltpu.VMEM
        D = pltpu.SemaphoreType.DMA
        kp, ap, bp = max(K - 1, 1), max(A - 1, 1), max(B - 1, 1)
        dims = (A, B, B2, K, H, T, T_loc, G, HPD, SL)
        scratch = [
            V((H, A, T, G, width), bf), V((H, B, 2, SL, width), bf), V((B, H, 2, T, width), bf),
            V((B, T, 128), i32), V((A, 8, R), i32), V((width, B * T), bf), V((B * SL, R), f32),
            V((H * A, 128, R), f32), V((H * A, 8, R), f32),
            V((H, A, 128, R), bf), V((H, A, 8, R), f32),
            V((H, A, 128, R), bf), V((H, A, 8, R), f32),
            V((H, A, 128, R), bf), V((H, A, 8, R), f32),
            V((H, T, G, width), bf),
            D((H,)), D((H,)), D, D((H, kp)), D((H, kp)), D((H, A)), D((H, A)), D((H, A)),
            D((H, B)), D((H, B)), D((H, max(B1 - 1, 1), max(B2 - 1, 1))),
            D((bp,)), D((bp,)), D((bp,)), D((bp,)), D((ap,)), D((ap,)),
            D((H, A)), D((H, A)), D((H, A)), D((H, A)),
            D((H, A)), D((H, A)), D((H, A)), D((H, A)), D((H, kp)), D((H, kp)),
        ]
        any_ = pl.BlockSpec(memory_space=pl.ANY)
        vm = pl.BlockSpec(memory_space=pltpu.VMEM)
        work = A * R * (B * SL + B * T) * H
        return pl.pallas_call(
            lambda *refs: kernel(dims, *refs),
            out_shape=jax.ShapeDtypeStruct((T_loc, QH, width), bf),
            in_specs=[any_, any_, any_, vm, vm, pl.BlockSpec(memory_space=pltpu.SMEM)],
            out_specs=vm,
            scratch_shapes=scratch,
            cost_estimate=pl.CostEstimate(flops=4 * work * width, bytes_accessed=2 * hist.size + 4 * queries.size, transcendentals=work),
            compiler_params=pltpu.CompilerParams(
                collective_id=0, has_side_effects=True, vmem_limit_bytes=40 * 1024 * 1024),
        )(queries, hist, new, posk, posq, bias)

    in_specs = (
        P(("ctx", "kvh"), None, None), P("ctx", "kvh", None), P("ctx", "kvh", None), P("ctx"),
        P("ctx", None, "kvh", None), P("ctx", None, "kvh", None), P(),
    )
    out_specs = P(("ctx", "kvh"), None, None)
    return jax.shard_map(body, mesh=mesh, in_specs=in_specs, out_specs=out_specs, check_vma=False)
```

```python
import math

import jax
import jax.numpy as jnp
from jax import lax
from jax.experimental import pallas as pl
from jax.experimental.pallas import tpu as pltpu
from jax.sharding import PartitionSpec as P

MESH = pl.DeviceIdType.MESH
NEG = -1e30
FIRST_DELAY = 4
HOP_DELAY = 2


def split_ctx(n):
    rows = max(a for a in range(1, n + 1) if n % a == 0 and a * a <= n)
    group = n // rows
    pair = 2 if group > 2 and group % 2 == 0 else 1
    return rows, group, pair


def kernel(dims, q_in, hist, new, pos, pages, out,
           qbuf, kvbuf, nbuf, pkbuf, pqbuf, bias, nvt, sbuf, pbuf, lbuf, obuf, stbuf,
           in_l, st_l, in_r, st_r, fin,
           loc_q, loc_kv, loc_n, qx_s, qx_r, qr_s, ql_s, qz_r, kv_s, kv_r, fw_s,
           n_s, n_r, pk_s, pk_r, pq_s, pq_r, or_s, ol_s, sr_s, sl_s,
           ol_r, or_r, tl_r, tr_r, ox_s, ox_r):
    A, B, B2, K, H, T, T_loc, G, HPD, SL = dims
    B1 = B // B2
    R = T * G
    c = lax.axis_index("ctx")
    k = lax.axis_index("kvh")
    z, g = c // B, c % B
    b1, b2 = g // B2, g % B2
    cc = math.log2(math.e) / math.sqrt(128)

    def remote(src, dst, ss, rs, dev):
        return pltpu.make_async_remote_copy(
            src_ref=src, dst_ref=dst, send_sem=ss, recv_sem=rs,
            device_id=dev, device_id_type=MESH)

    def heads(kk, h):
        return pl.ds(pl.multiple_of(kk * HPD + h * G, G), G)

    def toks(kk):
        return pl.ds(kk * T_loc, T_loc)

    def grp(d):
        return (g + d) % B

    def q_x(h, d):
        kk = (k + d) % K
        return remote(q_in.at[:, heads(kk, h), :], qbuf.at[h, z, toks(k)],
                      qx_s.at[h, d - 1], qx_r.at[h, d - 1], (c, kk))

    def q_x_in(h, d):
        kk = (k + K - d) % K
        dst = qbuf.at[h, z, toks(kk)]
        return remote(dst, dst, qx_s.at[h, d - 1], qx_r.at[h, d - 1], (c, kk))

    def q_loc(h):
        return pltpu.make_async_copy(q_in.at[:, heads(k, h), :], qbuf.at[h, z, toks(k)], loc_q.at[h])

    def kv_loc(h):
        return pltpu.make_async_copy(hist.at[h], kvbuf.at[h, g], loc_kv.at[h])

    def q_right(h, o):
        return remote(qbuf.at[h, o], qbuf.at[h, o], qr_s.at[h, o], qz_r.at[h, o], (c + B, k))

    def q_left(h, o):
        return remote(qbuf.at[h, o], qbuf.at[h, o], ql_s.at[h, o], qz_r.at[h, o], (c - B, k))

    def kv_far(h, d1):
        to = z * B + ((b1 + d1) % B1) * B2 + b2
        return remote(hist.at[h], kvbuf.at[h, g], kv_s.at[h, d1 - 1], kv_r.at[h, g], (to, k))

    def kv_near(h, d2):
        to = z * B + b1 * B2 + (b2 + d2) % B2
        return remote(hist.at[h], kvbuf.at[h, g], kv_s.at[h, B1 - 1 + d2 - 1], kv_r.at[h, g], (to, k))

    def kv_in(h, src):
        dst = kvbuf.at[h, src]
        return remote(dst, dst, kv_s.at[h, 0], kv_r.at[h, src], (c, k))

    def kv_pass(h, d1, d2):
        src = ((b1 + B1 - d1) % B1) * B2 + b2
        to = z * B + b1 * B2 + (b2 + d2) % B2
        return remote(kvbuf.at[h, src], kvbuf.at[h, src], fw_s.at[h, d1 - 1, d2 - 1], kv_r.at[h, src], (to, k))

    def n_out(d):
        return remote(new, nbuf.at[g], n_s.at[d - 1], n_r.at[d - 1], (z * B + grp(d), k))

    def pk_out(d):
        return remote(pkbuf.at[g], pkbuf.at[g], pk_s.at[d - 1], pk_r.at[d - 1], (z * B + grp(d), k))

    def pq_out(d):
        return remote(pqbuf.at[z], pqbuf.at[z], pq_s.at[d - 1], pq_r.at[d - 1], (((z + d) % A) * B + g, k))

    def n_in(d):
        src = nbuf.at[(g + B - d) % B]
        return remote(src, src, n_s.at[d - 1], n_r.at[d - 1], (c, k))

    def pk_in(d):
        src = pkbuf.at[(g + B - d) % B]
        return remote(src, src, pk_s.at[d - 1], pk_r.at[d - 1], (c, k))

    def pq_in(d):
        src = pqbuf.at[(z + A - d) % A]
        return remote(src, src, pq_s.at[d - 1], pq_r.at[d - 1], (c, k))

    def o_right(h, o):
        return (remote(obuf.at[h, o], in_l.at[h, o], or_s.at[h, o], ol_r.at[h, o], (c + B, k)),
                remote(stbuf.at[h, o, 0:1], st_l.at[h, o, 0:1], sr_s.at[h, o], tl_r.at[h, o], (c + B, k)))

    def o_left(h, o):
        return (remote(obuf.at[h, o], in_r.at[h, o], ol_s.at[h, o], or_r.at[h, o], (c - B, k)),
                remote(stbuf.at[h, o, 0:1], st_r.at[h, o, 0:1], sl_s.at[h, o], tr_r.at[h, o], (c - B, k)))

    def out_x(h, d):
        kk = (k + d) % K
        return remote(fin.at[h, toks(kk)], out.at[:, heads(k, h), :],
                      ox_s.at[h, d - 1], ox_r.at[h, d - 1], (c, kk))

    def out_x_in(h, d):
        kk = (k + K - d) % K
        dst = out.at[:, heads(kk, h), :]
        return remote(fin.at[h, toks(kk)], dst, ox_s.at[h, d - 1], ox_r.at[h, d - 1], (c, kk))

    def iota(shape, axis):
        return lax.broadcasted_iota(jnp.int32, shape, axis)

    row = jnp.broadcast_to(pos[...].astype(jnp.float32), (T, T))
    column = jnp.sum(jnp.where(iota((T, T), 0) == iota((T, T), 1), row, 0.0), axis=1, keepdims=True)
    pkbuf[g] = jnp.broadcast_to(column, (T, 128)).astype(jnp.int32)
    own = iota((T, R), 0) == iota((T, R), 1) // G
    spread = jnp.sum(jnp.where(own, jnp.broadcast_to(column, (T, R)), 0.0), axis=0, keepdims=True)
    pqbuf[z] = jnp.broadcast_to(spread, (8, R)).astype(jnp.int32)

    barrier = pltpu.get_barrier_semaphore()
    for d in range(1, K):
        pl.semaphore_signal(barrier, inc=1, device_id=(c, (k + d) % K), device_id_type=MESH)
    for d in range(1, A):
        pl.semaphore_signal(barrier, inc=1, device_id=(((z + d) % A) * B + g, k), device_id_type=MESH)
    for d in range(1, B):
        pl.semaphore_signal(barrier, inc=1, device_id=(z * B + grp(d), k), device_id_type=MESH)
    pl.semaphore_wait(barrier, K - 1 + A - 1 + B - 1)

    def kv_send(h):
        for d1 in range(1, B1):
            kv_far(h, d1).start()
        for d2 in range(1, B2):
            kv_near(h, d2).start()
        kv_loc(h).start()

    for h in range(H):
        for d in range(1, K):
            q_x(h, d).start()
        q_loc(h).start()
        kv_send(h)
        if h == 0:
            for d in range(1, B):
                n_out(d).start()
                pk_out(d).start()
            for d in range(1, A):
                pq_out(d).start()
            pltpu.make_async_copy(new, nbuf.at[g], loc_n).start()

    def q_own(h):
        q_loc(h).wait()
        for d in range(1, K):
            q_x_in(h, d).wait_recv()

        @pl.when(z < A - 1)
        def _():
            q_right(h, z).start()

        @pl.when(z > 0)
        def _():
            q_left(h, z).start()

    def q_forward(h, d):
        @pl.when(z - d >= 0)
        def _():
            q_right(h, z - d).wait_recv()

            @pl.when(z < A - 1)
            def _():
                q_right(h, z - d).start()

        @pl.when(z + d <= A - 1)
        def _():
            q_left(h, z + d).wait_recv()

            @pl.when(z > 0)
            def _():
                q_left(h, z + d).start()

    def kv_stage1(h):
        for d1 in range(1, B1):
            kv_in(h, ((b1 + B1 - d1) % B1) * B2 + b2).wait_recv()
            for d2 in range(1, B2):
                kv_pass(h, d1, d2).start()

    def kv_stage2(h):
        kv_loc(h).wait()
        for d2 in range(1, B2):
            for d1 in range(B1):
                kv_in(h, ((b1 + B1 - d1) % B1) * B2 + (b2 + B2 - d2) % B2).wait_recv()

    for i in range(B * SL // 128):
        hit = jnp.where(pages[...] == z * (B * SL // 128) + i, 1.0, 0.0)
        hit = jnp.max(hit, axis=1, keepdims=True)
        bias[i] = jnp.broadcast_to((1.0 - hit) * NEG, (8, R))

    q_own(0)
    if H > 1:
        q_own(1)
    if H == 1:
        for d in range(1, A):
            q_forward(0, d)
    kv_stage1(0)
    pltpu.make_async_copy(new, nbuf.at[g], loc_n).wait()
    for d in range(1, B):
        n_in(d).wait_recv()
        pk_in(d).wait_recv()
    for d in range(1, A):
        pq_in(d).wait_recv()

    low = z < A // 2
    zf = jnp.where(low, z, A - 1 - z)

    def order(j):
        far = A - 1 - zf
        f = jnp.where(j < far, A - 1 - j, jnp.where(j < A - 1, j - far, zf))
        return jnp.where(low, f, A - 1 - f)

    def attend(h, o, slot):
        q = qbuf[h, o].reshape(R, 128)
        fold = (-1, 8, R)
        top = jnp.full((8, R), NEG, jnp.float32)
        for b in range(B):
            s = lax.dot_general(kvbuf[h, b, 0], q, (((1,), (1,)), ((), ())),
                                preferred_element_type=jnp.float32)
            sbuf[b * SL:(b + 1) * SL, :] = s
            for i in range(SL // 128):
                part = jnp.max(s[i * 128:(i + 1) * 128].reshape(fold), axis=0)
                top = jnp.maximum(top, part + bias[b * (SL // 128) + i])
        nk = nbuf[:, h, 0].reshape(B * T, 128)
        sn = lax.dot_general(nk, q, (((1,), (1,)), ((), ())), preferred_element_type=jnp.float32)
        pos_k = pkbuf[...].reshape(B * T, 128)
        pos_k = jnp.concatenate([pos_k] * (R // 128), axis=1)
        sn = jnp.where(pos_k <= pqbuf[o][0:1, :], sn, NEG)
        top = jnp.maximum(top, jnp.max(sn.reshape(fold), axis=0))
        m = jnp.max(top, axis=0, keepdims=True) * cc
        pn = jnp.exp2(sn * cc - m)
        total = jnp.sum(pn.reshape(fold), axis=0)
        acc = jnp.dot(nvt[...], pn.astype(jnp.bfloat16), preferred_element_type=jnp.float32)
        for b0 in range(0, B, 2):
            ps, vs = [], []
            for b in range(b0, min(b0 + 2, B)):
                for i in range(SL // 128):
                    row = b * SL + i * 128
                    p = jnp.exp2(sbuf[row:row + 128, :] * cc - (m - bias[b * (SL // 128) + i, 0:1, :]))
                    total = total + jnp.sum(p.reshape(fold), axis=0)
                    ps.append(p.astype(jnp.bfloat16))
                    vs.append(kvbuf[h, b, 1, i * 128:(i + 1) * 128, :])
            acc = acc + jnp.dot(jnp.concatenate(vs, axis=1), jnp.concatenate(ps, axis=0),
                                preferred_element_type=jnp.float32)
        denom = jnp.sum(total, axis=0, keepdims=True)
        pbuf[slot] = acc * (1.0 / denom)
        lbuf[slot] = jnp.broadcast_to(m + jnp.log(denom) * math.log2(math.e), (8, R))

    def merge(h, o, slot, copies, data, stats):
        for cp in copies:
            cp.wait_recv()
        x = data[h, o].astype(jnp.float32)
        lx, lo = stats[h, o, 0:1, :], lbuf[slot, 0:1, :]
        m = jnp.maximum(lx, lo)
        wx, wo = jnp.exp2(lx - m), jnp.exp2(lo - m)
        den = wx + wo
        inv = 1.0 / den
        pbuf[slot] = (wx * inv) * x + (wo * inv) * pbuf[slot]
        lbuf[slot] = jnp.broadcast_to(m + jnp.log(den) * math.log2(math.e), (8, R))

    def emit(h, o, slot, copies):
        obuf[h, o] = pbuf[slot].astype(jnp.bfloat16)
        stbuf[h, o] = lbuf[slot]
        for cp in copies:
            cp.start()

    steps = H * A
    from_left = FIRST_DELAY + HOP_DELAY * (z - 1)
    from_right = FIRST_DELAY + HOP_DELAY * (A - 2 - z)
    own_delay = FIRST_DELAY + HOP_DELAY * (A - 2)

    def step(s, carry):
        @pl.when(s < steps)
        def _():
            h, j = s // A, s % A

            @pl.when(j == 0)
            def _():
                kv_stage2(h)
                nv = nbuf[:, h, 1].reshape(B * T, 128).astype(jnp.float32)
                nvt[...] = jnp.transpose(nv).astype(jnp.bfloat16)

                @pl.when(h + 2 < H)
                def _():
                    q_own(h + 2)

            for d in range(1, A):
                @pl.when((j == d) & (h == 0) & (H > 1))
                def _():
                    q_forward(0, d)

                @pl.when((j == d) & (h + 1 < H))
                def _():
                    q_forward(h + 1, d)

            @pl.when((h + 1 < H) & (j == max(A - 2, 0)))
            def _():
                kv_stage1(h + 1)

            o = order(jnp.where((h == 0) & (H > 1), A - 1 - j, j))
            slot = h * A + o
            attend(h, o, slot)

            @pl.when((o > z) & (z == 0))
            def _():
                emit(h, o, slot, o_right(h, o))

            @pl.when((o < z) & (z == A - 1))
            def _():
                emit(h, o, slot, o_left(h, o))

        tr = s - from_left

        @pl.when((z > 0) & (tr >= 0) & (tr < steps))
        def _():
            h, o = tr // A, order(tr % A)

            @pl.when(o > z)
            def _():
                merge(h, o, h * A + o, o_right(h, o), in_l, st_l)
                emit(h, o, h * A + o, o_right(h, o))

        tl = s - from_right

        @pl.when((z < A - 1) & (tl >= 0) & (tl < steps))
        def _():
            h, o = tl // A, order(tl % A)

            @pl.when(o < z)
            def _():
                merge(h, o, h * A + o, o_left(h, o), in_r, st_r)
                emit(h, o, h * A + o, o_left(h, o))

        to = s - own_delay

        @pl.when((to >= 0) & (to % A == A - 1))
        def _():
            h = to // A
            slot = h * A + z

            @pl.when(z > 0)
            def _():
                merge(h, z, slot, o_right(h, z), in_l, st_l)

            @pl.when(z < A - 1)
            def _():
                merge(h, z, slot, o_left(h, z), in_r, st_r)

            fin[h] = jnp.transpose(pbuf[slot]).astype(jnp.bfloat16).reshape(T, G, 128)
            for d in range(1, K):
                out_x(h, d).start()
            out[:, heads(k, h), :] = fin[h, toks(k)]

        return carry

    lax.fori_loop(0, steps + own_delay, step, 0)

    for d in range(1, B):
        n_out(d).wait_send()
        pk_out(d).wait_send()
    for d in range(1, A):
        pq_out(d).wait_send()

    def drain(h, carry):
        for d in range(1, K):
            q_x(h, d).wait_send()
            out_x(h, d).wait_send()
            out_x_in(h, d).wait_recv()
        for d1 in range(1, B1):
            kv_far(h, d1).wait_send()
            for d2 in range(1, B2):
                kv_pass(h, d1, d2).wait_send()
        for d2 in range(1, B2):
            kv_near(h, d2).wait_send()

        def per_owner(o, inner):
            @pl.when((o <= z) & (z < A - 1))
            def _():
                q_right(h, o).wait_send()

            @pl.when((o >= z) & (z > 0))
            def _():
                q_left(h, o).wait_send()

            @pl.when(o > z)
            def _():
                for cp in o_right(h, o):
                    cp.wait_send()

            @pl.when(o < z)
            def _():
                for cp in o_left(h, o):
                    cp.wait_send()

            return inner

        lax.fori_loop(0, A, per_owner, 0)
        return carry

    lax.fori_loop(0, H, drain, 0)


def solution(mesh):
    n_ctx, K = mesh.shape["ctx"], mesh.shape["kvh"]
    A, B, B2 = split_ctx(n_ctx)
    B1 = B // B2

    def body(queries, new_keys, new_values, new_positions, hist_keys, hist_values, page_slots):
        T_loc, QH, width = queries.shape
        T, H = new_keys.shape[0], new_keys.shape[1]
        HPD = QH // K
        G = HPD // H
        slots, page = hist_keys.shape[:2]
        SL = slots * page
        R = T * G
        keys = hist_keys.transpose(2, 0, 1, 3)
        values = hist_values.transpose(2, 0, 3, 1)
        hist = jnp.stack([keys, values], axis=1).reshape(H, 2, SL, width)
        new = jnp.stack([new_keys, new_values]).transpose(2, 0, 1, 3)

        bf, f32, i32 = jnp.bfloat16, jnp.float32, jnp.int32
        V = pltpu.VMEM
        D = pltpu.SemaphoreType.DMA
        kp, ap, bp = max(K - 1, 1), max(A - 1, 1), max(B - 1, 1)
        dims = (A, B, B2, K, H, T, T_loc, G, HPD, SL)
        scratch = [
            V((H, A, T, G, width), bf), V((H, B, 2, SL, width), bf), V((B, H, 2, T, width), bf),
            V((B, T, 128), i32), V((A, 8, R), i32), V((B * slots, 8, R), f32), V((width, B * T), bf), V((B * SL, R), f32),
            V((H * A, 128, R), f32), V((H * A, 8, R), f32),
            V((H, A, 128, R), bf), V((H, A, 8, R), f32),
            V((H, A, 128, R), bf), V((H, A, 8, R), f32),
            V((H, A, 128, R), bf), V((H, A, 8, R), f32),
            V((H, T, G, width), bf),
            D((H,)), D((H,)), D, D((H, kp)), D((H, kp)), D((H, A)), D((H, A)), D((H, A)),
            D((H, B)), D((H, B)), D((H, max(B1 - 1, 1), max(B2 - 1, 1))),
            D((bp,)), D((bp,)), D((bp,)), D((bp,)), D((ap,)), D((ap,)),
            D((H, A)), D((H, A)), D((H, A)), D((H, A)),
            D((H, A)), D((H, A)), D((H, A)), D((H, A)), D((H, kp)), D((H, kp)),
        ]
        any_ = pl.BlockSpec(memory_space=pl.ANY)
        vm = pl.BlockSpec(memory_space=pltpu.VMEM)
        work = A * R * (B * SL + B * T) * H
        return pl.pallas_call(
            lambda *refs: kernel(dims, *refs),
            out_shape=jax.ShapeDtypeStruct((T_loc, QH, width), bf),
            in_specs=[any_, any_, any_, vm, vm],
            out_specs=vm,
            scratch_shapes=scratch,
            cost_estimate=pl.CostEstimate(flops=4 * work * width, bytes_accessed=2 * hist.size + 4 * queries.size, transcendentals=work),
            compiler_params=pltpu.CompilerParams(
                collective_id=0, has_side_effects=True, vmem_limit_bytes=40 * 1024 * 1024),
        )(queries, hist, new, new_positions[None, :], page_slots[None, :])

    in_specs = (
        P(("ctx", "kvh"), None, None), P("ctx", "kvh", None), P("ctx", "kvh", None), P("ctx"),
        P("ctx", None, "kvh", None), P("ctx", None, "kvh", None), P(),
    )
    out_specs = P(("ctx", "kvh"), None, None)
    return jax.shard_map(body, mesh=mesh, in_specs=in_specs, out_specs=out_specs, check_vma=False)
```

```python
import math

import jax
import jax.numpy as jnp
from jax import lax
from jax.experimental import pallas as pl
from jax.experimental.pallas import tpu as pltpu
from jax.sharding import PartitionSpec as P

MESH = pl.DeviceIdType.MESH
NEG = -1e30
FIRST_DELAY = 4
HOP_DELAY = 2


def split_ctx(n):
    rows = max(a for a in range(1, n + 1) if n % a == 0 and a * a <= n)
    group = n // rows
    pair = 2 if group > 2 and group % 2 == 0 else 1
    return rows, group, pair


def kernel(dims, q_in, hist, new, pos, pages, out,
           qbuf, kvbuf, nbuf, pkbuf, pqbuf, bias, nvt, sbuf, pbuf, lbuf, obuf, stbuf,
           in_l, st_l, in_r, st_r, fin,
           loc_q, loc_kv, loc_n, qx_s, qx_r, qr_s, ql_s, qz_r, kv_s, kv_r, fw_s,
           n_s, n_r, pk_s, pk_r, pq_s, pq_r, or_s, ol_s, sr_s, sl_s,
           ol_r, or_r, tl_r, tr_r, ox_s, ox_r):
    A, B, B2, K, H, T, T_loc, G, HPD, SL = dims
    B1 = B // B2
    R = T * G
    c = lax.axis_index("ctx")
    k = lax.axis_index("kvh")
    z, g = c // B, c % B
    b1, b2 = g // B2, g % B2
    cc = math.log2(math.e) / math.sqrt(128)

    def remote(src, dst, ss, rs, dev):
        return pltpu.make_async_remote_copy(
            src_ref=src, dst_ref=dst, send_sem=ss, recv_sem=rs,
            device_id=dev, device_id_type=MESH)

    def heads(kk, h):
        return pl.ds(pl.multiple_of(kk * HPD + h * G, G), G)

    def toks(kk):
        return pl.ds(kk * T_loc, T_loc)

    def grp(d):
        return (g + d) % B

    def q_x(h, d):
        kk = (k + d) % K
        return remote(q_in.at[:, heads(kk, h), :], qbuf.at[h, z, toks(k)],
                      qx_s.at[h, d - 1], qx_r.at[h, d - 1], (c, kk))

    def q_x_in(h, d):
        kk = (k + K - d) % K
        dst = qbuf.at[h, z, toks(kk)]
        return remote(dst, dst, qx_s.at[h, d - 1], qx_r.at[h, d - 1], (c, kk))

    def q_loc(h):
        return pltpu.make_async_copy(q_in.at[:, heads(k, h), :], qbuf.at[h, z, toks(k)], loc_q.at[h])

    def kv_loc(h):
        return pltpu.make_async_copy(hist.at[h], kvbuf.at[h, g], loc_kv.at[h])

    def q_right(h, o):
        return remote(qbuf.at[h, o], qbuf.at[h, o], qr_s.at[h, o], qz_r.at[h, o], (c + B, k))

    def q_left(h, o):
        return remote(qbuf.at[h, o], qbuf.at[h, o], ql_s.at[h, o], qz_r.at[h, o], (c - B, k))

    def kv_far(h, d1):
        to = z * B + ((b1 + d1) % B1) * B2 + b2
        return remote(hist.at[h], kvbuf.at[h, g], kv_s.at[h, d1 - 1], kv_r.at[h, g], (to, k))

    def kv_near(h, d2):
        to = z * B + b1 * B2 + (b2 + d2) % B2
        return remote(hist.at[h], kvbuf.at[h, g], kv_s.at[h, B1 - 1 + d2 - 1], kv_r.at[h, g], (to, k))

    def kv_in(h, src):
        dst = kvbuf.at[h, src]
        return remote(dst, dst, kv_s.at[h, 0], kv_r.at[h, src], (c, k))

    def kv_pass(h, d1, d2):
        src = ((b1 + B1 - d1) % B1) * B2 + b2
        to = z * B + b1 * B2 + (b2 + d2) % B2
        return remote(kvbuf.at[h, src], kvbuf.at[h, src], fw_s.at[h, d1 - 1, d2 - 1], kv_r.at[h, src], (to, k))

    def n_out(d):
        return remote(new, nbuf.at[g], n_s.at[d - 1], n_r.at[d - 1], (z * B + grp(d), k))

    def pk_out(d):
        return remote(pkbuf.at[g], pkbuf.at[g], pk_s.at[d - 1], pk_r.at[d - 1], (z * B + grp(d), k))

    def pq_out(d):
        return remote(pqbuf.at[z], pqbuf.at[z], pq_s.at[d - 1], pq_r.at[d - 1], (((z + d) % A) * B + g, k))

    def n_in(d):
        src = nbuf.at[(g + B - d) % B]
        return remote(src, src, n_s.at[d - 1], n_r.at[d - 1], (c, k))

    def pk_in(d):
        src = pkbuf.at[(g + B - d) % B]
        return remote(src, src, pk_s.at[d - 1], pk_r.at[d - 1], (c, k))

    def pq_in(d):
        src = pqbuf.at[(z + A - d) % A]
        return remote(src, src, pq_s.at[d - 1], pq_r.at[d - 1], (c, k))

    def o_right(h, o):
        return (remote(obuf.at[h, o], in_l.at[h, o], or_s.at[h, o], ol_r.at[h, o], (c + B, k)),
                remote(stbuf.at[h, o, 0:1], st_l.at[h, o, 0:1], sr_s.at[h, o], tl_r.at[h, o], (c + B, k)))

    def o_left(h, o):
        return (remote(obuf.at[h, o], in_r.at[h, o], ol_s.at[h, o], or_r.at[h, o], (c - B, k)),
                remote(stbuf.at[h, o, 0:1], st_r.at[h, o, 0:1], sl_s.at[h, o], tr_r.at[h, o], (c - B, k)))

    def out_x(h, d):
        kk = (k + d) % K
        return remote(fin.at[h, toks(kk)], out.at[:, heads(k, h), :],
                      ox_s.at[h, d - 1], ox_r.at[h, d - 1], (c, kk))

    def out_x_in(h, d):
        kk = (k + K - d) % K
        dst = out.at[:, heads(kk, h), :]
        return remote(fin.at[h, toks(kk)], dst, ox_s.at[h, d - 1], ox_r.at[h, d - 1], (c, kk))

    def iota(shape, axis):
        return lax.broadcasted_iota(jnp.int32, shape, axis)

    row = jnp.broadcast_to(pos[...].astype(jnp.float32), (T, T))
    column = jnp.sum(jnp.where(iota((T, T), 0) == iota((T, T), 1), row, 0.0), axis=1, keepdims=True)
    pkbuf[g] = jnp.broadcast_to(column, (T, 128)).astype(jnp.int32)
    own = iota((T, R), 0) == iota((T, R), 1) // G
    spread = jnp.sum(jnp.where(own, jnp.broadcast_to(column, (T, R)), 0.0), axis=0, keepdims=True)
    pqbuf[z] = jnp.broadcast_to(spread, (8, R)).astype(jnp.int32)

    barrier = pltpu.get_barrier_semaphore()
    for d in range(1, K):
        pl.semaphore_signal(barrier, inc=1, device_id=(c, (k + d) % K), device_id_type=MESH)
    for d in range(1, A):
        pl.semaphore_signal(barrier, inc=1, device_id=(((z + d) % A) * B + g, k), device_id_type=MESH)
    for d in range(1, B):
        pl.semaphore_signal(barrier, inc=1, device_id=(z * B + grp(d), k), device_id_type=MESH)
    pl.semaphore_wait(barrier, K - 1 + A - 1 + B - 1)

    def kv_send(h):
        for d1 in range(1, B1):
            kv_far(h, d1).start()
        for d2 in range(1, B2):
            kv_near(h, d2).start()
        kv_loc(h).start()

    for h in range(H):
        for d in range(1, K):
            q_x(h, d).start()
        q_loc(h).start()
        kv_send(h)
        if h == 0:
            for d in range(1, B):
                n_out(d).start()
                pk_out(d).start()
            for d in range(1, A):
                pq_out(d).start()
            pltpu.make_async_copy(new, nbuf.at[g], loc_n).start()

    def q_own(h):
        q_loc(h).wait()
        for d in range(1, K):
            q_x_in(h, d).wait_recv()

        @pl.when(z < A - 1)
        def _():
            q_right(h, z).start()

        @pl.when(z > 0)
        def _():
            q_left(h, z).start()

    def q_forward(h, d):
        @pl.when(z - d >= 0)
        def _():
            q_right(h, z - d).wait_recv()

            @pl.when(z < A - 1)
            def _():
                q_right(h, z - d).start()

        @pl.when(z + d <= A - 1)
        def _():
            q_left(h, z + d).wait_recv()

            @pl.when(z > 0)
            def _():
                q_left(h, z + d).start()

    def kv_stage1(h):
        for d1 in range(1, B1):
            kv_in(h, ((b1 + B1 - d1) % B1) * B2 + b2).wait_recv()
            for d2 in range(1, B2):
                kv_pass(h, d1, d2).start()

    def kv_stage2(h):
        kv_loc(h).wait()
        for d2 in range(1, B2):
            for d1 in range(B1):
                kv_in(h, ((b1 + B1 - d1) % B1) * B2 + (b2 + B2 - d2) % B2).wait_recv()

    for i in range(B * SL // 128):
        hit = jnp.where(pages[...] == z * (B * SL // 128) + i, 1.0, 0.0)
        hit = jnp.max(hit, axis=1, keepdims=True)
        bias[i] = jnp.broadcast_to((1.0 - hit) * NEG, (8, R))

    for h in range(H):
        q_own(h)
    if H == 1:
        for d in range(1, A):
            q_forward(0, d)
    kv_stage1(0)
    pltpu.make_async_copy(new, nbuf.at[g], loc_n).wait()
    for d in range(1, B):
        n_in(d).wait_recv()
        pk_in(d).wait_recv()
    for d in range(1, A):
        pq_in(d).wait_recv()

    low = z < A // 2
    zf = jnp.where(low, z, A - 1 - z)

    def order(j):
        far = A - 1 - zf
        f = jnp.where(j < far, A - 1 - j, jnp.where(j < A - 1, j - far, zf))
        return jnp.where(low, f, A - 1 - f)

    fold = (-1, 8, R)

    def score(h, o, lane):
        q = qbuf[h, o].reshape(R, 128)
        top = jnp.full((8, R), NEG, jnp.float32)
        for b in range(B):
            s = lax.dot_general(kvbuf[h, b, 0], q, (((1,), (1,)), ((), ())),
                                preferred_element_type=jnp.float32)
            sbuf[lane, b * SL:(b + 1) * SL, :] = s
            for i in range(SL // 128):
                part = jnp.max(s[i * 128:(i + 1) * 128].reshape(fold), axis=0)
                top = jnp.maximum(top, part + bias[b * (SL // 128) + i])
        nk = nbuf[:, h, 0].reshape(B * T, 128)
        sn = lax.dot_general(nk, q, (((1,), (1,)), ((), ())), preferred_element_type=jnp.float32)
        pos_k = pkbuf[...].reshape(B * T, 128)
        pos_k = jnp.concatenate([pos_k] * (R // 128), axis=1)
        sn = jnp.where(pos_k <= pqbuf[o][0:1, :], sn, NEG)
        top = jnp.maximum(top, jnp.max(sn.reshape(fold), axis=0))
        return sn, jnp.max(top, axis=0, keepdims=True) * cc

    def weigh(h, slot, lane, sn, m):
        pn = jnp.exp2(sn * cc - m)
        total = jnp.sum(pn.reshape(fold), axis=0)
        acc = jnp.dot(nvt[...], pn.astype(jnp.bfloat16), preferred_element_type=jnp.float32)
        for b0 in range(0, B, 2):
            ps, vs = [], []
            for b in range(b0, min(b0 + 2, B)):
                for i in range(SL // 128):
                    row = b * SL + i * 128
                    p = jnp.exp2(sbuf[lane, row:row + 128, :] * cc - (m - bias[b * (SL // 128) + i, 0:1, :]))
                    total = total + jnp.sum(p.reshape(fold), axis=0)
                    ps.append(p.astype(jnp.bfloat16))
                    vs.append(kvbuf[h, b, 1, i * 128:(i + 1) * 128, :])
            acc = acc + jnp.dot(jnp.concatenate(vs, axis=1), jnp.concatenate(ps, axis=0),
                                preferred_element_type=jnp.float32)
        denom = jnp.sum(total, axis=0, keepdims=True)
        pbuf[slot] = acc * (1.0 / denom)
        lbuf[slot] = jnp.broadcast_to(m + jnp.log(denom) * math.log2(math.e), (8, R))

    def attend(h, owners):
        found = [score(h, o, i) for i, o in enumerate(owners)]
        for i, o in enumerate(owners):
            weigh(h, h * A + o, i, *found[i])

    def merge(h, o, slot, copies, data, stats):
        for cp in copies:
            cp.wait_recv()
        x = data[h, o].astype(jnp.float32)
        lx, lo = stats[h, o, 0:1, :], lbuf[slot, 0:1, :]
        m = jnp.maximum(lx, lo)
        wx, wo = jnp.exp2(lx - m), jnp.exp2(lo - m)
        den = wx + wo
        inv = 1.0 / den
        pbuf[slot] = (wx * inv) * x + (wo * inv) * pbuf[slot]
        lbuf[slot] = jnp.broadcast_to(m + jnp.log(den) * math.log2(math.e), (8, R))

    def emit(h, o, slot, copies):
        obuf[h, o] = pbuf[slot].astype(jnp.bfloat16)
        stbuf[h, o] = lbuf[slot]
        for cp in copies:
            cp.start()

    steps = H * A
    width = 2 if A % 2 == 0 else 1
    from_left = FIRST_DELAY + HOP_DELAY * (z - 1)
    from_right = FIRST_DELAY + HOP_DELAY * (A - 2 - z)
    own_delay = FIRST_DELAY + HOP_DELAY * (A - 2)

    def step(s, carry):
        @pl.when(s < steps)
        def _():
            h, j = s // A, s % A

            @pl.when(j == 0)
            def _():
                kv_stage2(h)
                nv = nbuf[:, h, 1].reshape(B * T, 128).astype(jnp.float32)
                nvt[...] = jnp.transpose(nv).astype(jnp.bfloat16)

            for d in range(1, A):
                @pl.when((j == d // width * width) & (h == 0) & (H > 1))
                def _():
                    q_forward(0, d)

                @pl.when((j == d) & (h + 1 < H))
                def _():
                    q_forward(h + 1, d)

            @pl.when((h + 1 < H) & (j == max(A - 2, 0)))
            def _():
                kv_stage1(h + 1)

            first = (h == 0) & (H > 1)
            owners = [order(jnp.where(first, A - 1 - j - i, j + i)) for i in range(width)]

            @pl.when(j % width == 0)
            def _():
                attend(h, owners)

                for o in owners:
                    @pl.when((o > z) & (z == 0))
                    def _():
                        emit(h, o, h * A + o, o_right(h, o))

                    @pl.when((o < z) & (z == A - 1))
                    def _():
                        emit(h, o, h * A + o, o_left(h, o))

        tr = s - from_left

        @pl.when((z > 0) & (tr >= 0) & (tr < steps))
        def _():
            h, o = tr // A, order(tr % A)

            @pl.when(o > z)
            def _():
                merge(h, o, h * A + o, o_right(h, o), in_l, st_l)
                emit(h, o, h * A + o, o_right(h, o))

        tl = s - from_right

        @pl.when((z < A - 1) & (tl >= 0) & (tl < steps))
        def _():
            h, o = tl // A, order(tl % A)

            @pl.when(o < z)
            def _():
                merge(h, o, h * A + o, o_left(h, o), in_r, st_r)
                emit(h, o, h * A + o, o_left(h, o))

        to = s - own_delay

        @pl.when((to >= 0) & (to % A == A - 1))
        def _():
            h = to // A
            slot = h * A + z

            @pl.when(z > 0)
            def _():
                merge(h, z, slot, o_right(h, z), in_l, st_l)

            @pl.when(z < A - 1)
            def _():
                merge(h, z, slot, o_left(h, z), in_r, st_r)

            fin[h] = jnp.transpose(pbuf[slot]).astype(jnp.bfloat16).reshape(T, G, 128)
            for d in range(1, K):
                out_x(h, d).start()
            out[:, heads(k, h), :] = fin[h, toks(k)]

        return carry

    lax.fori_loop(0, steps + own_delay, step, 0)

    for d in range(1, B):
        n_out(d).wait_send()
        pk_out(d).wait_send()
    for d in range(1, A):
        pq_out(d).wait_send()

    def drain(h, carry):
        for d in range(1, K):
            q_x(h, d).wait_send()
            out_x(h, d).wait_send()
            out_x_in(h, d).wait_recv()
        for d1 in range(1, B1):
            kv_far(h, d1).wait_send()
            for d2 in range(1, B2):
                kv_pass(h, d1, d2).wait_send()
        for d2 in range(1, B2):
            kv_near(h, d2).wait_send()

        def per_owner(o, inner):
            @pl.when((o <= z) & (z < A - 1))
            def _():
                q_right(h, o).wait_send()

            @pl.when((o >= z) & (z > 0))
            def _():
                q_left(h, o).wait_send()

            @pl.when(o > z)
            def _():
                for cp in o_right(h, o):
                    cp.wait_send()

            @pl.when(o < z)
            def _():
                for cp in o_left(h, o):
                    cp.wait_send()

            return inner

        lax.fori_loop(0, A, per_owner, 0)
        return carry

    lax.fori_loop(0, H, drain, 0)


def solution(mesh):
    n_ctx, K = mesh.shape["ctx"], mesh.shape["kvh"]
    A, B, B2 = split_ctx(n_ctx)
    B1 = B // B2

    def body(queries, new_keys, new_values, new_positions, hist_keys, hist_values, page_slots):
        T_loc, QH, width = queries.shape
        T, H = new_keys.shape[0], new_keys.shape[1]
        HPD = QH // K
        G = HPD // H
        slots, page = hist_keys.shape[:2]
        SL = slots * page
        R = T * G
        keys = hist_keys.transpose(2, 0, 1, 3)
        values = hist_values.transpose(2, 0, 3, 1)
        hist = jnp.stack([keys, values], axis=1).reshape(H, 2, SL, width)
        new = jnp.stack([new_keys, new_values]).transpose(2, 0, 1, 3)

        bf, f32, i32 = jnp.bfloat16, jnp.float32, jnp.int32
        V = pltpu.VMEM
        D = pltpu.SemaphoreType.DMA
        kp, ap, bp = max(K - 1, 1), max(A - 1, 1), max(B - 1, 1)
        dims = (A, B, B2, K, H, T, T_loc, G, HPD, SL)
        scratch = [
            V((H, A, T, G, width), bf), V((H, B, 2, SL, width), bf), V((B, H, 2, T, width), bf),
            V((B, T, 128), i32), V((A, 8, R), i32), V((B * slots, 8, R), f32), V((width, B * T), bf), V((2, B * SL, R), f32),
            V((H * A, 128, R), f32), V((H * A, 8, R), f32),
            V((H, A, 128, R), bf), V((H, A, 8, R), f32),
            V((H, A, 128, R), bf), V((H, A, 8, R), f32),
            V((H, A, 128, R), bf), V((H, A, 8, R), f32),
            V((H, T, G, width), bf),
            D((H,)), D((H,)), D, D((H, kp)), D((H, kp)), D((H, A)), D((H, A)), D((H, A)),
            D((H, B)), D((H, B)), D((H, max(B1 - 1, 1), max(B2 - 1, 1))),
            D((bp,)), D((bp,)), D((bp,)), D((bp,)), D((ap,)), D((ap,)),
            D((H, A)), D((H, A)), D((H, A)), D((H, A)),
            D((H, A)), D((H, A)), D((H, A)), D((H, A)), D((H, kp)), D((H, kp)),
        ]
        any_ = pl.BlockSpec(memory_space=pl.ANY)
        vm = pl.BlockSpec(memory_space=pltpu.VMEM)
        work = A * R * (B * SL + B * T) * H
        return pl.pallas_call(
            lambda *refs: kernel(dims, *refs),
            out_shape=jax.ShapeDtypeStruct((T_loc, QH, width), bf),
            in_specs=[any_, any_, any_, vm, vm],
            out_specs=vm,
            scratch_shapes=scratch,
            cost_estimate=pl.CostEstimate(flops=4 * work * width, bytes_accessed=2 * hist.size + 4 * queries.size, transcendentals=work),
            compiler_params=pltpu.CompilerParams(
                collective_id=0, has_side_effects=True, vmem_limit_bytes=40 * 1024 * 1024),
        )(queries, hist, new, new_positions[None, :], page_slots[None, :])

    in_specs = (
        P(("ctx", "kvh"), None, None), P("ctx", "kvh", None), P("ctx", "kvh", None), P("ctx"),
        P("ctx", None, "kvh", None), P("ctx", None, "kvh", None), P(),
    )
    out_specs = P(("ctx", "kvh"), None, None)
    return jax.shard_map(body, mesh=mesh, in_specs=in_specs, out_specs=out_specs, check_vma=False)
```

```python
import math

import jax
import jax.numpy as jnp
from jax import lax
from jax.experimental import pallas as pl
from jax.experimental.pallas import tpu as pltpu
from jax.sharding import PartitionSpec as P

MESH = pl.DeviceIdType.MESH
NEG = -1e30
FIRST_DELAY = 3
HOP_DELAY = 1


def split_ctx(n):
    rows = max(a for a in range(1, n + 1) if n % a == 0 and a * a <= n)
    group = n // rows
    pair = 2 if group > 2 and group % 2 == 0 else 1
    return rows, group, pair


def kernel(dims, q_in, hist, pos, pages, out,
           qbuf, kvbuf, pkbuf, pqbuf, bias, nvt, sbuf, pbuf, lbuf, obuf, stbuf,
           in_l, st_l, in_r, st_r, fin,
           loc_q, loc_kv, qx_s, qx_r, qr_s, ql_s, qz_r, kv_s, kv_r, fw_s,
           pk_s, pk_r, pq_s, pq_r, or_s, ol_s, sr_s, sl_s,
           ol_r, or_r, tl_r, tr_r, ox_s, ox_r):
    A, B, B2, K, H, T, T_loc, G, HPD, SL = dims
    B1 = B // B2
    R = T * G
    c = lax.axis_index("ctx")
    k = lax.axis_index("kvh")
    z, g = c // B, c % B
    b1, b2 = g // B2, g % B2
    cc = math.log2(math.e) / math.sqrt(128)

    def remote(src, dst, ss, rs, dev):
        return pltpu.make_async_remote_copy(
            src_ref=src, dst_ref=dst, send_sem=ss, recv_sem=rs,
            device_id=dev, device_id_type=MESH)

    def heads(kk, h):
        return pl.ds(pl.multiple_of(kk * HPD + h * G, G), G)

    def toks(kk):
        return pl.ds(kk * T_loc, T_loc)

    def grp(d):
        return (g + d) % B

    def q_x(h, d):
        kk = (k + d) % K
        return remote(q_in.at[:, heads(kk, h), :], qbuf.at[h, z, toks(k)],
                      qx_s.at[h, d - 1], qx_r.at[h, d - 1], (c, kk))

    def q_x_in(h, d):
        kk = (k + K - d) % K
        dst = qbuf.at[h, z, toks(kk)]
        return remote(dst, dst, qx_s.at[h, d - 1], qx_r.at[h, d - 1], (c, kk))

    def q_loc(h):
        return pltpu.make_async_copy(q_in.at[:, heads(k, h), :], qbuf.at[h, z, toks(k)], loc_q.at[h])

    def kv_loc(h):
        return pltpu.make_async_copy(hist.at[h], kvbuf.at[h, g], loc_kv.at[h])

    def q_right(h, o):
        return remote(qbuf.at[h, o], qbuf.at[h, o], qr_s.at[h, o], qz_r.at[h, o], (c + B, k))

    def q_left(h, o):
        return remote(qbuf.at[h, o], qbuf.at[h, o], ql_s.at[h, o], qz_r.at[h, o], (c - B, k))

    def kv_far(h, d1):
        to = z * B + ((b1 + d1) % B1) * B2 + b2
        return remote(hist.at[h], kvbuf.at[h, g], kv_s.at[h, d1 - 1], kv_r.at[h, g], (to, k))

    def kv_near(h, d2):
        to = z * B + b1 * B2 + (b2 + d2) % B2
        return remote(hist.at[h], kvbuf.at[h, g], kv_s.at[h, B1 - 1 + d2 - 1], kv_r.at[h, g], (to, k))

    def kv_in(h, src):
        dst = kvbuf.at[h, src]
        return remote(dst, dst, kv_s.at[h, 0], kv_r.at[h, src], (c, k))

    def kv_pass(h, d1, d2):
        src = ((b1 + B1 - d1) % B1) * B2 + b2
        to = z * B + b1 * B2 + (b2 + d2) % B2
        return remote(kvbuf.at[h, src], kvbuf.at[h, src], fw_s.at[h, d1 - 1, d2 - 1], kv_r.at[h, src], (to, k))

    def pk_out(d):
        return remote(pkbuf.at[g], pkbuf.at[g], pk_s.at[d - 1], pk_r.at[d - 1], (z * B + grp(d), k))

    def pq_out(d):
        return remote(pqbuf.at[z], pqbuf.at[z], pq_s.at[d - 1], pq_r.at[d - 1], (((z + d) % A) * B + g, k))

    def pk_in(d):
        src = pkbuf.at[(g + B - d) % B]
        return remote(src, src, pk_s.at[d - 1], pk_r.at[d - 1], (c, k))

    def pq_in(d):
        src = pqbuf.at[(z + A - d) % A]
        return remote(src, src, pq_s.at[d - 1], pq_r.at[d - 1], (c, k))

    def o_right(h, o):
        return (remote(obuf.at[h, o], in_l.at[h, o], or_s.at[h, o], ol_r.at[h, o], (c + B, k)),
                remote(stbuf.at[h, o, 0:1], st_l.at[h, o, 0:1], sr_s.at[h, o], tl_r.at[h, o], (c + B, k)))

    def o_left(h, o):
        return (remote(obuf.at[h, o], in_r.at[h, o], ol_s.at[h, o], or_r.at[h, o], (c - B, k)),
                remote(stbuf.at[h, o, 0:1], st_r.at[h, o, 0:1], sl_s.at[h, o], tr_r.at[h, o], (c - B, k)))

    def out_x(h, d):
        kk = (k + d) % K
        return remote(fin.at[h, toks(kk)], out.at[:, heads(k, h), :],
                      ox_s.at[h, d - 1], ox_r.at[h, d - 1], (c, kk))

    def out_x_in(h, d):
        kk = (k + K - d) % K
        dst = out.at[:, heads(kk, h), :]
        return remote(fin.at[h, toks(kk)], dst, ox_s.at[h, d - 1], ox_r.at[h, d - 1], (c, kk))

    def iota(shape, axis):
        return lax.broadcasted_iota(jnp.int32, shape, axis)

    row = jnp.broadcast_to(pos[...].astype(jnp.float32), (T, T))
    column = jnp.sum(jnp.where(iota((T, T), 0) == iota((T, T), 1), row, 0.0), axis=1, keepdims=True)
    pkbuf[g] = jnp.broadcast_to(column, (T, 128)).astype(jnp.int32)
    own = iota((T, R), 0) == iota((T, R), 1) // G
    spread = jnp.sum(jnp.where(own, jnp.broadcast_to(column, (T, R)), 0.0), axis=0, keepdims=True)
    pqbuf[z] = jnp.broadcast_to(spread, (8, R)).astype(jnp.int32)

    barrier = pltpu.get_barrier_semaphore()
    for d in range(1, K):
        pl.semaphore_signal(barrier, inc=1, device_id=(c, (k + d) % K), device_id_type=MESH)
    for d in range(1, A):
        pl.semaphore_signal(barrier, inc=1, device_id=(((z + d) % A) * B + g, k), device_id_type=MESH)
    for d in range(1, B):
        pl.semaphore_signal(barrier, inc=1, device_id=(z * B + grp(d), k), device_id_type=MESH)
    pl.semaphore_wait(barrier, K - 1 + A - 1 + B - 1)

    def kv_send(h):
        for d1 in range(1, B1):
            kv_far(h, d1).start()
        for d2 in range(1, B2):
            kv_near(h, d2).start()
        kv_loc(h).start()

    for h in range(H):
        for d in range(1, K):
            q_x(h, d).start()
        q_loc(h).start()
        kv_send(h)
        if h == 0:
            for d in range(1, B):
                pk_out(d).start()
            for d in range(1, A):
                pq_out(d).start()

    def q_own(h):
        q_loc(h).wait()
        for d in range(1, K):
            q_x_in(h, d).wait_recv()

        @pl.when(z < A - 1)
        def _():
            q_right(h, z).start()

        @pl.when(z > 0)
        def _():
            q_left(h, z).start()

    def q_forward(h, d):
        @pl.when(z - d >= 0)
        def _():
            q_right(h, z - d).wait_recv()

            @pl.when(z < A - 1)
            def _():
                q_right(h, z - d).start()

        @pl.when(z + d <= A - 1)
        def _():
            q_left(h, z + d).wait_recv()

            @pl.when(z > 0)
            def _():
                q_left(h, z + d).start()

    def kv_stage1(h):
        for d1 in range(1, B1):
            kv_in(h, ((b1 + B1 - d1) % B1) * B2 + b2).wait_recv()
            for d2 in range(1, B2):
                kv_pass(h, d1, d2).start()

    def kv_stage2(h):
        kv_loc(h).wait()
        for d2 in range(1, B2):
            for d1 in range(B1):
                kv_in(h, ((b1 + B1 - d1) % B1) * B2 + (b2 + B2 - d2) % B2).wait_recv()

    for i in range(B * SL // 128):
        hit = jnp.where(pages[...] == z * (B * SL // 128) + i, 1.0, 0.0)
        hit = jnp.max(hit, axis=1, keepdims=True)
        bias[i] = jnp.broadcast_to((1.0 - hit) * NEG, (8, R))

    for h in range(H):
        q_own(h)
    if H == 1:
        for d in range(1, A):
            q_forward(0, d)
    kv_stage1(0)
    for d in range(1, B):
        pk_in(d).wait_recv()
    for d in range(1, A):
        pq_in(d).wait_recv()

    low = z < A // 2
    zf = jnp.where(low, z, A - 1 - z)

    def order(j):
        far = A - 1 - zf
        f = jnp.where(j < far, A - 1 - j, jnp.where(j < A - 1, j - far, zf))
        return jnp.where(low, f, A - 1 - f)

    fold = (-1, 8, R)

    def score(h, o, lane):
        q = qbuf[h, o].reshape(R, 128)
        top = jnp.full((8, R), NEG, jnp.float32)
        for b in range(B):
            s = lax.dot_general(kvbuf[h, b, 0, :SL, :], q, (((1,), (1,)), ((), ())),
                                preferred_element_type=jnp.float32)
            sbuf[lane, b * SL:(b + 1) * SL, :] = s
            for i in range(SL // 128):
                part = jnp.max(s[i * 128:(i + 1) * 128].reshape(fold), axis=0)
                top = jnp.maximum(top, part + bias[b * (SL // 128) + i])
        nk = kvbuf[h, :, 0, SL:SL + T, :].reshape(B * T, 128)
        sn = lax.dot_general(nk, q, (((1,), (1,)), ((), ())), preferred_element_type=jnp.float32)
        pos_k = pkbuf[...].reshape(B * T, 128)
        pos_k = jnp.concatenate([pos_k] * (R // 128), axis=1)
        sn = jnp.where(pos_k <= pqbuf[o][0:1, :], sn, NEG)
        top = jnp.maximum(top, jnp.max(sn.reshape(fold), axis=0))
        return sn, jnp.max(top, axis=0, keepdims=True) * cc

    def weigh(h, slot, lane, sn, m):
        pn = jnp.exp2(sn * cc - m)
        total = jnp.sum(pn.reshape(fold), axis=0)
        acc = jnp.dot(nvt[...], pn.astype(jnp.bfloat16), preferred_element_type=jnp.float32)
        for b0 in range(0, B, 2):
            ps, vs = [], []
            for b in range(b0, min(b0 + 2, B)):
                for i in range(SL // 128):
                    row = b * SL + i * 128
                    p = jnp.exp2(sbuf[lane, row:row + 128, :] * cc - (m - bias[b * (SL // 128) + i, 0:1, :]))
                    total = total + jnp.sum(p.reshape(fold), axis=0)
                    ps.append(p.astype(jnp.bfloat16))
                    vs.append(kvbuf[h, b, 1, i * 128:(i + 1) * 128, :])
            acc = acc + jnp.dot(jnp.concatenate(vs, axis=1), jnp.concatenate(ps, axis=0),
                                preferred_element_type=jnp.float32)
        denom = jnp.sum(total, axis=0, keepdims=True)
        pbuf[slot] = acc * (1.0 / denom)
        lbuf[slot] = jnp.broadcast_to(m + jnp.log(denom) * math.log2(math.e), (8, R))

    def attend(h, owners):
        found = [score(h, o, i) for i, o in enumerate(owners)]
        for i, o in enumerate(owners):
            weigh(h, h * A + o, i, *found[i])

    def merge(h, o, slot, copies, data, stats):
        for cp in copies:
            cp.wait_recv()
        x = data[h, o].astype(jnp.float32)
        lx, lo = stats[h, o, 0:1, :], lbuf[slot, 0:1, :]
        m = jnp.maximum(lx, lo)
        wx, wo = jnp.exp2(lx - m), jnp.exp2(lo - m)
        den = wx + wo
        inv = 1.0 / den
        pbuf[slot] = (wx * inv) * x + (wo * inv) * pbuf[slot]
        lbuf[slot] = jnp.broadcast_to(m + jnp.log(den) * math.log2(math.e), (8, R))

    def emit(h, o, slot, copies):
        obuf[h, o] = pbuf[slot].astype(jnp.bfloat16)
        stbuf[h, o] = lbuf[slot]
        for cp in copies:
            cp.start()

    steps = H * A
    width = 2 if A % 2 == 0 else 1
    from_left = FIRST_DELAY + HOP_DELAY * (z - 1)
    from_right = FIRST_DELAY + HOP_DELAY * (A - 2 - z)
    own_delay = FIRST_DELAY + HOP_DELAY * (A - 2)

    def step(s, carry):
        @pl.when(s < steps)
        def _():
            h, j = s // A, s % A

            @pl.when(j == 0)
            def _():
                kv_stage2(h)
                nv = kvbuf[h, :, 1, SL:SL + T, :].reshape(B * T, 128).astype(jnp.float32)
                nvt[...] = jnp.transpose(nv).astype(jnp.bfloat16)

            for d in range(1, A):
                @pl.when((j == d // width * width) & (h == 0) & (H > 1))
                def _():
                    q_forward(0, d)

                @pl.when((j == d) & (h + 1 < H))
                def _():
                    q_forward(h + 1, d)

            @pl.when((h + 1 < H) & (j == max(A - 2, 0)))
            def _():
                kv_stage1(h + 1)

            first = (h == 0) & (H > 1)
            owners = [order(jnp.where(first, A - 1 - j - i, j + i)) for i in range(width)]

            @pl.when(j % width == 0)
            def _():
                attend(h, owners)

                for o in owners:
                    @pl.when((o > z) & (z == 0))
                    def _():
                        emit(h, o, h * A + o, o_right(h, o))

                    @pl.when((o < z) & (z == A - 1))
                    def _():
                        emit(h, o, h * A + o, o_left(h, o))

        tr = s - from_left

        @pl.when((z > 0) & (tr >= 0) & (tr < steps))
        def _():
            h, o = tr // A, order(tr % A)

            @pl.when(o > z)
            def _():
                merge(h, o, h * A + o, o_right(h, o), in_l, st_l)
                emit(h, o, h * A + o, o_right(h, o))

        tl = s - from_right

        @pl.when((z < A - 1) & (tl >= 0) & (tl < steps))
        def _():
            h, o = tl // A, order(tl % A)

            @pl.when(o < z)
            def _():
                merge(h, o, h * A + o, o_left(h, o), in_r, st_r)
                emit(h, o, h * A + o, o_left(h, o))

        to = s - own_delay

        @pl.when((to >= 0) & (to % A == A - 1))
        def _():
            h = to // A
            slot = h * A + z

            @pl.when(z > 0)
            def _():
                merge(h, z, slot, o_right(h, z), in_l, st_l)

            @pl.when(z < A - 1)
            def _():
                merge(h, z, slot, o_left(h, z), in_r, st_r)

            fin[h] = jnp.transpose(pbuf[slot]).astype(jnp.bfloat16).reshape(T, G, 128)
            for d in range(1, K):
                out_x(h, d).start()
            out[:, heads(k, h), :] = fin[h, toks(k)]

        return carry

    lax.fori_loop(0, steps + own_delay, step, 0)

    for d in range(1, B):
        pk_out(d).wait_send()
    for d in range(1, A):
        pq_out(d).wait_send()

    def drain(h, carry):
        for d in range(1, K):
            q_x(h, d).wait_send()
            out_x(h, d).wait_send()
            out_x_in(h, d).wait_recv()
        for d1 in range(1, B1):
            kv_far(h, d1).wait_send()
            for d2 in range(1, B2):
                kv_pass(h, d1, d2).wait_send()
        for d2 in range(1, B2):
            kv_near(h, d2).wait_send()

        def per_owner(o, inner):
            @pl.when((o <= z) & (z < A - 1))
            def _():
                q_right(h, o).wait_send()

            @pl.when((o >= z) & (z > 0))
            def _():
                q_left(h, o).wait_send()

            @pl.when(o > z)
            def _():
                for cp in o_right(h, o):
                    cp.wait_send()

            @pl.when(o < z)
            def _():
                for cp in o_left(h, o):
                    cp.wait_send()

            return inner

        lax.fori_loop(0, A, per_owner, 0)
        return carry

    lax.fori_loop(0, H, drain, 0)


def solution(mesh):
    n_ctx, K = mesh.shape["ctx"], mesh.shape["kvh"]
    A, B, B2 = split_ctx(n_ctx)
    B1 = B // B2

    def body(queries, new_keys, new_values, new_positions, hist_keys, hist_values, page_slots):
        T_loc, QH, width = queries.shape
        T, H = new_keys.shape[0], new_keys.shape[1]
        HPD = QH // K
        G = HPD // H
        slots, page = hist_keys.shape[:2]
        SL = slots * page
        R = T * G
        keys = hist_keys.transpose(2, 0, 1, 3)
        values = hist_values.transpose(2, 0, 3, 1)
        new = jnp.stack([new_keys, new_values]).transpose(2, 0, 1, 3)
        hist = jnp.stack([keys, values], axis=1).reshape(H, 2, SL, width)
        hist = jnp.concatenate([hist, new], axis=2)

        bf, f32, i32 = jnp.bfloat16, jnp.float32, jnp.int32
        V = pltpu.VMEM
        D = pltpu.SemaphoreType.DMA
        kp, ap, bp = max(K - 1, 1), max(A - 1, 1), max(B - 1, 1)
        dims = (A, B, B2, K, H, T, T_loc, G, HPD, SL)
        scratch = [
            V((H, A, T, G, width), bf), V((H, B, 2, SL + T, width), bf),
            V((B, T, 128), i32), V((A, 8, R), i32), V((B * slots, 8, R), f32), V((width, B * T), bf), V((2, B * SL, R), f32),
            V((H * A, 128, R), f32), V((H * A, 8, R), f32),
            V((H, A, 128, R), bf), V((H, A, 8, R), f32),
            V((H, A, 128, R), bf), V((H, A, 8, R), f32),
            V((H, A, 128, R), bf), V((H, A, 8, R), f32),
            V((H, T, G, width), bf),
            D((H,)), D((H,)), D((H, kp)), D((H, kp)), D((H, A)), D((H, A)), D((H, A)),
            D((H, B)), D((H, B)), D((H, max(B1 - 1, 1), max(B2 - 1, 1))),
            D((bp,)), D((bp,)), D((ap,)), D((ap,)),
            D((H, A)), D((H, A)), D((H, A)), D((H, A)),
            D((H, A)), D((H, A)), D((H, A)), D((H, A)), D((H, kp)), D((H, kp)),
        ]
        any_ = pl.BlockSpec(memory_space=pl.ANY)
        vm = pl.BlockSpec(memory_space=pltpu.VMEM)
        work = A * R * (B * SL + B * T) * H
        return pl.pallas_call(
            lambda *refs: kernel(dims, *refs),
            out_shape=jax.ShapeDtypeStruct((T_loc, QH, width), bf),
            in_specs=[any_, any_, vm, vm],
            out_specs=vm,
            scratch_shapes=scratch,
            cost_estimate=pl.CostEstimate(flops=4 * work * width, bytes_accessed=2 * hist.size + 4 * queries.size, transcendentals=work),
            compiler_params=pltpu.CompilerParams(
                collective_id=0, has_side_effects=True, vmem_limit_bytes=40 * 1024 * 1024),
        )(queries, hist, new_positions[None, :], page_slots[None, :])

    in_specs = (
        P(("ctx", "kvh"), None, None), P("ctx", "kvh", None), P("ctx", "kvh", None), P("ctx"),
        P("ctx", None, "kvh", None), P("ctx", None, "kvh", None), P(),
    )
    out_specs = P(("ctx", "kvh"), None, None)
    return jax.shard_map(body, mesh=mesh, in_specs=in_specs, out_specs=out_specs, check_vma=False)
```

```python
import math

import jax
import jax.numpy as jnp
from jax import lax
from jax.experimental import pallas as pl
from jax.experimental.pallas import tpu as pltpu
from jax.sharding import PartitionSpec as P

MESH = pl.DeviceIdType.MESH
NEG = -1e30
FIRST_DELAY = 5
HOP_DELAY = 3


def split_ctx(n):
    rows = max(a for a in range(1, n + 1) if n % a == 0 and a * a <= n)
    group = n // rows
    pair = 2 if group > 2 and group % 2 == 0 else 1
    return rows, group, pair


def kernel(dims, q_in, hist, pos, pages, out,
           qbuf, kvbuf, pkbuf, pqbuf, bias, nvt, sbuf, pbuf, lbuf, obuf, stbuf,
           in_l, st_l, in_r, st_r, fin,
           loc_q, loc_kv, qx_s, qx_r, qr_s, ql_s, qz_r, kv_s, kv_r, fw_s,
           pk_s, pk_r, pq_s, pq_r, or_s, ol_s, sr_s, sl_s,
           ol_r, or_r, tl_r, tr_r, ox_s, ox_r):
    A, B, B2, K, H, T, T_loc, G, HPD, SL = dims
    B1 = B // B2
    R = T * G
    c = lax.axis_index("ctx")
    k = lax.axis_index("kvh")
    z, g = c // B, c % B
    b1, b2 = g // B2, g % B2
    cc = math.log2(math.e) / math.sqrt(128)

    def remote(src, dst, ss, rs, dev):
        return pltpu.make_async_remote_copy(
            src_ref=src, dst_ref=dst, send_sem=ss, recv_sem=rs,
            device_id=dev, device_id_type=MESH)

    def heads(kk, h):
        return pl.ds(pl.multiple_of(kk * HPD + h * G, G), G)

    def toks(kk):
        return pl.ds(kk * T_loc, T_loc)

    def grp(d):
        return (g + d) % B

    def q_x(h, d):
        kk = (k + d) % K
        return remote(q_in.at[:, heads(kk, h), :], qbuf.at[h, z, toks(k)],
                      qx_s.at[h, d - 1], qx_r.at[h, d - 1], (c, kk))

    def q_x_in(h, d):
        kk = (k + K - d) % K
        dst = qbuf.at[h, z, toks(kk)]
        return remote(dst, dst, qx_s.at[h, d - 1], qx_r.at[h, d - 1], (c, kk))

    def q_loc(h):
        return pltpu.make_async_copy(q_in.at[:, heads(k, h), :], qbuf.at[h, z, toks(k)], loc_q.at[h])

    def kv_loc(h):
        return pltpu.make_async_copy(hist.at[h], kvbuf.at[h, g], loc_kv.at[h])

    def q_right(h, o):
        return remote(qbuf.at[h, o], qbuf.at[h, o], qr_s.at[h, o], qz_r.at[h, o], (c + B, k))

    def q_left(h, o):
        return remote(qbuf.at[h, o], qbuf.at[h, o], ql_s.at[h, o], qz_r.at[h, o], (c - B, k))

    def kv_far(h, d1):
        to = z * B + ((b1 + d1) % B1) * B2 + b2
        return remote(hist.at[h], kvbuf.at[h, g], kv_s.at[h, d1 - 1], kv_r.at[h, g], (to, k))

    def kv_near(h, d2):
        to = z * B + b1 * B2 + (b2 + d2) % B2
        return remote(hist.at[h], kvbuf.at[h, g], kv_s.at[h, B1 - 1 + d2 - 1], kv_r.at[h, g], (to, k))

    def kv_in(h, src):
        dst = kvbuf.at[h, src]
        return remote(dst, dst, kv_s.at[h, 0], kv_r.at[h, src], (c, k))

    def kv_pass(h, d1, d2):
        src = ((b1 + B1 - d1) % B1) * B2 + b2
        to = z * B + b1 * B2 + (b2 + d2) % B2
        return remote(kvbuf.at[h, src], kvbuf.at[h, src], fw_s.at[h, d1 - 1, d2 - 1], kv_r.at[h, src], (to, k))

    def pk_out(d):
        return remote(pkbuf.at[g], pkbuf.at[g], pk_s.at[d - 1], pk_r.at[d - 1], (z * B + grp(d), k))

    def pq_out(d):
        return remote(pqbuf.at[z], pqbuf.at[z], pq_s.at[d - 1], pq_r.at[d - 1], (((z + d) % A) * B + g, k))

    def pk_in(d):
        src = pkbuf.at[(g + B - d) % B]
        return remote(src, src, pk_s.at[d - 1], pk_r.at[d - 1], (c, k))

    def pq_in(d):
        src = pqbuf.at[(z + A - d) % A]
        return remote(src, src, pq_s.at[d - 1], pq_r.at[d - 1], (c, k))

    def o_right(h, o):
        return (remote(obuf.at[h, o], in_l.at[h, o], or_s.at[h, o], ol_r.at[h, o], (c + B, k)),
                remote(stbuf.at[h, o, 0:1], st_l.at[h, o, 0:1], sr_s.at[h, o], tl_r.at[h, o], (c + B, k)))

    def o_left(h, o):
        return (remote(obuf.at[h, o], in_r.at[h, o], ol_s.at[h, o], or_r.at[h, o], (c - B, k)),
                remote(stbuf.at[h, o, 0:1], st_r.at[h, o, 0:1], sl_s.at[h, o], tr_r.at[h, o], (c - B, k)))

    def out_x(h, d):
        kk = (k + d) % K
        return remote(fin.at[h, toks(kk)], out.at[:, heads(k, h), :],
                      ox_s.at[h, d - 1], ox_r.at[h, d - 1], (c, kk))

    def out_x_in(h, d):
        kk = (k + K - d) % K
        dst = out.at[:, heads(kk, h), :]
        return remote(fin.at[h, toks(kk)], dst, ox_s.at[h, d - 1], ox_r.at[h, d - 1], (c, kk))

    def iota(shape, axis):
        return lax.broadcasted_iota(jnp.int32, shape, axis)

    row = jnp.broadcast_to(pos[...].astype(jnp.float32), (T, T))
    column = jnp.sum(jnp.where(iota((T, T), 0) == iota((T, T), 1), row, 0.0), axis=1, keepdims=True)
    pkbuf[g] = jnp.broadcast_to(column, (T, 128)).astype(jnp.int32)
    own = iota((T, R), 0) == iota((T, R), 1) // G
    spread = jnp.sum(jnp.where(own, jnp.broadcast_to(column, (T, R)), 0.0), axis=0, keepdims=True)
    pqbuf[z] = jnp.broadcast_to(spread, (8, R)).astype(jnp.int32)

    barrier = pltpu.get_barrier_semaphore()
    for d in range(1, K):
        pl.semaphore_signal(barrier, inc=1, device_id=(c, (k + d) % K), device_id_type=MESH)
    for d in range(1, A):
        pl.semaphore_signal(barrier, inc=1, device_id=(((z + d) % A) * B + g, k), device_id_type=MESH)
    for d in range(1, B):
        pl.semaphore_signal(barrier, inc=1, device_id=(z * B + grp(d), k), device_id_type=MESH)
    pl.semaphore_wait(barrier, K - 1 + A - 1 + B - 1)

    def kv_send(h):
        for d1 in range(1, B1):
            kv_far(h, d1).start()
        for d2 in range(1, B2):
            kv_near(h, d2).start()
        kv_loc(h).start()

    for h in range(H):
        for d in range(1, K):
            q_x(h, d).start()
        q_loc(h).start()
        kv_send(h)
        if h == 0:
            for d in range(1, B):
                pk_out(d).start()
            for d in range(1, A):
                pq_out(d).start()

    def q_own(h):
        q_loc(h).wait()
        for d in range(1, K):
            q_x_in(h, d).wait_recv()

        @pl.when(z < A - 1)
        def _():
            q_right(h, z).start()

        @pl.when(z > 0)
        def _():
            q_left(h, z).start()

    def q_forward(h, d):
        @pl.when(z - d >= 0)
        def _():
            q_right(h, z - d).wait_recv()

            @pl.when(z < A - 1)
            def _():
                q_right(h, z - d).start()

        @pl.when(z + d <= A - 1)
        def _():
            q_left(h, z + d).wait_recv()

            @pl.when(z > 0)
            def _():
                q_left(h, z + d).start()

    def kv_stage1(h):
        for d1 in range(1, B1):
            kv_in(h, ((b1 + B1 - d1) % B1) * B2 + b2).wait_recv()
            for d2 in range(1, B2):
                kv_pass(h, d1, d2).start()

    def kv_stage2(h):
        kv_loc(h).wait()
        for d2 in range(1, B2):
            for d1 in range(B1):
                kv_in(h, ((b1 + B1 - d1) % B1) * B2 + (b2 + B2 - d2) % B2).wait_recv()

    for i in range(B * SL // 128):
        hit = jnp.where(pages[...] == z * (B * SL // 128) + i, 1.0, 0.0)
        hit = jnp.max(hit, axis=1, keepdims=True)
        bias[i] = jnp.broadcast_to((1.0 - hit) * NEG, (8, R))

    for h in range(H):
        q_own(h)
    if H == 1:
        for d in range(1, A):
            q_forward(0, d)
    kv_stage1(0)
    for d in range(1, B):
        pk_in(d).wait_recv()
    for d in range(1, A):
        pq_in(d).wait_recv()

    low = z < A // 2
    zf = jnp.where(low, z, A - 1 - z)

    def order(j):
        far = A - 1 - zf
        f = jnp.where(j < far, A - 1 - j, jnp.where(j < A - 1, j - far, zf))
        return jnp.where(low, f, A - 1 - f)

    fold = (-1, 8, R)

    def score(h, o, lane):
        q = qbuf[h, o].reshape(R, 128)
        top = jnp.full((8, R), NEG, jnp.float32)
        for b in range(B):
            s = lax.dot_general(kvbuf[h, b, 0, :SL, :], q, (((1,), (1,)), ((), ())),
                                preferred_element_type=jnp.float32)
            sbuf[lane, b * SL:(b + 1) * SL, :] = s
            for i in range(SL // 128):
                part = jnp.max(s[i * 128:(i + 1) * 128].reshape(fold), axis=0)
                top = jnp.maximum(top, part + bias[b * (SL // 128) + i])
        nk = kvbuf[h, :, 0, SL:SL + T, :].reshape(B * T, 128)
        sn = lax.dot_general(nk, q, (((1,), (1,)), ((), ())), preferred_element_type=jnp.float32)
        pos_k = pkbuf[...].reshape(B * T, 128)
        pos_k = jnp.concatenate([pos_k] * (R // 128), axis=1)
        sn = jnp.where(pos_k <= pqbuf[o][0:1, :], sn, NEG)
        top = jnp.maximum(top, jnp.max(sn.reshape(fold), axis=0))
        return sn, jnp.max(top, axis=0, keepdims=True) * cc

    def weigh(h, slot, lane, sn, m):
        pn = jnp.exp2(sn * cc - m)
        total = jnp.sum(pn.reshape(fold), axis=0)
        acc = jnp.dot(nvt[...], pn.astype(jnp.bfloat16), preferred_element_type=jnp.float32)
        for b0 in range(0, B, 2):
            ps, vs = [], []
            for b in range(b0, min(b0 + 2, B)):
                for i in range(SL // 128):
                    row = b * SL + i * 128
                    p = jnp.exp2(sbuf[lane, row:row + 128, :] * cc - (m - bias[b * (SL // 128) + i, 0:1, :]))
                    total = total + jnp.sum(p.reshape(fold), axis=0)
                    ps.append(p.astype(jnp.bfloat16))
                    vs.append(kvbuf[h, b, 1, i * 128:(i + 1) * 128, :])
            acc = acc + jnp.dot(jnp.concatenate(vs, axis=1), jnp.concatenate(ps, axis=0),
                                preferred_element_type=jnp.float32)
        denom = jnp.sum(total, axis=0, keepdims=True)
        pbuf[slot] = acc * (1.0 / denom)
        lbuf[slot] = jnp.broadcast_to(m + jnp.log(denom) * math.log2(math.e), (8, R))

    def attend(h, owners):
        found = [score(h, o, i) for i, o in enumerate(owners)]
        for i, o in enumerate(owners):
            weigh(h, h * A + o, i, *found[i])

    def merge(h, o, slot, copies, data, stats):
        for cp in copies:
            cp.wait_recv()
        x = data[h, o].astype(jnp.float32)
        lx, lo = stats[h, o, 0:1, :], lbuf[slot, 0:1, :]
        m = jnp.maximum(lx, lo)
        wx, wo = jnp.exp2(lx - m), jnp.exp2(lo - m)
        den = wx + wo
        inv = 1.0 / den
        pbuf[slot] = (wx * inv) * x + (wo * inv) * pbuf[slot]
        lbuf[slot] = jnp.broadcast_to(m + jnp.log(den) * math.log2(math.e), (8, R))

    def emit(h, o, slot, copies):
        obuf[h, o] = pbuf[slot].astype(jnp.bfloat16)
        stbuf[h, o] = lbuf[slot]
        for cp in copies:
            cp.start()

    steps = H * A
    width = 2 if A % 2 == 0 else 1
    from_left = FIRST_DELAY + HOP_DELAY * (z - 1)
    from_right = FIRST_DELAY + HOP_DELAY * (A - 2 - z)
    own_delay = FIRST_DELAY + HOP_DELAY * (A - 2)

    def step(s, carry):
        @pl.when(s < steps)
        def _():
            h, j = s // A, s % A

            @pl.when(j == 0)
            def _():
                kv_stage2(h)
                nv = kvbuf[h, :, 1, SL:SL + T, :].reshape(B * T, 128).astype(jnp.float32)
                nvt[...] = jnp.transpose(nv).astype(jnp.bfloat16)

            for d in range(1, A):
                @pl.when((j == d // width * width) & (h == 0) & (H > 1))
                def _():
                    q_forward(0, d)

                @pl.when((j == d) & (h + 1 < H))
                def _():
                    q_forward(h + 1, d)

            @pl.when((h + 1 < H) & (j == max(A - 2, 0)))
            def _():
                kv_stage1(h + 1)

            first = (h == 0) & (H > 1)
            owners = [order(jnp.where(first, A - 1 - j - i, j + i)) for i in range(width)]

            @pl.when(j % width == 0)
            def _():
                attend(h, owners)

                for o in owners:
                    @pl.when((o > z) & (z == 0))
                    def _():
                        emit(h, o, h * A + o, o_right(h, o))

                    @pl.when((o < z) & (z == A - 1))
                    def _():
                        emit(h, o, h * A + o, o_left(h, o))

        tr = s - from_left

        @pl.when((z > 0) & (tr >= 0) & (tr < steps))
        def _():
            h, o = tr // A, order(tr % A)

            @pl.when(o > z)
            def _():
                merge(h, o, h * A + o, o_right(h, o), in_l, st_l)
                emit(h, o, h * A + o, o_right(h, o))

        tl = s - from_right

        @pl.when((z < A - 1) & (tl >= 0) & (tl < steps))
        def _():
            h, o = tl // A, order(tl % A)

            @pl.when(o < z)
            def _():
                merge(h, o, h * A + o, o_left(h, o), in_r, st_r)
                emit(h, o, h * A + o, o_left(h, o))

        to = s - own_delay

        @pl.when((to >= 0) & (to % A == A - 1))
        def _():
            h = to // A
            slot = h * A + z

            @pl.when(z > 0)
            def _():
                merge(h, z, slot, o_right(h, z), in_l, st_l)

            @pl.when(z < A - 1)
            def _():
                merge(h, z, slot, o_left(h, z), in_r, st_r)

            fin[h] = jnp.transpose(pbuf[slot]).astype(jnp.bfloat16).reshape(T, G, 128)
            for d in range(1, K):
                out_x(h, d).start()
            out[:, heads(k, h), :] = fin[h, toks(k)]

        return carry

    lax.fori_loop(0, steps + own_delay, step, 0)

    for d in range(1, B):
        pk_out(d).wait_send()
    for d in range(1, A):
        pq_out(d).wait_send()

    def drain(h, carry):
        for d in range(1, K):
            q_x(h, d).wait_send()
            out_x(h, d).wait_send()
            out_x_in(h, d).wait_recv()
        for d1 in range(1, B1):
            kv_far(h, d1).wait_send()
            for d2 in range(1, B2):
                kv_pass(h, d1, d2).wait_send()
        for d2 in range(1, B2):
            kv_near(h, d2).wait_send()

        def per_owner(o, inner):
            @pl.when((o <= z) & (z < A - 1))
            def _():
                q_right(h, o).wait_send()

            @pl.when((o >= z) & (z > 0))
            def _():
                q_left(h, o).wait_send()

            @pl.when(o > z)
            def _():
                for cp in o_right(h, o):
                    cp.wait_send()

            @pl.when(o < z)
            def _():
                for cp in o_left(h, o):
                    cp.wait_send()

            return inner

        lax.fori_loop(0, A, per_owner, 0)
        return carry

    lax.fori_loop(0, H, drain, 0)


def solution(mesh):
    n_ctx, K = mesh.shape["ctx"], mesh.shape["kvh"]
    A, B, B2 = split_ctx(n_ctx)
    B1 = B // B2

    def body(queries, new_keys, new_values, new_positions, hist_keys, hist_values, page_slots):
        T_loc, QH, width = queries.shape
        T, H = new_keys.shape[0], new_keys.shape[1]
        HPD = QH // K
        G = HPD // H
        slots, page = hist_keys.shape[:2]
        SL = slots * page
        R = T * G
        keys = hist_keys.transpose(2, 0, 1, 3)
        values = hist_values.transpose(2, 0, 3, 1)
        new = jnp.stack([new_keys, new_values]).transpose(2, 0, 1, 3)
        hist = jnp.stack([keys, values], axis=1).reshape(H, 2, SL, width)
        hist = jnp.concatenate([hist, new], axis=2)

        bf, f32, i32 = jnp.bfloat16, jnp.float32, jnp.int32
        V = pltpu.VMEM
        D = pltpu.SemaphoreType.DMA
        kp, ap, bp = max(K - 1, 1), max(A - 1, 1), max(B - 1, 1)
        dims = (A, B, B2, K, H, T, T_loc, G, HPD, SL)
        scratch = [
            V((H, A, T, G, width), bf), V((H, B, 2, SL + T, width), bf),
            V((B, T, 128), i32), V((A, 8, R), i32), V((B * slots, 8, R), f32), V((width, B * T), bf), V((2, B * SL, R), f32),
            V((H * A, 128, R), f32), V((H * A, 8, R), f32),
            V((H, A, 128, R), bf), V((H, A, 8, R), f32),
            V((H, A, 128, R), bf), V((H, A, 8, R), f32),
            V((H, A, 128, R), bf), V((H, A, 8, R), f32),
            V((H, T, G, width), bf),
            D((H,)), D((H,)), D((H, kp)), D((H, kp)), D((H, A)), D((H, A)), D((H, A)),
            D((H, B)), D((H, B)), D((H, max(B1 - 1, 1), max(B2 - 1, 1))),
            D((bp,)), D((bp,)), D((ap,)), D((ap,)),
            D((H, A)), D((H, A)), D((H, A)), D((H, A)),
            D((H, A)), D((H, A)), D((H, A)), D((H, A)), D((H, kp)), D((H, kp)),
        ]
        any_ = pl.BlockSpec(memory_space=pl.ANY)
        vm = pl.BlockSpec(memory_space=pltpu.VMEM)
        work = A * R * (B * SL + B * T) * H
        return pl.pallas_call(
            lambda *refs: kernel(dims, *refs),
            out_shape=jax.ShapeDtypeStruct((T_loc, QH, width), bf),
            in_specs=[any_, any_, vm, vm],
            out_specs=vm,
            scratch_shapes=scratch,
            cost_estimate=pl.CostEstimate(flops=4 * work * width, bytes_accessed=2 * hist.size + 4 * queries.size, transcendentals=work),
            compiler_params=pltpu.CompilerParams(
                collective_id=0, has_side_effects=True, vmem_limit_bytes=40 * 1024 * 1024),
        )(queries, hist, new_positions[None, :], page_slots[None, :])

    in_specs = (
        P(("ctx", "kvh"), None, None), P("ctx", "kvh", None), P("ctx", "kvh", None), P("ctx"),
        P("ctx", None, "kvh", None), P("ctx", None, "kvh", None), P(),
    )
    out_specs = P(("ctx", "kvh"), None, None)
    return jax.shard_map(body, mesh=mesh, in_specs=in_specs, out_specs=out_specs, check_vma=False)
```

```python
import math

import jax
import jax.numpy as jnp
from jax import lax
from jax.experimental import pallas as pl
from jax.experimental.pallas import tpu as pltpu
from jax.sharding import PartitionSpec as P

MESH = pl.DeviceIdType.MESH
NEG = -1e30
FIRST_DELAY = 7
HOP_DELAY = 4


def split_ctx(n):
    rows = max(a for a in range(1, n + 1) if n % a == 0 and a * a <= n)
    group = n // rows
    pair = 2 if group > 2 and group % 2 == 0 else 1
    return rows, group, pair


def kernel(dims, q_in, hist, pos, pages, out,
           qbuf, kvbuf, pkbuf, pqbuf, bias, nvt, sbuf, pbuf, lbuf, obuf, stbuf,
           in_l, st_l, in_r, st_r, fin,
           loc_q, loc_kv, qx_s, qx_r, qr_s, ql_s, qz_r, kv_s, kv_r, fw_s,
           pk_s, pk_r, pq_s, pq_r, or_s, ol_s, sr_s, sl_s,
           ol_r, or_r, tl_r, tr_r, ox_s, ox_r):
    A, B, B2, K, H, T, T_loc, G, HPD, SL = dims
    B1 = B // B2
    R = T * G
    c = lax.axis_index("ctx")
    k = lax.axis_index("kvh")
    z, g = c // B, c % B
    b1, b2 = g // B2, g % B2
    cc = math.log2(math.e) / math.sqrt(128)

    def remote(src, dst, ss, rs, dev):
        return pltpu.make_async_remote_copy(
            src_ref=src, dst_ref=dst, send_sem=ss, recv_sem=rs,
            device_id=dev, device_id_type=MESH)

    def heads(kk, h):
        return pl.ds(pl.multiple_of(kk * HPD + h * G, G), G)

    def toks(kk):
        return pl.ds(kk * T_loc, T_loc)

    def grp(d):
        return (g + d) % B

    def q_x(h, d):
        kk = (k + d) % K
        return remote(q_in.at[:, heads(kk, h), :], qbuf.at[h, z, toks(k)],
                      qx_s.at[h, d - 1], qx_r.at[h, d - 1], (c, kk))

    def q_x_in(h, d):
        kk = (k + K - d) % K
        dst = qbuf.at[h, z, toks(kk)]
        return remote(dst, dst, qx_s.at[h, d - 1], qx_r.at[h, d - 1], (c, kk))

    def q_loc(h):
        return pltpu.make_async_copy(q_in.at[:, heads(k, h), :], qbuf.at[h, z, toks(k)], loc_q.at[h])

    def kv_loc(h):
        return pltpu.make_async_copy(hist.at[h], kvbuf.at[h, g], loc_kv.at[h])

    def q_right(h, o):
        return remote(qbuf.at[h, o], qbuf.at[h, o], qr_s.at[h, o], qz_r.at[h, o], (c + B, k))

    def q_left(h, o):
        return remote(qbuf.at[h, o], qbuf.at[h, o], ql_s.at[h, o], qz_r.at[h, o], (c - B, k))

    def kv_far(h, d1):
        to = z * B + ((b1 + d1) % B1) * B2 + b2
        return remote(hist.at[h], kvbuf.at[h, g], kv_s.at[h, d1 - 1], kv_r.at[h, g], (to, k))

    def kv_near(h, d2):
        to = z * B + b1 * B2 + (b2 + d2) % B2
        return remote(hist.at[h], kvbuf.at[h, g], kv_s.at[h, B1 - 1 + d2 - 1], kv_r.at[h, g], (to, k))

    def kv_in(h, src):
        dst = kvbuf.at[h, src]
        return remote(dst, dst, kv_s.at[h, 0], kv_r.at[h, src], (c, k))

    def kv_pass(h, d1, d2):
        src = ((b1 + B1 - d1) % B1) * B2 + b2
        to = z * B + b1 * B2 + (b2 + d2) % B2
        return remote(kvbuf.at[h, src], kvbuf.at[h, src], fw_s.at[h, d1 - 1, d2 - 1], kv_r.at[h, src], (to, k))

    def pk_out(d):
        return remote(pkbuf.at[g], pkbuf.at[g], pk_s.at[d - 1], pk_r.at[d - 1], (z * B + grp(d), k))

    def pq_out(d):
        return remote(pqbuf.at[z], pqbuf.at[z], pq_s.at[d - 1], pq_r.at[d - 1], (((z + d) % A) * B + g, k))

    def pk_in(d):
        src = pkbuf.at[(g + B - d) % B]
        return remote(src, src, pk_s.at[d - 1], pk_r.at[d - 1], (c, k))

    def pq_in(d):
        src = pqbuf.at[(z + A - d) % A]
        return remote(src, src, pq_s.at[d - 1], pq_r.at[d - 1], (c, k))

    def o_right(h, o):
        return (remote(obuf.at[h, o], in_l.at[h, o], or_s.at[h, o], ol_r.at[h, o], (c + B, k)),
                remote(stbuf.at[h, o, 0:1], st_l.at[h, o, 0:1], sr_s.at[h, o], tl_r.at[h, o], (c + B, k)))

    def o_left(h, o):
        return (remote(obuf.at[h, o], in_r.at[h, o], ol_s.at[h, o], or_r.at[h, o], (c - B, k)),
                remote(stbuf.at[h, o, 0:1], st_r.at[h, o, 0:1], sl_s.at[h, o], tr_r.at[h, o], (c - B, k)))

    def out_x(h, d):
        kk = (k + d) % K
        return remote(fin.at[h, toks(kk)], out.at[:, heads(k, h), :],
                      ox_s.at[h, d - 1], ox_r.at[h, d - 1], (c, kk))

    def out_x_in(h, d):
        kk = (k + K - d) % K
        dst = out.at[:, heads(kk, h), :]
        return remote(fin.at[h, toks(kk)], dst, ox_s.at[h, d - 1], ox_r.at[h, d - 1], (c, kk))

    def iota(shape, axis):
        return lax.broadcasted_iota(jnp.int32, shape, axis)

    row = jnp.broadcast_to(pos[...].astype(jnp.float32), (T, T))
    column = jnp.sum(jnp.where(iota((T, T), 0) == iota((T, T), 1), row, 0.0), axis=1, keepdims=True)
    pkbuf[g] = jnp.broadcast_to(column, (T, 128)).astype(jnp.int32)
    own = iota((T, R), 0) == iota((T, R), 1) // G
    spread = jnp.sum(jnp.where(own, jnp.broadcast_to(column, (T, R)), 0.0), axis=0, keepdims=True)
    pqbuf[z] = jnp.broadcast_to(spread, (8, R)).astype(jnp.int32)

    barrier = pltpu.get_barrier_semaphore()
    for d in range(1, K):
        pl.semaphore_signal(barrier, inc=1, device_id=(c, (k + d) % K), device_id_type=MESH)
    for d in range(1, A):
        pl.semaphore_signal(barrier, inc=1, device_id=(((z + d) % A) * B + g, k), device_id_type=MESH)
    for d in range(1, B):
        pl.semaphore_signal(barrier, inc=1, device_id=(z * B + grp(d), k), device_id_type=MESH)
    pl.semaphore_wait(barrier, K - 1 + A - 1 + B - 1)

    def kv_send(h):
        for d1 in range(1, B1):
            kv_far(h, d1).start()
        for d2 in range(1, B2):
            kv_near(h, d2).start()
        kv_loc(h).start()

    for h in range(H):
        for d in range(1, K):
            q_x(h, d).start()
        q_loc(h).start()
        kv_send(h)
        if h == 0:
            for d in range(1, B):
                pk_out(d).start()
            for d in range(1, A):
                pq_out(d).start()

    def q_own(h):
        q_loc(h).wait()
        for d in range(1, K):
            q_x_in(h, d).wait_recv()

        @pl.when(z < A - 1)
        def _():
            q_right(h, z).start()

        @pl.when(z > 0)
        def _():
            q_left(h, z).start()

    def q_forward(h, d):
        @pl.when(z - d >= 0)
        def _():
            q_right(h, z - d).wait_recv()

            @pl.when(z < A - 1)
            def _():
                q_right(h, z - d).start()

        @pl.when(z + d <= A - 1)
        def _():
            q_left(h, z + d).wait_recv()

            @pl.when(z > 0)
            def _():
                q_left(h, z + d).start()

    def kv_stage1(h):
        for d1 in range(1, B1):
            kv_in(h, ((b1 + B1 - d1) % B1) * B2 + b2).wait_recv()
            for d2 in range(1, B2):
                kv_pass(h, d1, d2).start()

    def kv_stage2(h):
        kv_loc(h).wait()
        for d2 in range(1, B2):
            for d1 in range(B1):
                kv_in(h, ((b1 + B1 - d1) % B1) * B2 + (b2 + B2 - d2) % B2).wait_recv()

    for i in range(B * SL // 128):
        hit = jnp.where(pages[...] == z * (B * SL // 128) + i, 1.0, 0.0)
        hit = jnp.max(hit, axis=1, keepdims=True)
        bias[i] = jnp.broadcast_to((1.0 - hit) * NEG, (8, R))

    for h in range(H):
        q_own(h)
    if H == 1:
        for d in range(1, A):
            q_forward(0, d)
    kv_stage1(0)
    for d in range(1, B):
        pk_in(d).wait_recv()
    for d in range(1, A):
        pq_in(d).wait_recv()

    low = z < A // 2
    zf = jnp.where(low, z, A - 1 - z)

    def order(j):
        far = A - 1 - zf
        f = jnp.where(j < far, A - 1 - j, jnp.where(j < A - 1, j - far, zf))
        return jnp.where(low, f, A - 1 - f)

    fold = (-1, 8, R)

    def score(h, o, lane):
        q = qbuf[h, o].reshape(R, 128)
        top = jnp.full((8, R), NEG, jnp.float32)
        for b in range(B):
            s = lax.dot_general(kvbuf[h, b, 0, :SL, :], q, (((1,), (1,)), ((), ())),
                                preferred_element_type=jnp.float32)
            sbuf[lane, b * SL:(b + 1) * SL, :] = s
            for i in range(SL // 128):
                part = jnp.max(s[i * 128:(i + 1) * 128].reshape(fold), axis=0)
                top = jnp.maximum(top, part + bias[b * (SL // 128) + i])
        nk = kvbuf[h, :, 0, SL:SL + T, :].reshape(B * T, 128)
        sn = lax.dot_general(nk, q, (((1,), (1,)), ((), ())), preferred_element_type=jnp.float32)
        pos_k = pkbuf[...].reshape(B * T, 128)
        pos_k = jnp.concatenate([pos_k] * (R // 128), axis=1)
        sn = jnp.where(pos_k <= pqbuf[o][0:1, :], sn, NEG)
        top = jnp.maximum(top, jnp.max(sn.reshape(fold), axis=0))
        return sn, jnp.max(top, axis=0, keepdims=True) * cc

    def weigh(h, slot, lane, sn, m):
        pn = jnp.exp2(sn * cc - m)
        total = jnp.sum(pn.reshape(fold), axis=0)
        acc = jnp.dot(nvt[...], pn.astype(jnp.bfloat16), preferred_element_type=jnp.float32)
        for b0 in range(0, B, 2):
            ps, vs = [], []
            for b in range(b0, min(b0 + 2, B)):
                for i in range(SL // 128):
                    row = b * SL + i * 128
                    p = jnp.exp2(sbuf[lane, row:row + 128, :] * cc - (m - bias[b * (SL // 128) + i, 0:1, :]))
                    total = total + jnp.sum(p.reshape(fold), axis=0)
                    ps.append(p.astype(jnp.bfloat16))
                    vs.append(kvbuf[h, b, 1, i * 128:(i + 1) * 128, :])
            acc = acc + jnp.dot(jnp.concatenate(vs, axis=1), jnp.concatenate(ps, axis=0),
                                preferred_element_type=jnp.float32)
        denom = jnp.sum(total, axis=0, keepdims=True)
        pbuf[slot] = acc * (1.0 / denom)
        lbuf[slot] = jnp.broadcast_to(m + jnp.log(denom) * math.log2(math.e), (8, R))

    def attend(h, owners):
        found = [score(h, o, i) for i, o in enumerate(owners)]
        for i, o in enumerate(owners):
            weigh(h, h * A + o, i, *found[i])

    def merge(h, o, slot, copies, data, stats):
        for cp in copies:
            cp.wait_recv()
        x = data[h, o].astype(jnp.float32)
        lx, lo = stats[h, o, 0:1, :], lbuf[slot, 0:1, :]
        m = jnp.maximum(lx, lo)
        wx, wo = jnp.exp2(lx - m), jnp.exp2(lo - m)
        den = wx + wo
        inv = 1.0 / den
        pbuf[slot] = (wx * inv) * x + (wo * inv) * pbuf[slot]
        lbuf[slot] = jnp.broadcast_to(m + jnp.log(den) * math.log2(math.e), (8, R))

    def emit(h, o, slot, copies):
        obuf[h, o] = pbuf[slot].astype(jnp.bfloat16)
        stbuf[h, o] = lbuf[slot]
        for cp in copies:
            cp.start()

    steps = H * A
    width = 2 if A % 2 == 0 else 1
    from_left = FIRST_DELAY + HOP_DELAY * (z - 1)
    from_right = FIRST_DELAY + HOP_DELAY * (A - 2 - z)
    own_delay = FIRST_DELAY + HOP_DELAY * (A - 2)

    def step(s, carry):
        @pl.when(s < steps)
        def _():
            h, j = s // A, s % A

            @pl.when(j == 0)
            def _():
                kv_stage2(h)
                nv = kvbuf[h, :, 1, SL:SL + T, :].reshape(B * T, 128).astype(jnp.float32)
                nvt[...] = jnp.transpose(nv).astype(jnp.bfloat16)

            for d in range(1, A):
                @pl.when((j == d // width * width) & (h == 0) & (H > 1))
                def _():
                    q_forward(0, d)

                @pl.when((j == d) & (h + 1 < H))
                def _():
                    q_forward(h + 1, d)

            @pl.when((h + 1 < H) & (j == max(A - 2, 0)))
            def _():
                kv_stage1(h + 1)

            first = (h == 0) & (H > 1)
            owners = [order(jnp.where(first, A - 1 - j - i, j + i)) for i in range(width)]

            @pl.when(j % width == 0)
            def _():
                attend(h, owners)

                for o in owners:
                    @pl.when((o > z) & (z == 0))
                    def _():
                        emit(h, o, h * A + o, o_right(h, o))

                    @pl.when((o < z) & (z == A - 1))
                    def _():
                        emit(h, o, h * A + o, o_left(h, o))

        tr = s - from_left

        @pl.when((z > 0) & (tr >= 0) & (tr < steps))
        def _():
            h, o = tr // A, order(tr % A)

            @pl.when(o > z)
            def _():
                merge(h, o, h * A + o, o_right(h, o), in_l, st_l)
                emit(h, o, h * A + o, o_right(h, o))

        tl = s - from_right

        @pl.when((z < A - 1) & (tl >= 0) & (tl < steps))
        def _():
            h, o = tl // A, order(tl % A)

            @pl.when(o < z)
            def _():
                merge(h, o, h * A + o, o_left(h, o), in_r, st_r)
                emit(h, o, h * A + o, o_left(h, o))

        to = s - own_delay

        @pl.when((to >= 0) & (to % A == A - 1))
        def _():
            h = to // A
            slot = h * A + z

            @pl.when(z > 0)
            def _():
                merge(h, z, slot, o_right(h, z), in_l, st_l)

            @pl.when(z < A - 1)
            def _():
                merge(h, z, slot, o_left(h, z), in_r, st_r)

            fin[h] = jnp.transpose(pbuf[slot]).astype(jnp.bfloat16).reshape(T, G, 128)
            for d in range(1, K):
                out_x(h, d).start()
            out[:, heads(k, h), :] = fin[h, toks(k)]

        return carry

    lax.fori_loop(0, steps + own_delay, step, 0)

    for d in range(1, B):
        pk_out(d).wait_send()
    for d in range(1, A):
        pq_out(d).wait_send()

    def drain(h, carry):
        for d in range(1, K):
            q_x(h, d).wait_send()
            out_x(h, d).wait_send()
            out_x_in(h, d).wait_recv()
        for d1 in range(1, B1):
            kv_far(h, d1).wait_send()
            for d2 in range(1, B2):
                kv_pass(h, d1, d2).wait_send()
        for d2 in range(1, B2):
            kv_near(h, d2).wait_send()

        def per_owner(o, inner):
            @pl.when((o <= z) & (z < A - 1))
            def _():
                q_right(h, o).wait_send()

            @pl.when((o >= z) & (z > 0))
            def _():
                q_left(h, o).wait_send()

            @pl.when(o > z)
            def _():
                for cp in o_right(h, o):
                    cp.wait_send()

            @pl.when(o < z)
            def _():
                for cp in o_left(h, o):
                    cp.wait_send()

            return inner

        lax.fori_loop(0, A, per_owner, 0)
        return carry

    lax.fori_loop(0, H, drain, 0)


def solution(mesh):
    n_ctx, K = mesh.shape["ctx"], mesh.shape["kvh"]
    A, B, B2 = split_ctx(n_ctx)
    B1 = B // B2

    def body(queries, new_keys, new_values, new_positions, hist_keys, hist_values, page_slots):
        T_loc, QH, width = queries.shape
        T, H = new_keys.shape[0], new_keys.shape[1]
        HPD = QH // K
        G = HPD // H
        slots, page = hist_keys.shape[:2]
        SL = slots * page
        R = T * G
        keys = hist_keys.transpose(2, 0, 1, 3)
        values = hist_values.transpose(2, 0, 3, 1)
        new = jnp.stack([new_keys, new_values]).transpose(2, 0, 1, 3)
        hist = jnp.stack([keys, values], axis=1).reshape(H, 2, SL, width)
        hist = jnp.concatenate([hist, new], axis=2)

        bf, f32, i32 = jnp.bfloat16, jnp.float32, jnp.int32
        V = pltpu.VMEM
        D = pltpu.SemaphoreType.DMA
        kp, ap, bp = max(K - 1, 1), max(A - 1, 1), max(B - 1, 1)
        dims = (A, B, B2, K, H, T, T_loc, G, HPD, SL)
        scratch = [
            V((H, A, T, G, width), bf), V((H, B, 2, SL + T, width), bf),
            V((B, T, 128), i32), V((A, 8, R), i32), V((B * slots, 8, R), f32), V((width, B * T), bf), V((2, B * SL, R), f32),
            V((H * A, 128, R), f32), V((H * A, 8, R), f32),
            V((H, A, 128, R), bf), V((H, A, 8, R), f32),
            V((H, A, 128, R), bf), V((H, A, 8, R), f32),
            V((H, A, 128, R), bf), V((H, A, 8, R), f32),
            V((H, T, G, width), bf),
            D((H,)), D((H,)), D((H, kp)), D((H, kp)), D((H, A)), D((H, A)), D((H, A)),
            D((H, B)), D((H, B)), D((H, max(B1 - 1, 1), max(B2 - 1, 1))),
            D((bp,)), D((bp,)), D((ap,)), D((ap,)),
            D((H, A)), D((H, A)), D((H, A)), D((H, A)),
            D((H, A)), D((H, A)), D((H, A)), D((H, A)), D((H, kp)), D((H, kp)),
        ]
        any_ = pl.BlockSpec(memory_space=pl.ANY)
        vm = pl.BlockSpec(memory_space=pltpu.VMEM)
        work = A * R * (B * SL + B * T) * H
        return pl.pallas_call(
            lambda *refs: kernel(dims, *refs),
            out_shape=jax.ShapeDtypeStruct((T_loc, QH, width), bf),
            in_specs=[any_, any_, vm, vm],
            out_specs=vm,
            scratch_shapes=scratch,
            cost_estimate=pl.CostEstimate(flops=4 * work * width, bytes_accessed=2 * hist.size + 4 * queries.size, transcendentals=work),
            compiler_params=pltpu.CompilerParams(
                collective_id=0, has_side_effects=True, vmem_limit_bytes=40 * 1024 * 1024),
        )(queries, hist, new_positions[None, :], page_slots[None, :])

    in_specs = (
        P(("ctx", "kvh"), None, None), P("ctx", "kvh", None), P("ctx", "kvh", None), P("ctx"),
        P("ctx", None, "kvh", None), P("ctx", None, "kvh", None), P(),
    )
    out_specs = P(("ctx", "kvh"), None, None)
    return jax.shard_map(body, mesh=mesh, in_specs=in_specs, out_specs=out_specs, check_vma=False)
```

```python
import math

import jax
import jax.numpy as jnp
from jax import lax
from jax.experimental import pallas as pl
from jax.experimental.pallas import tpu as pltpu
from jax.sharding import PartitionSpec as P

MESH = pl.DeviceIdType.MESH
NEG = -1e30
FIRST_DELAY = 5
HOP_DELAY = 3


def split_ctx(n):
    rows = max(a for a in range(1, n + 1) if n % a == 0 and a * a <= n)
    group = n // rows
    pair = 2 if group > 2 and group % 2 == 0 else 1
    return rows, group, pair


def kernel(dims, q_in, hist, pos, pages, out,
           qbuf, kvbuf, pkbuf, pqbuf, bias, nvt, sbuf, pbuf, lbuf, obuf, stbuf,
           in_l, st_l, in_r, st_r, fin,
           loc_q, loc_kv, qx_s, qx_r, qr_s, ql_s, qz_r, kv_s, kv_r, fw_s,
           pk_s, pk_r, pq_s, pq_r, or_s, ol_s, sr_s, sl_s,
           ol_r, or_r, tl_r, tr_r, ox_s, ox_r):
    A, B, B2, K, H, T, T_loc, G, HPD, SL = dims
    B1 = B // B2
    R = T * G
    c = lax.axis_index("ctx")
    k = lax.axis_index("kvh")
    z, g = c // B, c % B
    b1, b2 = g // B2, g % B2
    cc = math.log2(math.e) / math.sqrt(128)

    def remote(src, dst, ss, rs, dev):
        return pltpu.make_async_remote_copy(
            src_ref=src, dst_ref=dst, send_sem=ss, recv_sem=rs,
            device_id=dev, device_id_type=MESH)

    def heads(kk, h):
        return pl.ds(pl.multiple_of(kk * HPD + h * G, G), G)

    def toks(kk):
        return pl.ds(kk * T_loc, T_loc)

    def grp(d):
        return (g + d) % B

    def q_x(h, d):
        kk = (k + d) % K
        return remote(q_in.at[:, heads(kk, h), :], qbuf.at[h, z, toks(k)],
                      qx_s.at[h, d - 1], qx_r.at[h, d - 1], (c, kk))

    def q_x_in(h, d):
        kk = (k + K - d) % K
        dst = qbuf.at[h, z, toks(kk)]
        return remote(dst, dst, qx_s.at[h, d - 1], qx_r.at[h, d - 1], (c, kk))

    def q_loc(h):
        return pltpu.make_async_copy(q_in.at[:, heads(k, h), :], qbuf.at[h, z, toks(k)], loc_q.at[h])

    def kv_loc(h):
        return pltpu.make_async_copy(hist.at[h], kvbuf.at[h, g], loc_kv.at[h])

    def q_right(h, o):
        return remote(qbuf.at[h, o], qbuf.at[h, o], qr_s.at[h, o], qz_r.at[h, o], (c + B, k))

    def q_left(h, o):
        return remote(qbuf.at[h, o], qbuf.at[h, o], ql_s.at[h, o], qz_r.at[h, o], (c - B, k))

    def kv_far(h, d1):
        to = z * B + ((b1 + d1) % B1) * B2 + b2
        return remote(hist.at[h], kvbuf.at[h, g], kv_s.at[h, d1 - 1], kv_r.at[h, g], (to, k))

    def kv_near(h, d2):
        to = z * B + b1 * B2 + (b2 + d2) % B2
        return remote(hist.at[h], kvbuf.at[h, g], kv_s.at[h, B1 - 1 + d2 - 1], kv_r.at[h, g], (to, k))

    def kv_in(h, src):
        dst = kvbuf.at[h, src]
        return remote(dst, dst, kv_s.at[h, 0], kv_r.at[h, src], (c, k))

    def kv_pass(h, d1, d2):
        src = ((b1 + B1 - d1) % B1) * B2 + b2
        to = z * B + b1 * B2 + (b2 + d2) % B2
        return remote(kvbuf.at[h, src], kvbuf.at[h, src], fw_s.at[h, d1 - 1, d2 - 1], kv_r.at[h, src], (to, k))

    def pk_out(d):
        return remote(pkbuf.at[g], pkbuf.at[g], pk_s.at[d - 1], pk_r.at[d - 1], (z * B + grp(d), k))

    def pq_out(d):
        return remote(pqbuf.at[z], pqbuf.at[z], pq_s.at[d - 1], pq_r.at[d - 1], (((z + d) % A) * B + g, k))

    def pk_in(d):
        src = pkbuf.at[(g + B - d) % B]
        return remote(src, src, pk_s.at[d - 1], pk_r.at[d - 1], (c, k))

    def pq_in(d):
        src = pqbuf.at[(z + A - d) % A]
        return remote(src, src, pq_s.at[d - 1], pq_r.at[d - 1], (c, k))

    def o_right(h, o):
        return (remote(obuf.at[h, o], in_l.at[h, o], or_s.at[h, o], ol_r.at[h, o], (c + B, k)),
                remote(stbuf.at[h, o, 0:1], st_l.at[h, o, 0:1], sr_s.at[h, o], tl_r.at[h, o], (c + B, k)))

    def o_left(h, o):
        return (remote(obuf.at[h, o], in_r.at[h, o], ol_s.at[h, o], or_r.at[h, o], (c - B, k)),
                remote(stbuf.at[h, o, 0:1], st_r.at[h, o, 0:1], sl_s.at[h, o], tr_r.at[h, o], (c - B, k)))

    def out_x(h, d):
        kk = (k + d) % K
        return remote(fin.at[h, toks(kk)], out.at[:, heads(k, h), :],
                      ox_s.at[h, d - 1], ox_r.at[h, d - 1], (c, kk))

    def out_x_in(h, d):
        kk = (k + K - d) % K
        dst = out.at[:, heads(kk, h), :]
        return remote(fin.at[h, toks(kk)], dst, ox_s.at[h, d - 1], ox_r.at[h, d - 1], (c, kk))

    def iota(shape, axis):
        return lax.broadcasted_iota(jnp.int32, shape, axis)

    row = jnp.broadcast_to(pos[...].astype(jnp.float32), (T, T))
    column = jnp.sum(jnp.where(iota((T, T), 0) == iota((T, T), 1), row, 0.0), axis=1, keepdims=True)
    pkbuf[g] = jnp.broadcast_to(column, (T, 128)).astype(jnp.int32)
    own = iota((T, R), 0) == iota((T, R), 1) // G
    spread = jnp.sum(jnp.where(own, jnp.broadcast_to(column, (T, R)), 0.0), axis=0, keepdims=True)
    pqbuf[z] = jnp.broadcast_to(spread, (8, R)).astype(jnp.int32)

    barrier = pltpu.get_barrier_semaphore()
    for d in range(1, K):
        pl.semaphore_signal(barrier, inc=1, device_id=(c, (k + d) % K), device_id_type=MESH)
    for d in range(1, A):
        pl.semaphore_signal(barrier, inc=1, device_id=(((z + d) % A) * B + g, k), device_id_type=MESH)
    for d in range(1, B):
        pl.semaphore_signal(barrier, inc=1, device_id=(z * B + grp(d), k), device_id_type=MESH)
    pl.semaphore_wait(barrier, K - 1 + A - 1 + B - 1)

    def kv_send(h):
        for d1 in range(1, B1):
            kv_far(h, d1).start()
        for d2 in range(1, B2):
            kv_near(h, d2).start()
        kv_loc(h).start()

    for h in range(H):
        for d in range(1, K):
            q_x(h, d).start()
        q_loc(h).start()
        kv_send(h)
        if h == 0:
            for d in range(1, B):
                pk_out(d).start()
            for d in range(1, A):
                pq_out(d).start()

    def q_own(h):
        q_loc(h).wait()
        for d in range(1, K):
            q_x_in(h, d).wait_recv()

        @pl.when(z < A - 1)
        def _():
            q_right(h, z).start()

        @pl.when(z > 0)
        def _():
            q_left(h, z).start()

    def q_forward(h, d):
        @pl.when(z - d >= 0)
        def _():
            q_right(h, z - d).wait_recv()

            @pl.when(z < A - 1)
            def _():
                q_right(h, z - d).start()

        @pl.when(z + d <= A - 1)
        def _():
            q_left(h, z + d).wait_recv()

            @pl.when(z > 0)
            def _():
                q_left(h, z + d).start()

    def kv_stage1(h):
        for d1 in range(1, B1):
            kv_in(h, ((b1 + B1 - d1) % B1) * B2 + b2).wait_recv()
            for d2 in range(1, B2):
                kv_pass(h, d1, d2).start()

    def kv_stage2(h):
        kv_loc(h).wait()
        for d2 in range(1, B2):
            for d1 in range(B1):
                kv_in(h, ((b1 + B1 - d1) % B1) * B2 + (b2 + B2 - d2) % B2).wait_recv()

    for i in range(B * SL // 128):
        hit = jnp.where(pages[...] == z * (B * SL // 128) + i, 1.0, 0.0)
        hit = jnp.max(hit, axis=1, keepdims=True)
        bias[i] = jnp.broadcast_to((1.0 - hit) * NEG, (8, R))

    for h in range(H):
        q_own(h)
    if H == 1:
        for d in range(1, A):
            q_forward(0, d)
    kv_stage1(0)
    for d in range(1, B):
        pk_in(d).wait_recv()
    for d in range(1, A):
        pq_in(d).wait_recv()

    low = z < A // 2
    zf = jnp.where(low, z, A - 1 - z)

    def order(j):
        far = A - 1 - zf
        f = jnp.where(j < far, A - 1 - j, jnp.where(j < A - 1, j - far, zf))
        return jnp.where(low, f, A - 1 - f)

    fold = (-1, 8, R)

    def score(h, o, lane):
        q = qbuf[h, o].reshape(R, 128)
        top = jnp.full((8, R), NEG, jnp.float32)
        for b in range(B):
            s = lax.dot_general(kvbuf[h, b, 0, :SL, :], q, (((1,), (1,)), ((), ())),
                                preferred_element_type=jnp.float32)
            sbuf[lane, b * SL:(b + 1) * SL, :] = s
            for i in range(SL // 128):
                part = jnp.max(s[i * 128:(i + 1) * 128].reshape(fold), axis=0)
                top = jnp.maximum(top, part + bias[b * (SL // 128) + i])
        nk = kvbuf[h, :, 0, SL:SL + T, :].reshape(B * T, 128)
        sn = lax.dot_general(nk, q, (((1,), (1,)), ((), ())), preferred_element_type=jnp.float32)
        pos_k = pkbuf[...].reshape(B * T, 128)
        pos_k = jnp.concatenate([pos_k] * (R // 128), axis=1)
        sn = jnp.where(pos_k <= pqbuf[o][0:1, :], sn, NEG)
        top = jnp.maximum(top, jnp.max(sn.reshape(fold), axis=0))
        return sn, jnp.max(top, axis=0, keepdims=True) * cc

    def weigh(h, slot, lane, sn, m):
        pn = jnp.exp2(sn * cc - m)
        total = jnp.sum(pn.reshape(fold), axis=0)
        acc = jnp.dot(nvt[...], pn.astype(jnp.bfloat16), preferred_element_type=jnp.float32)
        for b0 in range(0, B, 2):
            ps, vs = [], []
            for b in range(b0, min(b0 + 2, B)):
                for i in range(SL // 128):
                    row = b * SL + i * 128
                    p = jnp.exp2(sbuf[lane, row:row + 128, :] * cc - (m - bias[b * (SL // 128) + i, 0:1, :]))
                    total = total + jnp.sum(p.reshape(fold), axis=0)
                    ps.append(p.astype(jnp.bfloat16))
                    vs.append(kvbuf[h, b, 1, i * 128:(i + 1) * 128, :])
            acc = acc + jnp.dot(jnp.concatenate(vs, axis=1), jnp.concatenate(ps, axis=0),
                                preferred_element_type=jnp.float32)
        denom = jnp.sum(total, axis=0, keepdims=True)
        pbuf[slot] = acc * (1.0 / denom)
        lbuf[slot] = jnp.broadcast_to(m + jnp.log(denom) * math.log2(math.e), (8, R))

    def attend(h, owners):
        found = [score(h, o, i) for i, o in enumerate(owners)]
        for i, o in enumerate(owners):
            weigh(h, h * A + o, i, *found[i])

    def merge(h, o, slot, copies, data, stats):
        for cp in copies:
            cp.wait_recv()
        x = data[h, o].astype(jnp.float32)
        lx, lo = stats[h, o, 0:1, :], lbuf[slot, 0:1, :]
        m = jnp.maximum(lx, lo)
        wx, wo = jnp.exp2(lx - m), jnp.exp2(lo - m)
        den = wx + wo
        inv = 1.0 / den
        pbuf[slot] = (wx * inv) * x + (wo * inv) * pbuf[slot]
        lbuf[slot] = jnp.broadcast_to(m + jnp.log(den) * math.log2(math.e), (8, R))

    def emit(h, o, slot, copies):
        obuf[h, o] = pbuf[slot].astype(jnp.bfloat16)
        stbuf[h, o] = lbuf[slot]
        for cp in copies:
            cp.start()

    steps = H * A
    width = 2 if A % 2 == 0 else 1
    from_left = FIRST_DELAY + HOP_DELAY * (z - 1)
    from_right = FIRST_DELAY + HOP_DELAY * (A - 2 - z)
    own_delay = FIRST_DELAY + HOP_DELAY * (A - 2)

    def step(s, carry):
        @pl.when(s < steps)
        def _():
            h, j = s // A, s % A

            @pl.when(j == 0)
            def _():
                kv_stage2(h)
                nv = kvbuf[h, :, 1, SL:SL + T, :].reshape(B * T, 128).astype(jnp.float32)
                nvt[...] = jnp.transpose(nv).astype(jnp.bfloat16)

            for d in range(1, A):
                @pl.when((j == d // width * width) & (h == 0) & (H > 1))
                def _():
                    q_forward(0, d)

                @pl.when((j == d) & (h + 1 < H))
                def _():
                    q_forward(h + 1, d)

            @pl.when((h + 1 < H) & (j == A - 1))
            def _():
                kv_stage1(h + 1)

            first = (h == 0) & (H > 1)
            owners = [order(jnp.where(first, A - 1 - j - i, j + i)) for i in range(width)]

            @pl.when(j % width == 0)
            def _():
                attend(h, owners)

                for o in owners:
                    @pl.when((o > z) & (z == 0))
                    def _():
                        emit(h, o, h * A + o, o_right(h, o))

                    @pl.when((o < z) & (z == A - 1))
                    def _():
                        emit(h, o, h * A + o, o_left(h, o))

        tr = s - from_left

        @pl.when((z > 0) & (tr >= 0) & (tr < steps))
        def _():
            h, o = tr // A, order(tr % A)

            @pl.when(o > z)
            def _():
                merge(h, o, h * A + o, o_right(h, o), in_l, st_l)
                emit(h, o, h * A + o, o_right(h, o))

        tl = s - from_right

        @pl.when((z < A - 1) & (tl >= 0) & (tl < steps))
        def _():
            h, o = tl // A, order(tl % A)

            @pl.when(o < z)
            def _():
                merge(h, o, h * A + o, o_left(h, o), in_r, st_r)
                emit(h, o, h * A + o, o_left(h, o))

        to = s - own_delay

        @pl.when((to >= 0) & (to % A == A - 1))
        def _():
            h = to // A
            slot = h * A + z

            @pl.when(z > 0)
            def _():
                merge(h, z, slot, o_right(h, z), in_l, st_l)

            @pl.when(z < A - 1)
            def _():
                merge(h, z, slot, o_left(h, z), in_r, st_r)

            fin[h] = jnp.transpose(pbuf[slot]).astype(jnp.bfloat16).reshape(T, G, 128)
            for d in range(1, K):
                out_x(h, d).start()
            out[:, heads(k, h), :] = fin[h, toks(k)]

        return carry

    lax.fori_loop(0, steps + own_delay, step, 0)

    for d in range(1, B):
        pk_out(d).wait_send()
    for d in range(1, A):
        pq_out(d).wait_send()

    def drain(h, carry):
        for d in range(1, K):
            q_x(h, d).wait_send()
            out_x(h, d).wait_send()
            out_x_in(h, d).wait_recv()
        for d1 in range(1, B1):
            kv_far(h, d1).wait_send()
            for d2 in range(1, B2):
                kv_pass(h, d1, d2).wait_send()
        for d2 in range(1, B2):
            kv_near(h, d2).wait_send()

        def per_owner(o, inner):
            @pl.when((o <= z) & (z < A - 1))
            def _():
                q_right(h, o).wait_send()

            @pl.when((o >= z) & (z > 0))
            def _():
                q_left(h, o).wait_send()

            @pl.when(o > z)
            def _():
                for cp in o_right(h, o):
                    cp.wait_send()

            @pl.when(o < z)
            def _():
                for cp in o_left(h, o):
                    cp.wait_send()

            return inner

        lax.fori_loop(0, A, per_owner, 0)
        return carry

    lax.fori_loop(0, H, drain, 0)


def solution(mesh):
    n_ctx, K = mesh.shape["ctx"], mesh.shape["kvh"]
    A, B, B2 = split_ctx(n_ctx)
    B1 = B // B2

    def body(queries, new_keys, new_values, new_positions, hist_keys, hist_values, page_slots):
        T_loc, QH, width = queries.shape
        T, H = new_keys.shape[0], new_keys.shape[1]
        HPD = QH // K
        G = HPD // H
        slots, page = hist_keys.shape[:2]
        SL = slots * page
        R = T * G
        keys = hist_keys.transpose(2, 0, 1, 3)
        values = hist_values.transpose(2, 0, 3, 1)
        new = jnp.stack([new_keys, new_values]).transpose(2, 0, 1, 3)
        hist = jnp.stack([keys, values], axis=1).reshape(H, 2, SL, width)
        hist = jnp.concatenate([hist, new], axis=2)

        bf, f32, i32 = jnp.bfloat16, jnp.float32, jnp.int32
        V = pltpu.VMEM
        D = pltpu.SemaphoreType.DMA
        kp, ap, bp = max(K - 1, 1), max(A - 1, 1), max(B - 1, 1)
        dims = (A, B, B2, K, H, T, T_loc, G, HPD, SL)
        scratch = [
            V((H, A, T, G, width), bf), V((H, B, 2, SL + T, width), bf),
            V((B, T, 128), i32), V((A, 8, R), i32), V((B * slots, 8, R), f32), V((width, B * T), bf), V((2, B * SL, R), f32),
            V((H * A, 128, R), f32), V((H * A, 8, R), f32),
            V((H, A, 128, R), bf), V((H, A, 8, R), f32),
            V((H, A, 128, R), bf), V((H, A, 8, R), f32),
            V((H, A, 128, R), bf), V((H, A, 8, R), f32),
            V((H, T, G, width), bf),
            D((H,)), D((H,)), D((H, kp)), D((H, kp)), D((H, A)), D((H, A)), D((H, A)),
            D((H, B)), D((H, B)), D((H, max(B1 - 1, 1), max(B2 - 1, 1))),
            D((bp,)), D((bp,)), D((ap,)), D((ap,)),
            D((H, A)), D((H, A)), D((H, A)), D((H, A)),
            D((H, A)), D((H, A)), D((H, A)), D((H, A)), D((H, kp)), D((H, kp)),
        ]
        any_ = pl.BlockSpec(memory_space=pl.ANY)
        vm = pl.BlockSpec(memory_space=pltpu.VMEM)
        work = A * R * (B * SL + B * T) * H
        return pl.pallas_call(
            lambda *refs: kernel(dims, *refs),
            out_shape=jax.ShapeDtypeStruct((T_loc, QH, width), bf),
            in_specs=[any_, any_, vm, vm],
            out_specs=vm,
            scratch_shapes=scratch,
            cost_estimate=pl.CostEstimate(flops=4 * work * width, bytes_accessed=2 * hist.size + 4 * queries.size, transcendentals=work),
            compiler_params=pltpu.CompilerParams(
                collective_id=0, has_side_effects=True, vmem_limit_bytes=40 * 1024 * 1024),
        )(queries, hist, new_positions[None, :], page_slots[None, :])

    in_specs = (
        P(("ctx", "kvh"), None, None), P("ctx", "kvh", None), P("ctx", "kvh", None), P("ctx"),
        P("ctx", None, "kvh", None), P("ctx", None, "kvh", None), P(),
    )
    out_specs = P(("ctx", "kvh"), None, None)
    return jax.shard_map(body, mesh=mesh, in_specs=in_specs, out_specs=out_specs, check_vma=False)
```

```python
import math

import jax
import jax.numpy as jnp
from jax import lax
from jax.experimental import pallas as pl
from jax.experimental.pallas import tpu as pltpu
from jax.sharding import PartitionSpec as P

MESH = pl.DeviceIdType.MESH
NEG = -1e30
FIRST_DELAY = 5
HOP_DELAY = 3


def split_ctx(n):
    rows = max(a for a in range(1, n + 1) if n % a == 0 and a * a <= n)
    group = n // rows
    pair = 2 if group > 2 and group % 2 == 0 else 1
    return rows, group, pair


def kernel(dims, q_in, hist, pos, pages, out,
           qbuf, kvbuf, pkbuf, pqbuf, bias, nvt, sbuf, pbuf, lbuf, obuf, stbuf,
           in_l, st_l, in_r, st_r, fin,
           loc_q, loc_kv, qx_s, qx_r, qr_s, ql_s, qz_r, kv_s, kv_r, fw_s,
           pk_s, pk_r, pq_s, pq_r, or_s, ol_s, sr_s, sl_s,
           ol_r, or_r, tl_r, tr_r, ox_s, ox_r):
    A, B, B2, K, H, T, T_loc, G, HPD, SL = dims
    B1 = B // B2
    R = T * G
    c = lax.axis_index("ctx")
    k = lax.axis_index("kvh")
    z, g = c // B, c % B
    b1, b2 = g // B2, g % B2
    cc = math.log2(math.e) / math.sqrt(128)

    def remote(src, dst, ss, rs, dev):
        return pltpu.make_async_remote_copy(
            src_ref=src, dst_ref=dst, send_sem=ss, recv_sem=rs,
            device_id=dev, device_id_type=MESH)

    def heads(kk, h):
        return pl.ds(pl.multiple_of(kk * HPD + h * G, G), G)

    def toks(kk):
        return pl.ds(kk * T_loc, T_loc)

    def grp(d):
        return (g + d) % B

    def q_x(h, d):
        kk = (k + d) % K
        return remote(q_in.at[:, heads(kk, h), :], qbuf.at[h, z, toks(k)],
                      qx_s.at[h, d - 1], qx_r.at[h, d - 1], (c, kk))

    def q_x_in(h, d):
        kk = (k + K - d) % K
        dst = qbuf.at[h, z, toks(kk)]
        return remote(dst, dst, qx_s.at[h, d - 1], qx_r.at[h, d - 1], (c, kk))

    def q_loc(h):
        return pltpu.make_async_copy(q_in.at[:, heads(k, h), :], qbuf.at[h, z, toks(k)], loc_q.at[h])

    def kv_loc(h):
        return pltpu.make_async_copy(hist.at[h], kvbuf.at[h, g], loc_kv.at[h])

    def q_right(h, o):
        return remote(qbuf.at[h, o], qbuf.at[h, o], qr_s.at[h, o], qz_r.at[h, o], (c + B, k))

    def q_left(h, o):
        return remote(qbuf.at[h, o], qbuf.at[h, o], ql_s.at[h, o], qz_r.at[h, o], (c - B, k))

    def kv_far(h, d1):
        to = z * B + ((b1 + d1) % B1) * B2 + b2
        return remote(hist.at[h], kvbuf.at[h, g], kv_s.at[h, d1 - 1], kv_r.at[h, g], (to, k))

    def kv_near(h, d2):
        to = z * B + b1 * B2 + (b2 + d2) % B2
        return remote(hist.at[h], kvbuf.at[h, g], kv_s.at[h, B1 - 1 + d2 - 1], kv_r.at[h, g], (to, k))

    def kv_in(h, src):
        dst = kvbuf.at[h, src]
        return remote(dst, dst, kv_s.at[h, 0], kv_r.at[h, src], (c, k))

    def kv_pass(h, d1, d2):
        src = ((b1 + B1 - d1) % B1) * B2 + b2
        to = z * B + b1 * B2 + (b2 + d2) % B2
        return remote(kvbuf.at[h, src], kvbuf.at[h, src], fw_s.at[h, d1 - 1, d2 - 1], kv_r.at[h, src], (to, k))

    def pk_out(d):
        return remote(pkbuf.at[g], pkbuf.at[g], pk_s.at[d - 1], pk_r.at[d - 1], (z * B + grp(d), k))

    def pq_out(d):
        return remote(pqbuf.at[z], pqbuf.at[z], pq_s.at[d - 1], pq_r.at[d - 1], (((z + d) % A) * B + g, k))

    def pk_in(d):
        src = pkbuf.at[(g + B - d) % B]
        return remote(src, src, pk_s.at[d - 1], pk_r.at[d - 1], (c, k))

    def pq_in(d):
        src = pqbuf.at[(z + A - d) % A]
        return remote(src, src, pq_s.at[d - 1], pq_r.at[d - 1], (c, k))

    def o_right(h, o):
        return (remote(obuf.at[h, o], in_l.at[h, o], or_s.at[h, o], ol_r.at[h, o], (c + B, k)),
                remote(stbuf.at[h, o, 0:1], st_l.at[h, o, 0:1], sr_s.at[h, o], tl_r.at[h, o], (c + B, k)))

    def o_left(h, o):
        return (remote(obuf.at[h, o], in_r.at[h, o], ol_s.at[h, o], or_r.at[h, o], (c - B, k)),
                remote(stbuf.at[h, o, 0:1], st_r.at[h, o, 0:1], sl_s.at[h, o], tr_r.at[h, o], (c - B, k)))

    def out_x(h, d):
        kk = (k + d) % K
        return remote(fin.at[h, toks(kk)], out.at[:, heads(k, h), :],
                      ox_s.at[h, d - 1], ox_r.at[h, d - 1], (c, kk))

    def out_x_in(h, d):
        kk = (k + K - d) % K
        dst = out.at[:, heads(kk, h), :]
        return remote(fin.at[h, toks(kk)], dst, ox_s.at[h, d - 1], ox_r.at[h, d - 1], (c, kk))

    def iota(shape, axis):
        return lax.broadcasted_iota(jnp.int32, shape, axis)

    row = jnp.broadcast_to(pos[...].astype(jnp.float32), (T, T))
    column = jnp.sum(jnp.where(iota((T, T), 0) == iota((T, T), 1), row, 0.0), axis=1, keepdims=True)
    pkbuf[g] = jnp.broadcast_to(column, (T, 128)).astype(jnp.int32)
    own = iota((T, R), 0) == iota((T, R), 1) // G
    spread = jnp.sum(jnp.where(own, jnp.broadcast_to(column, (T, R)), 0.0), axis=0, keepdims=True)
    pqbuf[z] = jnp.broadcast_to(spread, (8, R)).astype(jnp.int32)

    barrier = pltpu.get_barrier_semaphore()
    for d in range(1, K):
        pl.semaphore_signal(barrier, inc=1, device_id=(c, (k + d) % K), device_id_type=MESH)
    for d in range(1, A):
        pl.semaphore_signal(barrier, inc=1, device_id=(((z + d) % A) * B + g, k), device_id_type=MESH)
    for d in range(1, B):
        pl.semaphore_signal(barrier, inc=1, device_id=(z * B + grp(d), k), device_id_type=MESH)
    pl.semaphore_wait(barrier, K - 1 + A - 1 + B - 1)

    def kv_send(h):
        for d1 in range(1, B1):
            kv_far(h, d1).start()
        for d2 in range(1, B2):
            kv_near(h, d2).start()
        kv_loc(h).start()

    for h in range(H):
        for d in range(1, K):
            q_x(h, d).start()
        q_loc(h).start()
        kv_send(h)
        if h == 0:
            for d in range(1, B):
                pk_out(d).start()
            for d in range(1, A):
                pq_out(d).start()

    def q_own(h):
        q_loc(h).wait()
        for d in range(1, K):
            q_x_in(h, d).wait_recv()

        @pl.when(z < A - 1)
        def _():
            q_right(h, z).start()

        @pl.when(z > 0)
        def _():
            q_left(h, z).start()

    def q_forward(h, d):
        @pl.when(z - d >= 0)
        def _():
            q_right(h, z - d).wait_recv()

            @pl.when(z < A - 1)
            def _():
                q_right(h, z - d).start()

        @pl.when(z + d <= A - 1)
        def _():
            q_left(h, z + d).wait_recv()

            @pl.when(z > 0)
            def _():
                q_left(h, z + d).start()

    def kv_stage1(h):
        for d1 in range(1, B1):
            kv_in(h, ((b1 + B1 - d1) % B1) * B2 + b2).wait_recv()
            for d2 in range(1, B2):
                kv_pass(h, d1, d2).start()

    def kv_stage2(h):
        kv_loc(h).wait()
        for d2 in range(1, B2):
            for d1 in range(B1):
                kv_in(h, ((b1 + B1 - d1) % B1) * B2 + (b2 + B2 - d2) % B2).wait_recv()

    for i in range(B * SL // 128):
        hit = jnp.where(pages[...] == z * (B * SL // 128) + i, 1.0, 0.0)
        hit = jnp.max(hit, axis=1, keepdims=True)
        bias[i] = jnp.broadcast_to((1.0 - hit) * NEG, (8, R))

    for h in range(H):
        q_own(h)
    if H == 1:
        for d in range(1, A):
            q_forward(0, d)
    kv_stage1(0)
    for d in range(1, B):
        pk_in(d).wait_recv()
    for d in range(1, A):
        pq_in(d).wait_recv()

    low = z < A // 2
    zf = jnp.where(low, z, A - 1 - z)

    def order(j):
        far = A - 1 - zf
        f = jnp.where(j < far, A - 1 - j, jnp.where(j < A - 1, j - far, zf))
        return jnp.where(low, f, A - 1 - f)

    fold = (-1, 8, R)

    def score(h, o, lane):
        q = qbuf[h, o].reshape(R, 128)
        top = jnp.full((8, R), NEG, jnp.float32)
        for b in range(B):
            s = lax.dot_general(kvbuf[h, b, 0, :SL, :], q, (((1,), (1,)), ((), ())),
                                preferred_element_type=jnp.float32)
            sbuf[lane, b * SL:(b + 1) * SL, :] = s
            for i in range(SL // 128):
                part = jnp.max(s[i * 128:(i + 1) * 128].reshape(fold), axis=0)
                top = jnp.maximum(top, part + bias[b * (SL // 128) + i])
        nk = kvbuf[h, :, 0, SL:SL + T, :].reshape(B * T, 128)
        sn = lax.dot_general(nk, q, (((1,), (1,)), ((), ())), preferred_element_type=jnp.float32)
        pos_k = pkbuf[...].reshape(B * T, 128)
        pos_k = jnp.concatenate([pos_k] * (R // 128), axis=1)
        sn = jnp.where(pos_k <= pqbuf[o][0:1, :], sn, NEG)
        top = jnp.maximum(top, jnp.max(sn.reshape(fold), axis=0))
        return sn, jnp.max(top, axis=0, keepdims=True) * cc

    def weigh(h, slot, lane, sn, m):
        pn = jnp.exp2(sn * cc - m)
        total = jnp.sum(pn.reshape(fold), axis=0)
        acc = jnp.dot(nvt[...], pn.astype(jnp.bfloat16), preferred_element_type=jnp.float32)
        for b0 in range(0, B, 2):
            ps, vs = [], []
            for b in range(b0, min(b0 + 2, B)):
                for i in range(SL // 128):
                    row = b * SL + i * 128
                    p = jnp.exp2(sbuf[lane, row:row + 128, :] * cc - (m - bias[b * (SL // 128) + i, 0:1, :]))
                    total = total + jnp.sum(p.reshape(fold), axis=0)
                    ps.append(p.astype(jnp.bfloat16))
                    vs.append(kvbuf[h, b, 1, i * 128:(i + 1) * 128, :])
            acc = acc + jnp.dot(jnp.concatenate(vs, axis=1), jnp.concatenate(ps, axis=0),
                                preferred_element_type=jnp.float32)
        denom = jnp.sum(total, axis=0, keepdims=True)
        pbuf[slot] = acc * (1.0 / denom)
        lbuf[slot] = jnp.broadcast_to(m + jnp.log(denom) * math.log2(math.e), (8, R))

    def attend(h, owners):
        found = [score(h, o, i) for i, o in enumerate(owners)]
        for i, o in enumerate(owners):
            weigh(h, h * A + o, i, *found[i])

    def merge(h, o, slot, copies, data, stats):
        for cp in copies:
            cp.wait_recv()
        x = data[h, o].astype(jnp.float32)
        lx, lo = stats[h, o, 0:1, :], lbuf[slot, 0:1, :]
        m = jnp.maximum(lx, lo)
        wx, wo = jnp.exp2(lx - m), jnp.exp2(lo - m)
        den = wx + wo
        inv = 1.0 / den
        pbuf[slot] = (wx * inv) * x + (wo * inv) * pbuf[slot]
        lbuf[slot] = jnp.broadcast_to(m + jnp.log(den) * math.log2(math.e), (8, R))

    def emit(h, o, slot, copies):
        obuf[h, o] = pbuf[slot].astype(jnp.bfloat16)
        stbuf[h, o] = lbuf[slot]
        for cp in copies:
            cp.start()

    steps = H * A
    width = 2 if A % 2 == 0 else 1
    from_left = FIRST_DELAY + HOP_DELAY * (z - 1)
    from_right = FIRST_DELAY + HOP_DELAY * (A - 2 - z)
    own_delay = FIRST_DELAY + HOP_DELAY * (A - 2)

    def step(s, carry):
        @pl.when(s < steps)
        def _():
            h, j = s // A, s % A

            @pl.when(j == 0)
            def _():
                kv_stage2(h)
                nv = kvbuf[h, :, 1, SL:SL + T, :].reshape(B * T, 128).astype(jnp.float32)
                nvt[...] = jnp.transpose(nv).astype(jnp.bfloat16)

            for d in range(1, A):
                @pl.when((j == d // width * width) & (h == 0) & (H > 1))
                def _():
                    q_forward(0, d)

                @pl.when((j == d) & (h + 1 < H))
                def _():
                    q_forward(h + 1, d)

            @pl.when((h + 1 < H) & (j == 0))
            def _():
                kv_stage1(h + 1)

            first = (h == 0) & (H > 1)
            owners = [order(jnp.where(first, A - 1 - j - i, j + i)) for i in range(width)]

            @pl.when(j % width == 0)
            def _():
                attend(h, owners)

                for o in owners:
                    @pl.when((o > z) & (z == 0))
                    def _():
                        emit(h, o, h * A + o, o_right(h, o))

                    @pl.when((o < z) & (z == A - 1))
                    def _():
                        emit(h, o, h * A + o, o_left(h, o))

        tr = s - from_left

        @pl.when((z > 0) & (tr >= 0) & (tr < steps))
        def _():
            h, o = tr // A, order(tr % A)

            @pl.when(o > z)
            def _():
                merge(h, o, h * A + o, o_right(h, o), in_l, st_l)
                emit(h, o, h * A + o, o_right(h, o))

        tl = s - from_right

        @pl.when((z < A - 1) & (tl >= 0) & (tl < steps))
        def _():
            h, o = tl // A, order(tl % A)

            @pl.when(o < z)
            def _():
                merge(h, o, h * A + o, o_left(h, o), in_r, st_r)
                emit(h, o, h * A + o, o_left(h, o))

        to = s - own_delay

        @pl.when((to >= 0) & (to % A == A - 1))
        def _():
            h = to // A
            slot = h * A + z

            @pl.when(z > 0)
            def _():
                merge(h, z, slot, o_right(h, z), in_l, st_l)

            @pl.when(z < A - 1)
            def _():
                merge(h, z, slot, o_left(h, z), in_r, st_r)

            fin[h] = jnp.transpose(pbuf[slot]).astype(jnp.bfloat16).reshape(T, G, 128)
            for d in range(1, K):
                out_x(h, d).start()
            out[:, heads(k, h), :] = fin[h, toks(k)]

        return carry

    lax.fori_loop(0, steps + own_delay, step, 0)

    for d in range(1, B):
        pk_out(d).wait_send()
    for d in range(1, A):
        pq_out(d).wait_send()

    def drain(h, carry):
        for d in range(1, K):
            q_x(h, d).wait_send()
            out_x(h, d).wait_send()
            out_x_in(h, d).wait_recv()
        for d1 in range(1, B1):
            kv_far(h, d1).wait_send()
            for d2 in range(1, B2):
                kv_pass(h, d1, d2).wait_send()
        for d2 in range(1, B2):
            kv_near(h, d2).wait_send()

        def per_owner(o, inner):
            @pl.when((o <= z) & (z < A - 1))
            def _():
                q_right(h, o).wait_send()

            @pl.when((o >= z) & (z > 0))
            def _():
                q_left(h, o).wait_send()

            @pl.when(o > z)
            def _():
                for cp in o_right(h, o):
                    cp.wait_send()

            @pl.when(o < z)
            def _():
                for cp in o_left(h, o):
                    cp.wait_send()

            return inner

        lax.fori_loop(0, A, per_owner, 0)
        return carry

    lax.fori_loop(0, H, drain, 0)


def solution(mesh):
    n_ctx, K = mesh.shape["ctx"], mesh.shape["kvh"]
    A, B, B2 = split_ctx(n_ctx)
    B1 = B // B2

    def body(queries, new_keys, new_values, new_positions, hist_keys, hist_values, page_slots):
        T_loc, QH, width = queries.shape
        T, H = new_keys.shape[0], new_keys.shape[1]
        HPD = QH // K
        G = HPD // H
        slots, page = hist_keys.shape[:2]
        SL = slots * page
        R = T * G
        keys = hist_keys.transpose(2, 0, 1, 3)
        values = hist_values.transpose(2, 0, 3, 1)
        new = jnp.stack([new_keys, new_values]).transpose(2, 0, 1, 3)
        hist = jnp.stack([keys, values], axis=1).reshape(H, 2, SL, width)
        hist = jnp.concatenate([hist, new], axis=2)

        bf, f32, i32 = jnp.bfloat16, jnp.float32, jnp.int32
        V = pltpu.VMEM
        D = pltpu.SemaphoreType.DMA
        kp, ap, bp = max(K - 1, 1), max(A - 1, 1), max(B - 1, 1)
        dims = (A, B, B2, K, H, T, T_loc, G, HPD, SL)
        scratch = [
            V((H, A, T, G, width), bf), V((H, B, 2, SL + T, width), bf),
            V((B, T, 128), i32), V((A, 8, R), i32), V((B * slots, 8, R), f32), V((width, B * T), bf), V((2, B * SL, R), f32),
            V((H * A, 128, R), f32), V((H * A, 8, R), f32),
            V((H, A, 128, R), bf), V((H, A, 8, R), f32),
            V((H, A, 128, R), bf), V((H, A, 8, R), f32),
            V((H, A, 128, R), bf), V((H, A, 8, R), f32),
            V((H, T, G, width), bf),
            D((H,)), D((H,)), D((H, kp)), D((H, kp)), D((H, A)), D((H, A)), D((H, A)),
            D((H, B)), D((H, B)), D((H, max(B1 - 1, 1), max(B2 - 1, 1))),
            D((bp,)), D((bp,)), D((ap,)), D((ap,)),
            D((H, A)), D((H, A)), D((H, A)), D((H, A)),
            D((H, A)), D((H, A)), D((H, A)), D((H, A)), D((H, kp)), D((H, kp)),
        ]
        any_ = pl.BlockSpec(memory_space=pl.ANY)
        vm = pl.BlockSpec(memory_space=pltpu.VMEM)
        work = A * R * (B * SL + B * T) * H
        return pl.pallas_call(
            lambda *refs: kernel(dims, *refs),
            out_shape=jax.ShapeDtypeStruct((T_loc, QH, width), bf),
            in_specs=[any_, any_, vm, vm],
            out_specs=vm,
            scratch_shapes=scratch,
            cost_estimate=pl.CostEstimate(flops=4 * work * width, bytes_accessed=2 * hist.size + 4 * queries.size, transcendentals=work),
            compiler_params=pltpu.CompilerParams(
                collective_id=0, has_side_effects=True, vmem_limit_bytes=40 * 1024 * 1024),
        )(queries, hist, new_positions[None, :], page_slots[None, :])

    in_specs = (
        P(("ctx", "kvh"), None, None), P("ctx", "kvh", None), P("ctx", "kvh", None), P("ctx"),
        P("ctx", None, "kvh", None), P("ctx", None, "kvh", None), P(),
    )
    out_specs = P(("ctx", "kvh"), None, None)
    return jax.shard_map(body, mesh=mesh, in_specs=in_specs, out_specs=out_specs, check_vma=False)
```
